32 devices in a mesh: dp: 8 (over z, y), tensor: 4 (over x, core).
Axes of the slice: x: 2, y: 2, z: 4, core: 2. Of those that a mesh axis runs over, the one named last changes fastest.
Arguments:
- tokens: bfloat16 [8192, 768], P(('dp', 'tensor')), may hold values from -6 to 6
- cotangent: bfloat16 [8192, 768], P(('dp', 'tensor')), may hold values from -6 to 6
- gain_attn: bfloat16 [768], P('dp'), may hold values from 0.5 to 1.5
- w_query: bfloat16 [768, 768], P('dp', 'tensor'), may hold values from -0.21875 to 0.21875
- w_key: bfloat16 [768, 768], P('dp', 'tensor'), may hold values from -0.21875 to 0.21875
- w_value: bfloat16 [768, 768], P('dp', 'tensor'), may hold values from -0.21875 to 0.21875
- w_output: bfloat16 [768, 768], P('tensor', 'dp'), may hold values from -3.5 to 3.5
- gain_ffn: bfloat16 [768], P('dp'), may hold values from 0.5 to 1.5
- dense_gate: bfloat16 [768, 2048], P('dp', 'tensor'), may hold values from -0.21875 to 0.21875
- dense_up: bfloat16 [768, 2048], P('dp', 'tensor'), may hold values from -0.21875 to 0.21875
- dense_down: bfloat16 [2048, 768], P('tensor', 'dp'), may hold values from -0.125 to 0.125
- expert_gate: bfloat16 [768, 32768], P('tensor', 'dp'), may hold values from -0.21875 to 0.21875
- expert_up: bfloat16 [768, 32768], P('tensor', 'dp'), may hold values from -0.21875 to 0.21875
- expert_down: bfloat16 [32768, 768], P('dp', 'tensor'), may hold values from -0.125 to 0.125
- routes: int32 [8192, 2], P(('dp', 'tensor')), may hold values from 0 to 15, all different within a row
- slot_order: int32 [8192, 2], P(('dp', 'tensor')), may hold values from 0 to 511, as said below
- gate_values: float32 [8192, 2], P(('dp', 'tensor')), may hold values from 0.25 to 0.75
- prefix_len: int32 [8], P('dp'), may hold values from 102 to 512
Outputs:
- block_out: bfloat16 [8192, 768], P(('dp', 'tensor'))
- grad_tokens: float32 [8192, 768], P(('dp', 'tensor'))
- grad_gain_attn: float32 [768], P('dp')
- grad_query: float32 [768, 768], P('dp', 'tensor')
- grad_key: float32 [768, 768], P('dp', 'tensor')
- grad_value: float32 [768, 768], P('dp', 'tensor')
- grad_output: float32 [768, 768], P('tensor', 'dp')
- grad_gain_ffn: float32 [768], P('dp')
- grad_dense_gate: float32 [768, 2048], P('dp', 'tensor')
- grad_dense_up: float32 [768, 2048], P('dp', 'tensor')
- grad_dense_down: float32 [2048, 768], P('tensor', 'dp')
- grad_expert_gate: float32 [768, 32768], P('tensor', 'dp')
- grad_expert_up: float32 [768, 32768], P('tensor', 'dp')
- grad_expert_down: float32 [32768, 768], P('dp', 'tensor')
The draws below stay inside these ranges and needn't reach their ends.
Inputs may be any that keep to these rules, and one draw needn't show every extreme that they name: `routes`: each row names 2 different experts. `slot_order`: the 256 rows of each device hold every number from 0 to 511 once. `prefix_len`: one value for each sequence.
All inputs are finite; a program needn't handle non-finite values.
Results may differ from the reference program's by a relative error of at most 0.015.
Values may be sent and summed in bfloat16 or wider, within the bound.
No kernel may reach another device: no remote copies, remote signals or barrier semaphores. Data moves between devices by JAX's collectives and lax.ppermute only.
A program may use at most 192 MiB of HBM per device.

```python
import math
import jax
import jax.numpy as jnp
from jax import lax

D = 768
HEADS = 12
HEAD_DIM = 64
FF = 2048
EXPERTS = 16
EFF = 2048
TOP = 2
TOK_DEV = 256
CAP = 40
SEQ_LEN = 1024
SEQS = 8
TOKENS = 8192
N_DP = 8


def draw_slot_order(key, part):
    blocks = TOKENS // TOK_DEV
    block_keys = jax.random.split(key, blocks)
    ranking = jax.vmap(lambda single_key: jax.random.permutation(single_key, TOK_DEV * TOP))(block_keys)
    return ranking.reshape(TOKENS, TOP).astype(jnp.int32)


def with_ends(array, stream_key, least, top_value):
    shape = array.shape
    spot = [jax.random.randint(jax.random.fold_in(stream_key, axis), (), 0, shape[axis]) for axis in range(len(shape))]
    array = array.at[tuple(spot)].set(least)
    longest = shape.index(max(shape))
    spot[longest] = (spot[longest] + 1) % shape[longest]
    return array.at[tuple(spot)].set(top_value)


def with_spikes(array, stream_key, source, target, parts, factor):
    def block_of(dim):
        return (jnp.arange(array.shape[dim]) // (array.shape[dim] // parts)).reshape((-1,) + (1,) * (array.ndim - 1 - dim))

    near = jax.random.permutation(stream_key, parts)[block_of(target)]
    other_side = (block_of(target) + parts // 2) % parts
    return jnp.where((block_of(source) == near) | (block_of(source) == other_side), factor * array, array)


def shard_levels(own_key, dims, cuts, smallest, top_value):
    level, own = 1.0, jax.random.fold_in(own_key, 6)
    for dim, blocks in cuts:
        heights = jnp.exp(jax.random.uniform(jax.random.fold_in(own, dim), (blocks,), jnp.float32, smallest / len(cuts), top_value / len(cuts)))
        level = level * jnp.repeat(heights, dims[dim] // blocks).reshape([-1 if axis == dim else 1 for axis in range(len(dims))])
    return level


def choose_distinct(stream_key, rows, number_of, top, lift):
    order = jax.random.permutation(jax.random.fold_in(stream_key, 1), number_of)
    favour = order
    for power in range(3):
        favour = favour * favour // number_of
    favour = favour * lift // number_of
    tickets = jax.random.randint(jax.random.fold_in(stream_key, 2), (rows, number_of), 0, 4096) + favour
    holders = jax.random.permutation(jax.random.fold_in(stream_key, 3), rows)[jnp.arange(number_of) % rows]
    tickets = jnp.where(jnp.arange(rows)[:, None] == holders[None, :], 1 << 14, tickets)
    priority = tickets * number_of + jnp.arange(number_of)
    return lax.top_k(priority.astype(jnp.int32), top)[1].astype(jnp.int32)


def scatter_about(rng, shape, width, most, cuts=(), kind=jnp.bfloat16):
    values = jax.random.normal(rng, shape, jnp.float32) * width
    if len(cuts) > 0:
        values = shard_levels(rng, shape, cuts, -0.22, 0.18) * values
    return jnp.clip(values, min=-most, max=most).astype(kind)


def noise_with(rng, shape, spread, bound, shards, heavy, kind=jnp.bfloat16):
    values = spread * jax.random.normal(rng, shape, jnp.float32)
    if shards:
        values = values * shard_levels(rng, shape, shards, -0.22, 0.18)
    return jnp.clip(with_spikes(values, jax.random.fold_in(rng, 3), *heavy), -bound, bound).astype(kind)


def setup_inputs(seed: int = 0) -> dict:
    streams_of = jax.random.split(jax.random.key(seed), 19)
    tokens = noise_with(streams_of[0], (TOKENS, D), 1.0, 6.0, ((0, 32),), (0, 1, 32, 2.75))
    cotangent = noise_with(streams_of[1], (TOKENS, D), 1.0, 6.0, ((0, 32),), (0, 1, 32, 2.75))
    gain_attn = jnp.clip(1.0 + 0.1 * jax.random.normal(streams_of[2], (D,), jnp.float32), 0.5, 1.5).astype(jnp.bfloat16)
    w_query = scatter_about(streams_of[3], (D, D), D ** -0.5, 0.21875, ((0, 8), (1, 4)))
    w_key = scatter_about(streams_of[4], (D, D), D ** -0.5, 0.21875, ((0, 8), (1, 4)))
    w_value = scatter_about(streams_of[5], (D, D), D ** -0.5, 0.21875, ((0, 8), (1, 4)))
    w_output = scatter_about(streams_of[6], (D, D), 3 ** -0.5, 3.5, ((0, 4), (1, 8)))
    gain_ffn = jnp.clip(1.0 + 0.1 * jax.random.normal(streams_of[7], (D,), jnp.float32), 0.5, 1.5).astype(jnp.bfloat16)
    dense_gate = scatter_about(streams_of[8], (D, FF), D ** -0.5, 0.21875, ((0, 8), (1, 4)))
    dense_up = scatter_about(streams_of[9], (D, FF), D ** -0.5, 0.21875, ((0, 8), (1, 4)))
    dense_down = scatter_about(streams_of[10], (FF, D), FF ** -0.5, 0.125, ((0, 4), (1, 8)))
    expert_gate = scatter_about(streams_of[11], (D, EXPERTS * EFF), D ** -0.5, 0.21875, ((0, 4), (1, 8)))
    expert_up = scatter_about(streams_of[12], (D, EXPERTS * EFF), D ** -0.5, 0.21875, ((0, 4), (1, 8)))
    expert_down = scatter_about(streams_of[13], (EXPERTS * EFF, D), EFF ** -0.5, 0.125, ((0, 8), (1, 4)))
    routes = choose_distinct(streams_of[14], TOKENS, EXPERTS, TOP, 1024)
    slot_order = draw_slot_order(jax.random.fold_in(streams_of[18], 71), 0)
    gate_values = jnp.clip(0.25 + 0.5 * jax.random.uniform(streams_of[16], (TOKENS, TOP), jnp.float32) ** shard_levels(streams_of[16], (TOKENS, TOP), ((0, 32),), -0.2, 0.2), 0.25, 0.75)
    prefix_len = with_ends(jax.random.randint(streams_of[17], (SEQS,), SEQ_LEN // 10, SEQ_LEN // 2 + 1), jax.random.fold_in(streams_of[17], 1), SEQ_LEN // 10, (SEQ_LEN // 2 + 1) - 1).astype(jnp.int32)
    return dict(tokens=tokens, cotangent=cotangent, gain_attn=gain_attn, w_query=w_query, w_key=w_key, w_value=w_value, w_output=w_output, gain_ffn=gain_ffn, dense_gate=dense_gate, dense_up=dense_up, dense_down=dense_down, expert_gate=expert_gate, expert_up=expert_up, expert_down=expert_down, routes=routes, slot_order=slot_order, gate_values=gate_values, prefix_len=prefix_len)


@jax.custom_vjp
def low(v):
    return lax.optimization_barrier(v.astype(jnp.bfloat16)).astype(jnp.float32)

@jax.custom_vjp
def low_back(v):
    return v

def low_keep(v):
    return (low(v), None)

def low_pass(kept, grad):
    return (grad,)

def back_keep(v):
    return (v, None)

def back_low(kept, grad):
    return (low(grad),)
low.defvjp(low_keep, low_pass)
low_back.defvjp(back_keep, back_low)
highest = lax.Precision.HIGHEST
epsilon = 1e-06

def exact_dot(left, right):
    return jnp.dot(left, right, precision=highest)

def norm_rows(rows_in, gain_row):
    return rows_in * lax.rsqrt(lax.optimization_barrier(jnp.mean(rows_in * rows_in, axis=-1, keepdims=True)) + epsilon) * gain_row

def rotary(values, positions, direction):
    half_width = values.shape[-1] // 2
    frequency = jnp.power(10000.0, -jnp.arange(half_width).astype(jnp.float32) / half_width)
    angles = positions[:, None].astype(jnp.float32) * frequency[None, :]
    cosine = jnp.cos(angles)[:, None, :]
    sine_part = direction * jnp.sin(angles)[:, None, :]
    first_half = values[..., :half_width]
    second_half = values[..., half_width:]
    return jnp.concatenate([first_half * cosine - second_half * sine_part, second_half * cosine + first_half * sine_part], axis=-1)

def visible_mask(query_pos, key_pos, prefix_value):
    return (key_pos[None, :] <= query_pos[:, None]) | (key_pos[None, :] < prefix_value)

def slot_targets(route_block, order_block):
    expert_ids = route_block.reshape(-1)
    ranking = order_block.reshape(-1)
    same_expert = expert_ids[:, None] == expert_ids[None, :]
    earlier = ranking[None, :] < ranking[:, None]
    placed = lax.optimization_barrier(jnp.sum((same_expert & earlier).astype(jnp.int32), axis=1)).astype(jnp.int32)
    usable = placed < CAP
    targets = jnp.where(usable, expert_ids * CAP + placed, -1).astype(jnp.int32)
    return (targets, usable)

def take_rows(source_rows, row_index):
    return jnp.take(source_rows, row_index, axis=0)

def block_layer(inputs, weights, prefix_value, route_seq, order_seq, gate_seq):
    gain_attn, w_query, w_key, w_value, w_output, gain_ffn, dense_gate, dense_up, dense_down, expert_gate, expert_up, expert_down = weights
    length = inputs.shape[0]
    positions = jnp.arange(length).astype(jnp.int32)
    normed = low(norm_rows(inputs, gain_attn))
    queries = low_back(exact_dot(normed, w_query)).reshape(length, HEADS, HEAD_DIM)
    queries = low(rotary(queries, positions, 1.0))
    keys_all = low_back(exact_dot(normed, w_key)).reshape(length, HEADS, HEAD_DIM)
    keys_all = low(rotary(keys_all, positions, 1.0))
    values_all = low(low_back(exact_dot(normed, w_value))).reshape(length, HEADS, HEAD_DIM)
    block_rows = min(512, length)
    blocks = length // block_rows
    score_scale = 1.0 / math.sqrt(HEAD_DIM)

    def attend(block_item):
        block_query, block_pos = block_item
        scores = low_back(jnp.einsum('qhd,khd->hqk', block_query, keys_all, precision=highest) * score_scale)
        scores = jnp.where(visible_mask(block_pos, positions, prefix_value)[None], scores, -1e+30)
        softmaxed = jax.nn.softmax(scores, axis=-1)
        mixture = jnp.einsum('hqk,khd->qhd', low(softmaxed), values_all, precision=highest)
        return low_back(low(mixture))
    attended = lax.map(jax.checkpoint(attend), (queries.reshape(blocks, block_rows, HEADS, HEAD_DIM), positions.reshape(blocks, block_rows)))
    attended = attended.reshape(length, D)
    hidden = inputs + low_back(exact_dot(attended, w_output))
    normed_two = low(norm_rows(hidden, gain_ffn))
    gate_pre = low_back(exact_dot(normed_two, dense_gate))
    up_pre = low_back(exact_dot(normed_two, dense_up))
    activated = low(jax.nn.silu(gate_pre) * up_pre)
    dense_out = low_back(exact_dot(activated, dense_down))
    splits = max(1, N_DP // EXPERTS)
    piece_width = EFF // splits
    groups = length // TOK_DEV
    rows_two = normed_two.reshape(groups, TOK_DEV, D)
    targets, usable = jax.vmap(slot_targets)(route_seq.reshape(groups, TOK_DEV, TOP), order_seq.reshape(groups, TOK_DEV, TOP))
    slot_ids = jnp.arange(EXPERTS * CAP).astype(jnp.int32)
    onehot = (slot_ids[None, :, None] == targets[:, None, :]).astype(jnp.float32)
    pair_rows = jnp.repeat(rows_two, TOP, axis=1)
    dispatched = jnp.einsum('gsp,gpd->gsd', onehot, pair_rows, precision=highest)
    expert_rows = jnp.transpose(dispatched.reshape(groups, EXPERTS, CAP, D), (1, 0, 2, 3)).reshape(EXPERTS, groups * CAP, D)
    pieces_in = low_back(jnp.broadcast_to(expert_rows[:, None], (EXPERTS, splits, groups * CAP, D)))
    gate_split = expert_gate.reshape(D, EXPERTS, splits, piece_width)
    up_split = expert_up.reshape(D, EXPERTS, splits, piece_width)
    down_split = expert_down.reshape(EXPERTS, splits, piece_width, D)
    expert_gate_pre = low_back(jnp.einsum('esrd,desp->esrp', pieces_in, gate_split, precision=highest))
    expert_up_pre = low_back(jnp.einsum('esrd,desp->esrp', pieces_in, up_split, precision=highest))
    expert_act = low(jax.nn.silu(expert_gate_pre) * expert_up_pre)
    piece_out = low(low_back(jnp.einsum('esrp,espd->esrd', expert_act, down_split, precision=highest)))
    expert_result = lax.optimization_barrier(jnp.sum(piece_out, axis=1))
    result_groups = jnp.transpose(expert_result.reshape(EXPERTS, groups, CAP, D), (1, 0, 2, 3)).reshape(groups, EXPERTS * CAP, D)
    pick_index = jnp.where(usable, targets, 0).astype(jnp.int32)
    pair_weight = jnp.where(usable, gate_seq.reshape(groups, TOK_DEV * TOP), 0.0)
    picked = jax.vmap(take_rows)(result_groups, pick_index) * pair_weight[..., None]
    expert_mix = lax.optimization_barrier(jnp.sum(picked.reshape(groups, TOK_DEV, TOP, D), axis=2)).reshape(length, D)
    return hidden + dense_out + expert_mix

def reference(tokens, cotangent, gain_attn, w_query, w_key, w_value, w_output, gain_ffn, dense_gate, dense_up, dense_down, expert_gate, expert_up, expert_down, routes, slot_order, gate_values, prefix_len):
    weights = jax.tree.map(lambda array_in: array_in.astype(jnp.float32), (gain_attn, w_query, w_key, w_value, w_output, gain_ffn, dense_gate, dense_up, dense_down, expert_gate, expert_up, expert_down))
    inputs_all = tokens.astype(jnp.float32).reshape(SEQS, SEQ_LEN, D)
    cotangent_all = cotangent.astype(jnp.float32).reshape(SEQS, SEQ_LEN, D)
    sequence_items = (inputs_all, cotangent_all, routes.reshape(SEQS, SEQ_LEN, TOP), slot_order.reshape(SEQS, SEQ_LEN, TOP), gate_values.astype(jnp.float32).reshape(SEQS, SEQ_LEN, TOP), prefix_len)

    def per_sequence(running, element):
        inputs, cotangent_seq, route_seq, order_seq, gate_seq, prefix_value = element

        def forward(inputs_in, weights_in):
            return block_layer(inputs_in, weights_in, prefix_value, route_seq, order_seq, gate_seq)
        output, pullback = jax.vjp(forward, inputs, weights)
        grad_inputs, grad_weights = pullback(cotangent_seq)
        summed = jax.tree.map(jnp.add, running, grad_weights)
        return (summed, (output.astype(jnp.bfloat16), grad_inputs))
    zero_grads = jax.tree.map(jnp.zeros_like, weights)
    totals, (outputs, grads_in) = lax.scan(per_sequence, zero_grads, sequence_items)
    return (outputs.reshape(TOKENS, D), grads_in.reshape(TOKENS, D), totals[0], totals[1], totals[2], totals[3], totals[4], totals[5], totals[6], totals[7], totals[8], totals[9], totals[10], totals[11])
```

```python
import math

import jax
import jax.numpy as jnp
from jax import lax
from jax.sharding import PartitionSpec as P

HEAD_DIM = 64
EXPERTS = 16
TOP = 2
CAP = 40


epsilon = 1e-06


def norm_rows(rows_in, gain_row):
    return (
        rows_in
        * lax.rsqrt(jnp.mean(rows_in * rows_in, axis=-1, keepdims=True) + epsilon)
        * gain_row
    )


def norm_back(rows_in, gain_row, grad_out):
    inverse = lax.rsqrt(jnp.mean(rows_in * rows_in, axis=-1, keepdims=True) + epsilon)
    scaled = grad_out * gain_row
    grad_rows = inverse * scaled - rows_in * inverse**3 * jnp.mean(
        scaled * rows_in, axis=-1, keepdims=True
    )
    grad_gain = jnp.sum(grad_out * rows_in * inverse, axis=0)
    return (grad_rows, grad_gain)


def rotary(values, positions, direction):
    half_width = values.shape[-1] // 2
    frequency = jnp.power(10000.0, -jnp.arange(half_width).astype(jnp.float32) / half_width)
    angles = positions[:, None].astype(jnp.float32) * frequency[None, :]
    cosine = jnp.cos(angles)[:, None, :]
    sine_part = direction * jnp.sin(angles)[:, None, :]
    first_half = values[..., :half_width]
    second_half = values[..., half_width:]
    return jnp.concatenate(
        [
            first_half * cosine - second_half * sine_part,
            second_half * cosine + first_half * sine_part,
        ],
        axis=-1,
    )


def swiglu_back(grad_act, gate_pre, up_pre):
    sigmoid = jax.nn.sigmoid(gate_pre)
    silu_value = gate_pre * sigmoid
    grad_gate = grad_act * up_pre * sigmoid * (1.0 + gate_pre * (1.0 - sigmoid))
    grad_up = grad_act * silu_value
    return (grad_gate.astype(jnp.bfloat16), grad_up.astype(jnp.bfloat16))


def to_across(values):
    return lax.ppermute(values, "tensor", [(i, i ^ 2) for i in range(4)])


def to_beside(values):
    return lax.ppermute(values, "tensor", [(i, i ^ 1) for i in range(4)])


def gather_blocks(rows_in):
    near = jnp.stack([rows_in, to_across(rows_in)])
    return jnp.concatenate([near, to_beside(near)]).reshape(-1, rows_in.shape[-1])


def sum_blocks(partial):
    blocks = partial.reshape(4, -1, partial.shape[-1])
    near = blocks[:2] + to_beside(blocks[2:].astype(jnp.bfloat16)).astype(jnp.float32)
    return near[0] + to_across(near[1].astype(jnp.bfloat16)).astype(jnp.float32)


def paired(
    tokens,
    cotangent,
    gain_attn,
    w_query,
    w_key,
    w_value,
    w_output,
    gain_ffn,
    dense_gate,
    dense_up,
    dense_down,
    expert_gate,
    expert_up,
    expert_down,
    routes,
    slot_order,
    gate_values,
    prefix_len,
):
    dp_count = lax.axis_size("dp")
    tensor_count = lax.axis_size("tensor")
    place = lax.axis_index("tensor")
    local_rows, width = tokens.shape
    length = local_rows * tensor_count
    columns = w_query.shape[1]
    shard = w_query.shape[0]
    hidden_cols = dense_gate.shape[1]
    devices = dp_count * tensor_count
    slots = EXPERTS * CAP
    bf16, f32 = jnp.bfloat16, jnp.float32

    def dot(left, right, dims):
        return lax.dot_general(left, right, (dims, ((), ())), preferred_element_type=f32)

    nn, nt, tn = ((1,), (0,)), ((1,), (1,)), ((0,), (0,))

    gain_width = 64
    pad_width = -(4 * columns + gain_width) % 128
    first_shard = jnp.concatenate(
        [
            w_query,
            w_key,
            w_value,
            gain_attn[:, None],
            gain_ffn[:, None],
            jnp.zeros((shard, gain_width - 2), bf16),
            w_output.T,
            jnp.zeros((shard, pad_width), bf16),
        ],
        axis=1,
    )
    second_shard = jnp.concatenate([dense_gate, dense_up, dense_down.T], axis=1)
    first = lax.all_gather(first_shard, "dp", axis=0, tiled=True)
    second = lax.all_gather(second_shard, "dp", axis=0, tiled=True)
    mixer = first[:, : 3 * columns]
    gain_one = first[:, 3 * columns].astype(f32)
    gain_two = first[:, 3 * columns + 1].astype(f32)
    output_t = first[:, 3 * columns + gain_width :][:, :columns]
    gate_full = second[:, :hidden_cols]
    up_full = second[:, hidden_cols : 2 * hidden_cols]
    down_t = second[:, 2 * hidden_cols :]

    def to_pieces(weight):
        return lax.all_to_all(weight, "tensor", split_axis=1, concat_axis=0, tiled=True)

    def from_pieces(grad):
        return lax.all_to_all(
            grad.astype(bf16), "tensor", split_axis=0, concat_axis=1, tiled=True
        ).astype(f32)

    tokens_all = gather_blocks(tokens)
    cotangent_all = gather_blocks(cotangent)
    piece_gate = to_pieces(expert_gate)
    piece_up = to_pieces(expert_up)
    piece_down_t = to_pieces(expert_down.T)

    expert_ids = routes.reshape(-1)
    ranking = slot_order.reshape(-1)
    same_expert = expert_ids[:, None] == expert_ids[None, :]
    earlier = ranking[None, :] < ranking[:, None]
    placed = jnp.sum((same_expert & earlier).astype(jnp.int32), axis=1)
    targets = jnp.where(placed < CAP, expert_ids * CAP + placed, -1)
    slot_ids = jnp.arange(slots, dtype=jnp.int32)
    targets_two = targets.reshape(local_rows, TOP)
    hits = [slot_ids[:, None] == targets_two[None, :, k] for k in range(TOP)]
    token_map = sum(hit.astype(bf16) for hit in hits)
    gate_map = sum(jnp.where(hits[k], gate_values[None, :, k], 0.0) for k in range(TOP))
    slot_gate = jnp.sum(gate_map, axis=1)
    gate_high = gate_map.astype(bf16)
    gate_low = (gate_map - gate_high.astype(f32)).astype(bf16)

    def dispatch(slot_rows):
        own = lax.all_to_all(
            slot_rows.reshape(devices, slots // devices, width),
            ("dp", "tensor"),
            split_axis=0,
            concat_axis=0,
            tiled=True,
        ).reshape(slots, width)
        return jnp.concatenate([own, to_beside(own)])

    def send_back(partial):
        total = partial[:slots] + to_beside(partial[slots:].astype(bf16)).astype(f32)
        return lax.all_to_all(
            total.astype(bf16).reshape(devices, slots // devices, width),
            ("dp", "tensor"),
            split_axis=0,
            concat_axis=0,
            tiled=True,
        ).reshape(slots, width)

    slot_cotangent = dot(token_map, cotangent, nn) * slot_gate[:, None]
    grad_rows = dispatch(slot_cotangent.astype(bf16))

    positions = jnp.concatenate(
        [(place ^ k) * local_rows + jnp.arange(local_rows, dtype=jnp.int32) for k in (0, 2, 1, 3)]
    )
    prefix_value = prefix_len[0]
    head_count = columns // HEAD_DIM
    inputs_all = tokens_all.astype(f32)
    normed_all = norm_rows(inputs_all, gain_one).astype(bf16)
    projected = dot(normed_all, mixer, nn)
    per_head = (length, head_count, HEAD_DIM)
    queries = rotary(projected[:, :columns].reshape(per_head), positions, 1.0).astype(bf16)
    keys_all = rotary(
        projected[:, columns : 2 * columns].reshape(per_head), positions, 1.0
    ).astype(bf16)
    values_all = projected[:, 2 * columns :].astype(bf16).reshape(per_head)
    score_scale = 1.0 / math.sqrt(HEAD_DIM)
    visible = (positions[None, :] <= positions[:, None]) | (positions[None, :] < prefix_value)

    def scores_of():
        scores = (
            jnp.einsum("qhd,khd->hqk", queries, keys_all, preferred_element_type=f32) * score_scale
        )
        return jnp.where(visible[None], scores, -1e30)

    scores = scores_of()
    row_top = jnp.max(scores, axis=-1, keepdims=True)
    exponent = jnp.exp(scores - row_top)
    row_total = jnp.sum(exponent, axis=-1, keepdims=True)
    log_total = row_top + jnp.log(row_total)
    attended = (
        jnp.einsum(
            "hqk,khd->qhd",
            (exponent / row_total).astype(bf16),
            values_all,
            preferred_element_type=f32,
        )
        .astype(bf16)
        .reshape(length, columns)
    )
    inputs = tokens.astype(f32)
    hidden = inputs + sum_blocks(dot(attended, output_t, nt))
    normed_two = norm_rows(hidden, gain_two).astype(bf16)

    dispatched = dot(token_map, normed_two, nn).astype(bf16)
    expert_rows = dispatch(dispatched)

    normed_two_all = gather_blocks(normed_two)
    gate_pre = dot(normed_two_all, gate_full, nn)
    up_pre = dot(normed_two_all, up_full, nn)
    activated = (jax.nn.silu(gate_pre) * up_pre).astype(bf16)
    dense_out = sum_blocks(dot(activated, down_t, nt))
    grad_act = dot(cotangent_all, down_t, nn)
    grad_gate_pre, grad_up_pre = swiglu_back(grad_act, gate_pre, up_pre)
    dense_back = sum_blocks(dot(grad_gate_pre, gate_full, nt) + dot(grad_up_pre, up_full, nt))
    second_grad = jnp.concatenate(
        [
            dot(normed_two_all, grad_gate_pre, tn).astype(bf16),
            dot(normed_two_all, grad_up_pre, tn).astype(bf16),
            dot(cotangent_all, activated, tn).astype(bf16),
        ],
        axis=1,
    )
    second_total = lax.psum_scatter(second_grad, "dp", scatter_dimension=0, tiled=True).astype(f32)

    expert_gate_pre = dot(expert_rows, piece_gate, nn)
    expert_up_pre = dot(expert_rows, piece_up, nn)
    expert_act = (jax.nn.silu(expert_gate_pre) * expert_up_pre).astype(bf16)
    grad_expert_act = dot(grad_rows, piece_down_t, nn)
    grad_expert_gate, grad_expert_up = swiglu_back(grad_expert_act, expert_gate_pre, expert_up_pre)
    slots_back = send_back(
        dot(grad_expert_gate, piece_gate, nt) + dot(grad_expert_up, piece_up, nt)
    )
    slots_out = send_back(dot(expert_act, piece_down_t, nt))
    gate_total = from_pieces(dot(expert_rows, grad_expert_gate, tn))
    up_total = from_pieces(dot(expert_rows, grad_expert_up, tn))
    down_total = from_pieces(dot(grad_rows, expert_act, tn)).T

    expert_mix = dot(gate_high, slots_out, tn) + dot(gate_low, slots_out, tn)
    block_out = (hidden + dense_out + expert_mix).astype(bf16)

    expert_back = dot(token_map, slots_back, tn)
    grad_normed_two = dense_back + expert_back
    grad_hidden_norm, grad_gain_two = norm_back(hidden, gain_two, grad_normed_two)
    grad_hidden = cotangent.astype(f32) + grad_hidden_norm

    grad_attn_in = gather_blocks(grad_hidden.astype(bf16))
    grad_output_t = dot(grad_attn_in, attended, tn)
    grad_attended = dot(grad_attn_in, output_t, nn).astype(bf16).reshape(per_head)
    softmaxed = jnp.exp(scores_of() - log_total)
    grad_soft = jnp.einsum("qhd,khd->hqk", grad_attended, values_all, preferred_element_type=f32)
    inner_sum = jnp.sum(softmaxed * grad_soft, axis=-1, keepdims=True)
    grad_scores = (softmaxed * (grad_soft - inner_sum)).astype(bf16)
    grad_queries = (
        jnp.einsum("hqk,khd->qhd", grad_scores, keys_all, preferred_element_type=f32) * score_scale
    )
    grad_keys = (
        jnp.einsum("hqk,qhd->khd", grad_scores, queries, preferred_element_type=f32) * score_scale
    )
    grad_values = jnp.einsum(
        "hqk,qhd->khd", softmaxed.astype(bf16), grad_attended, preferred_element_type=f32
    )
    grad_projected = jnp.concatenate(
        [
            rotary(grad_queries, positions, -1.0).astype(bf16).reshape(length, columns),
            rotary(grad_keys, positions, -1.0).astype(bf16).reshape(length, columns),
            grad_values.astype(bf16).reshape(length, columns),
        ],
        axis=1,
    )
    grad_mixer = dot(normed_all, grad_projected, tn)
    normed_back = dot(grad_projected, mixer, nt)
    inverse_all = lax.rsqrt(jnp.mean(inputs_all * inputs_all, axis=-1, keepdims=True) + epsilon)
    gains = jnp.stack([jnp.sum(normed_back * inputs_all * inverse_all, axis=0), grad_gain_two])
    gains = gains + to_across(gains)
    gains = gains + to_beside(gains)
    first_grad = jnp.concatenate(
        [
            grad_mixer.astype(bf16),
            gains.T.astype(bf16),
            jnp.zeros((width, gain_width - 2), bf16),
            grad_output_t.astype(bf16),
            jnp.zeros((width, pad_width), bf16),
        ],
        axis=1,
    )
    first_parts = lax.all_to_all(
        first_grad.reshape(dp_count, shard, -1), "dp", split_axis=0, concat_axis=0, tiled=True
    )
    first_total = jnp.sum(first_parts.astype(f32), axis=0)
    grad_normed_one = sum_blocks(normed_back)
    grad_input_norm, _ = norm_back(inputs, gain_one, grad_normed_one)
    grad_tokens = grad_hidden + grad_input_norm
    return (
        block_out,
        grad_tokens,
        first_total[:, 3 * columns],
        first_total[:, :columns],
        first_total[:, columns : 2 * columns],
        first_total[:, 2 * columns : 3 * columns],
        first_total[:, 3 * columns + gain_width :][:, :columns].T,
        first_total[:, 3 * columns + 1],
        second_total[:, :hidden_cols],
        second_total[:, hidden_cols : 2 * hidden_cols],
        second_total[:, 2 * hidden_cols :].T,
        gate_total,
        up_total,
        down_total,
    )


def gather_rows(rows_in):
    return lax.all_gather(rows_in, "tensor", axis=0, tiled=True)


def sum_rows(rows_in):
    return lax.psum_scatter(rows_in, "tensor", scatter_dimension=0, tiled=True)


def gather_attn_rows(rows_in):
    return lax.all_gather(rows_in, "tensor", axis=0, tiled=True)


def sum_attn_rows(rows_in):
    return lax.psum_scatter(rows_in, "tensor", scatter_dimension=0, tiled=True)


def general(
    tokens,
    cotangent,
    gain_attn,
    w_query,
    w_key,
    w_value,
    w_output,
    gain_ffn,
    dense_gate,
    dense_up,
    dense_down,
    expert_gate,
    expert_up,
    expert_down,
    routes,
    slot_order,
    gate_values,
    prefix_len,
):
    dp_count = lax.axis_size("dp")
    tensor_count = lax.axis_size("tensor")
    local_rows = tokens.shape[0]
    model_width = tokens.shape[1]
    length = local_rows * tensor_count
    splits = max(1, dp_count // EXPERTS)
    per_device = max(1, EXPERTS // dp_count)
    inputs = tokens.astype(jnp.float32)
    dense_all = (
        lax.all_gather(gain_attn, "dp", axis=0, tiled=True),
        lax.all_gather(w_query, "dp", axis=0, tiled=True),
        lax.all_gather(w_key, "dp", axis=0, tiled=True),
        lax.all_gather(w_value, "dp", axis=0, tiled=True),
        lax.all_gather(w_output, "dp", axis=1, tiled=True),
        lax.all_gather(gain_ffn, "dp", axis=0, tiled=True),
        lax.all_gather(dense_gate, "dp", axis=0, tiled=True),
        lax.all_gather(dense_up, "dp", axis=0, tiled=True),
        lax.all_gather(dense_down, "dp", axis=1, tiled=True),
    )
    (
        gain_one,
        query_full,
        key_full,
        value_full,
        output_full,
        gain_two,
        gate_full,
        up_full,
        down_full,
    ) = dense_all
    gain_one = gain_one.astype(jnp.float32)
    gain_two = gain_two.astype(jnp.float32)
    positions = jnp.arange(length, dtype=jnp.int32)
    prefix_value = prefix_len[0]
    normed_one = norm_rows(inputs, gain_one).astype(jnp.bfloat16)
    head_count = query_full.shape[1] // HEAD_DIM
    normed_all = gather_attn_rows(normed_one)
    queries = rotary(
        jnp.dot(normed_all, query_full, preferred_element_type=jnp.float32).reshape(
            length, head_count, HEAD_DIM
        ),
        positions,
        1.0,
    ).astype(jnp.bfloat16)
    keys_all = rotary(
        jnp.dot(normed_all, key_full, preferred_element_type=jnp.float32).reshape(
            length, head_count, HEAD_DIM
        ),
        positions,
        1.0,
    ).astype(jnp.bfloat16)
    values_all = (
        jnp.dot(normed_all, value_full, preferred_element_type=jnp.float32)
        .astype(jnp.bfloat16)
        .reshape(length, head_count, HEAD_DIM)
    )
    score_scale = 1.0 / math.sqrt(HEAD_DIM)
    block_rows = min(512, length)
    blocks = length // block_rows
    query_blocks = queries.reshape(blocks, block_rows, head_count, HEAD_DIM)
    position_blocks = positions.reshape(blocks, block_rows)

    def block_scores(block_query, block_pos):
        scores = (
            jnp.einsum("qhd,khd->hqk", block_query, keys_all, preferred_element_type=jnp.float32)
            * score_scale
        )
        visible = (positions[None, :] <= block_pos[:, None]) | (positions[None, :] < prefix_value)
        return jnp.where(visible[None], scores, -1e30)

    def attend(block_item):
        block_query, block_pos = block_item
        scores = block_scores(block_query, block_pos)
        row_top = jnp.max(scores, axis=-1, keepdims=True)
        exponent = jnp.exp(scores - row_top)
        row_total = jnp.sum(exponent, axis=-1, keepdims=True)
        softmaxed = exponent / row_total
        mixture = jnp.einsum(
            "hqk,khd->qhd",
            softmaxed.astype(jnp.bfloat16),
            values_all,
            preferred_element_type=jnp.float32,
        ).astype(jnp.bfloat16)
        return (mixture, (row_top + jnp.log(row_total))[..., 0])

    attended, log_totals = lax.map(attend, (query_blocks, position_blocks))
    attended = attended.reshape(length, head_count * HEAD_DIM)
    hidden = inputs + sum_attn_rows(
        jnp.dot(attended, output_full, preferred_element_type=jnp.float32)
    )
    normed_two = norm_rows(hidden, gain_two).astype(jnp.bfloat16)
    normed_two_all = gather_rows(normed_two)
    gate_pre = jnp.dot(normed_two_all, gate_full, preferred_element_type=jnp.float32)
    up_pre = jnp.dot(normed_two_all, up_full, preferred_element_type=jnp.float32)
    activated = (jax.nn.silu(gate_pre) * up_pre).astype(jnp.bfloat16)
    dense_out = sum_rows(jnp.dot(activated, down_full, preferred_element_type=jnp.float32))
    expert_ids = routes.reshape(-1)
    ranking = slot_order.reshape(-1)
    same_expert = expert_ids[:, None] == expert_ids[None, :]
    earlier = ranking[None, :] < ranking[:, None]
    placed = jnp.sum((same_expert & earlier).astype(jnp.int32), axis=1)
    usable = placed < CAP
    targets = jnp.where(usable, expert_ids * CAP + placed, -1)
    slot_ids = jnp.arange(EXPERTS * CAP, dtype=jnp.int32)
    pair_map = (slot_ids[:, None] == targets[None, :]).astype(jnp.float32)
    token_map = jnp.sum(pair_map.reshape(EXPERTS * CAP, local_rows, TOP), axis=2).astype(
        jnp.bfloat16
    )
    dispatched = jnp.dot(token_map, normed_two, preferred_element_type=jnp.float32).astype(
        jnp.bfloat16
    )
    outgoing = jnp.broadcast_to(
        dispatched.reshape(EXPERTS, 1, CAP, model_width), (EXPERTS, splits, CAP, model_width)
    ).reshape(dp_count, per_device, CAP, model_width)
    expert_all = (
        lax.all_gather(expert_gate, "tensor", axis=0, tiled=True),
        lax.all_gather(expert_up, "tensor", axis=0, tiled=True),
        lax.all_gather(expert_down, "tensor", axis=1, tiled=True),
    )
    piece_width = expert_all[0].shape[1] // per_device
    gate_pieces = expert_all[0].reshape(model_width, per_device, piece_width)
    up_pieces = expert_all[1].reshape(model_width, per_device, piece_width)
    down_pieces = expert_all[2].reshape(per_device, piece_width, model_width)
    received = lax.all_to_all(outgoing, "dp", split_axis=0, concat_axis=0, tiled=True)
    gate_local = jnp.einsum(
        "sjnd,djp->sjnp", received, gate_pieces, preferred_element_type=jnp.float32
    )
    up_local = jnp.einsum("sjnd,djp->sjnp", received, up_pieces, preferred_element_type=jnp.float32)
    active_local = (jax.nn.silu(gate_local) * up_local).astype(jnp.bfloat16)
    result_local = jnp.einsum(
        "sjnp,jpd->sjnd", active_local, down_pieces, preferred_element_type=jnp.float32
    ).astype(jnp.bfloat16)
    returned = lax.all_to_all(result_local, "dp", split_axis=0, concat_axis=0, tiled=True)
    returned, kept_in, gate_local, up_local = (returned, received, gate_local, up_local)
    expert_sums = jnp.sum(
        returned.reshape(EXPERTS, splits, CAP, model_width).astype(jnp.float32), axis=1
    ).reshape(EXPERTS * CAP, model_width)
    pick_index = jnp.where(usable, targets, 0)
    pair_weight = jnp.where(usable, gate_values.reshape(-1), 0.0)
    picked = jnp.take(expert_sums, pick_index, axis=0) * pair_weight[:, None]
    expert_mix = jnp.sum(picked.reshape(local_rows, TOP, model_width), axis=1)
    block_out = (hidden + dense_out + expert_mix).astype(jnp.bfloat16)
    dense_back = (
        lax.all_gather(gain_attn, "dp", axis=0, tiled=True),
        lax.all_gather(w_query, "dp", axis=0, tiled=True),
        lax.all_gather(w_key, "dp", axis=0, tiled=True),
        lax.all_gather(w_value, "dp", axis=0, tiled=True),
        lax.all_gather(w_output, "dp", axis=1, tiled=True),
        lax.all_gather(gain_ffn, "dp", axis=0, tiled=True),
        lax.all_gather(dense_gate, "dp", axis=0, tiled=True),
        lax.all_gather(dense_up, "dp", axis=0, tiled=True),
        lax.all_gather(dense_down, "dp", axis=1, tiled=True),
    )
    (
        gain_one,
        query_full,
        key_full,
        value_full,
        output_full,
        gain_two,
        gate_full,
        up_full,
        down_full,
    ) = dense_back
    gain_one = gain_one.astype(jnp.float32)
    gain_two = gain_two.astype(jnp.float32)
    grad_out = cotangent.astype(jnp.float32)
    cotangent_all = gather_rows(cotangent)
    grad_down = jnp.einsum(
        "lf,ld->fd", activated, cotangent_all, preferred_element_type=jnp.float32
    )
    grad_act = jnp.einsum("ld,fd->lf", cotangent_all, down_full, preferred_element_type=jnp.float32)
    grad_gate_pre, grad_up_pre = swiglu_back(grad_act, gate_pre, up_pre)
    grad_gate = jnp.einsum(
        "ld,lf->df", normed_two_all, grad_gate_pre, preferred_element_type=jnp.float32
    )
    grad_up = jnp.einsum(
        "ld,lf->df", normed_two_all, grad_up_pre, preferred_element_type=jnp.float32
    )
    dense_back_in = jnp.einsum(
        "lf,df->ld", grad_gate_pre, gate_full, preferred_element_type=jnp.float32
    ) + jnp.einsum("lf,df->ld", grad_up_pre, up_full, preferred_element_type=jnp.float32)
    slot_gate = jnp.dot(pair_map, gate_values.reshape(-1), precision=lax.Precision.HIGHEST)
    slot_cotangent = jnp.dot(token_map, cotangent, preferred_element_type=jnp.float32)
    grad_slots = (slot_cotangent * slot_gate[:, None]).astype(jnp.bfloat16)
    grad_outgoing = jnp.broadcast_to(
        grad_slots.reshape(EXPERTS, 1, CAP, model_width), (EXPERTS, splits, CAP, model_width)
    ).reshape(dp_count, per_device, CAP, model_width)
    grad_received = lax.all_to_all(grad_outgoing, "dp", split_axis=0, concat_axis=0, tiled=True)
    active_local = (jax.nn.silu(gate_local) * up_local).astype(jnp.bfloat16)
    grad_down_expert = jnp.einsum(
        "sjnp,sjnd->jpd", active_local, grad_received, preferred_element_type=jnp.float32
    ).reshape(per_device * piece_width, model_width)
    grad_act_expert = jnp.einsum(
        "sjnd,jpd->sjnp", grad_received, down_pieces, preferred_element_type=jnp.float32
    )
    grad_gate_local, grad_up_local = swiglu_back(grad_act_expert, gate_local, up_local)
    grad_gate_expert = jnp.einsum(
        "sjnd,sjnp->djp", kept_in, grad_gate_local, preferred_element_type=jnp.float32
    ).reshape(model_width, per_device * piece_width)
    grad_up_expert = jnp.einsum(
        "sjnd,sjnp->djp", kept_in, grad_up_local, preferred_element_type=jnp.float32
    ).reshape(model_width, per_device * piece_width)
    grad_in_expert = (
        jnp.einsum(
            "sjnp,djp->sjnd", grad_gate_local, gate_pieces, preferred_element_type=jnp.float32
        )
        + jnp.einsum("sjnp,djp->sjnd", grad_up_local, up_pieces, preferred_element_type=jnp.float32)
    ).astype(jnp.bfloat16)
    grad_back = lax.all_to_all(grad_in_expert, "dp", split_axis=0, concat_axis=0, tiled=True)
    grad_slots_in = jnp.sum(
        grad_back.reshape(EXPERTS, splits, CAP, model_width).astype(jnp.float32), axis=1
    ).reshape(EXPERTS * CAP, model_width)
    grad_pairs = jnp.where(usable[:, None], jnp.take(grad_slots_in, pick_index, axis=0), 0.0)
    expert_back = jnp.sum(grad_pairs.reshape(local_rows, TOP, model_width), axis=1)
    grad_normed_two = sum_rows(dense_back_in) + expert_back
    grad_hidden_norm, grad_gain_two_part = norm_back(hidden, gain_two, grad_normed_two)
    grad_hidden = grad_out + grad_hidden_norm
    query_use, key_use, value_use, output_use = (query_full, key_full, value_full, output_full)
    grad_attn_in = gather_attn_rows(grad_hidden.astype(jnp.bfloat16))
    grad_output_w = jnp.einsum(
        "lc,ld->cd", attended, grad_attn_in, preferred_element_type=jnp.float32
    )
    grad_attended = (
        jnp.einsum("ld,cd->lc", grad_attn_in, output_use, preferred_element_type=jnp.float32)
        .astype(jnp.bfloat16)
        .reshape(blocks, block_rows, head_count, HEAD_DIM)
    )

    def attend_back(running, block_item):
        grad_keys, grad_values = running
        block_query, block_pos, block_grad, block_total = block_item
        scores = block_scores(block_query, block_pos)
        softmaxed = jnp.exp(scores - block_total[..., None])
        grad_soft = jnp.einsum(
            "qhd,khd->hqk", block_grad, values_all, preferred_element_type=jnp.float32
        )
        inner_sum = jnp.sum(softmaxed * grad_soft, axis=-1, keepdims=True)
        grad_scores = (softmaxed * (grad_soft - inner_sum)).astype(jnp.bfloat16)
        grad_block = (
            jnp.einsum("hqk,khd->qhd", grad_scores, keys_all, preferred_element_type=jnp.float32)
            * score_scale
        )
        grad_keys = (
            grad_keys
            + jnp.einsum(
                "hqk,qhd->khd", grad_scores, block_query, preferred_element_type=jnp.float32
            )
            * score_scale
        )
        grad_values = grad_values + jnp.einsum(
            "hqk,qhd->khd",
            softmaxed.astype(jnp.bfloat16),
            block_grad,
            preferred_element_type=jnp.float32,
        )
        return ((grad_keys, grad_values), grad_block)

    zero_start = (
        jnp.zeros((length, head_count, HEAD_DIM), jnp.float32),
        jnp.zeros((length, head_count, HEAD_DIM), jnp.float32),
    )
    (grad_keys, grad_values), grad_queries = lax.scan(
        attend_back, zero_start, (query_blocks, position_blocks, grad_attended, log_totals)
    )
    grad_queries = (
        rotary(grad_queries.reshape(length, head_count, HEAD_DIM), positions, -1.0)
        .astype(jnp.bfloat16)
        .reshape(length, head_count * HEAD_DIM)
    )
    grad_keys = (
        rotary(grad_keys, positions, -1.0)
        .astype(jnp.bfloat16)
        .reshape(length, head_count * HEAD_DIM)
    )
    grad_values = grad_values.astype(jnp.bfloat16).reshape(length, head_count * HEAD_DIM)
    grad_query_w = jnp.einsum(
        "ld,lc->dc", normed_all, grad_queries, preferred_element_type=jnp.float32
    )
    grad_key_w = jnp.einsum("ld,lc->dc", normed_all, grad_keys, preferred_element_type=jnp.float32)
    grad_value_w = jnp.einsum(
        "ld,lc->dc", normed_all, grad_values, preferred_element_type=jnp.float32
    )
    normed_back_part = (
        jnp.einsum("lc,dc->ld", grad_queries, query_use, preferred_element_type=jnp.float32)
        + jnp.einsum("lc,dc->ld", grad_keys, key_use, preferred_element_type=jnp.float32)
        + jnp.einsum("lc,dc->ld", grad_values, value_use, preferred_element_type=jnp.float32)
    )
    grad_normed_one = sum_attn_rows(normed_back_part)
    grad_input_norm, grad_gain_one_part = norm_back(inputs, gain_one, grad_normed_one)
    grad_tokens = grad_hidden + grad_input_norm
    dense_grads = (
        lax.psum_scatter(grad_gain_one_part, "dp", scatter_dimension=0, tiled=True),
        lax.psum_scatter(grad_query_w, "dp", scatter_dimension=0, tiled=True),
        lax.psum_scatter(grad_key_w, "dp", scatter_dimension=0, tiled=True),
        lax.psum_scatter(grad_value_w, "dp", scatter_dimension=0, tiled=True),
        lax.psum_scatter(grad_output_w, "dp", scatter_dimension=1, tiled=True),
        lax.psum_scatter(grad_gain_two_part, "dp", scatter_dimension=0, tiled=True),
        lax.psum_scatter(grad_gate, "dp", scatter_dimension=0, tiled=True),
        lax.psum_scatter(grad_up, "dp", scatter_dimension=0, tiled=True),
        lax.psum_scatter(grad_down, "dp", scatter_dimension=1, tiled=True),
    )
    gain_totals = lax.psum((dense_grads[0], dense_grads[5]), "tensor")
    expert_grads = (
        lax.psum_scatter(
            grad_gate_expert.astype(jnp.bfloat16), "tensor", scatter_dimension=0, tiled=True
        ).astype(jnp.float32),
        lax.psum_scatter(
            grad_up_expert.astype(jnp.bfloat16), "tensor", scatter_dimension=0, tiled=True
        ).astype(jnp.float32),
        lax.psum_scatter(
            grad_down_expert.astype(jnp.bfloat16), "tensor", scatter_dimension=1, tiled=True
        ).astype(jnp.float32),
    )
    return (
        block_out,
        grad_tokens,
        gain_totals[0],
        dense_grads[1],
        dense_grads[2],
        dense_grads[3],
        dense_grads[4],
        gain_totals[1],
        dense_grads[6],
        dense_grads[7],
        dense_grads[8],
        expert_grads[0],
        expert_grads[1],
        expert_grads[2],
    )


def solution(mesh):
    sizes = mesh.shape
    in_pairs = sizes["tensor"] == 4 and sizes["dp"] * 2 == EXPERTS
    local = paired if in_pairs else general
    return jax.shard_map(
        local,
        mesh=mesh,
        in_specs=(
            P(("dp", "tensor"), None),
            P(("dp", "tensor"), None),
            P("dp"),
            P("dp", "tensor"),
            P("dp", "tensor"),
            P("dp", "tensor"),
            P("tensor", "dp"),
            P("dp"),
            P("dp", "tensor"),
            P("dp", "tensor"),
            P("tensor", "dp"),
            P("tensor", "dp"),
            P("tensor", "dp"),
            P("dp", "tensor"),
            P(("dp", "tensor"), None),
            P(("dp", "tensor"), None),
            P(("dp", "tensor"), None),
            P("dp"),
        ),
        out_specs=(
            P(("dp", "tensor"), None),
            P(("dp", "tensor"), None),
            P("dp"),
            P("dp", "tensor"),
            P("dp", "tensor"),
            P("dp", "tensor"),
            P("tensor", "dp"),
            P("dp"),
            P("dp", "tensor"),
            P("dp", "tensor"),
            P("tensor", "dp"),
            P("tensor", "dp"),
            P("tensor", "dp"),
            P("dp", "tensor"),
        ),
        check_vma=False,
    )
```

```python
import math

import jax
import jax.numpy as jnp
import numpy as np
from jax import lax
from jax.experimental import pallas as pl
from jax.experimental.pallas import tpu as pltpu
from jax.sharding import PartitionSpec as P

HEAD_DIM = 64
EXPERTS = 16
TOP = 2
CAP = 40


epsilon = 1e-06


def norm_rows(rows_in, gain_row):
    return (
        rows_in
        * lax.rsqrt(jnp.mean(rows_in * rows_in, axis=-1, keepdims=True) + epsilon)
        * gain_row
    )


def norm_back(rows_in, gain_row, grad_out):
    inverse = lax.rsqrt(jnp.mean(rows_in * rows_in, axis=-1, keepdims=True) + epsilon)
    scaled = grad_out * gain_row
    grad_rows = inverse * scaled - rows_in * inverse**3 * jnp.mean(
        scaled * rows_in, axis=-1, keepdims=True
    )
    grad_gain = jnp.sum(grad_out * rows_in * inverse, axis=0)
    return (grad_rows, grad_gain)


def rotary(values, positions, direction):
    half_width = values.shape[-1] // 2
    frequency = jnp.power(10000.0, -jnp.arange(half_width).astype(jnp.float32) / half_width)
    angles = positions[:, None].astype(jnp.float32) * frequency[None, :]
    cosine = jnp.cos(angles)[:, None, :]
    sine_part = direction * jnp.sin(angles)[:, None, :]
    first_half = values[..., :half_width]
    second_half = values[..., half_width:]
    return jnp.concatenate(
        [
            first_half * cosine - second_half * sine_part,
            second_half * cosine + first_half * sine_part,
        ],
        axis=-1,
    )


def swiglu_back(grad_act, gate_pre, up_pre):
    sigmoid = jax.nn.sigmoid(gate_pre)
    silu_value = gate_pre * sigmoid
    grad_gate = grad_act * up_pre * sigmoid * (1.0 + gate_pre * (1.0 - sigmoid))
    grad_up = grad_act * silu_value
    return (grad_gate.astype(jnp.bfloat16), grad_up.astype(jnp.bfloat16))


def to_across(values):
    return lax.ppermute(values, "tensor", [(i, i ^ 2) for i in range(4)])


def to_beside(values):
    return lax.ppermute(values, "tensor", [(i, i ^ 1) for i in range(4)])


def gather_blocks(rows_in):
    near = jnp.stack([rows_in, to_across(rows_in)])
    return jnp.concatenate([near, to_beside(near)]).reshape(-1, rows_in.shape[-1])


def after(value, *before):
    return lax.optimization_barrier((value,) + before)[0]


def sum_blocks(partial):
    blocks = partial.reshape(4, -1, partial.shape[-1])
    near = blocks[:2] + to_beside(blocks[2:].astype(jnp.bfloat16)).astype(jnp.float32)
    return near[0] + to_across(near[1].astype(jnp.bfloat16)).astype(jnp.float32)


def along(values, axis, k):
    return lax.ppermute(values, axis, [(i, i ^ k) for i in range(lax.axis_size(axis))])


def gather_line(rows_in):
    return [along(rows_in, "dp", k) if k else rows_in for k in range(0, lax.axis_size("dp"), 2)]


def gather_pairs(line):
    return [part for own in line for part in (own, along(own, "dp", 1))]


def pair_halves(grad):
    count = lax.axis_size("dp")
    place = lax.axis_index("dp")
    blocks = grad.reshape(count // 2, 2, -1, grad.shape[1])
    mine = lax.dynamic_index_in_dim(blocks, place % 2, 1, keepdims=False)
    other = lax.dynamic_index_in_dim(blocks, 1 - place % 2, 1, keepdims=False)
    return mine, along(other, "dp", 1)


def send_line(halves):
    line = lax.axis_index("dp") // 2
    whole = halves[0].astype(jnp.float32) + halves[1].astype(jnp.float32)
    parts = [lax.dynamic_index_in_dim(whole, line, 0, keepdims=False)]
    for k in range(1, whole.shape[0]):
        part = lax.dynamic_index_in_dim(whole, line ^ k, 0, keepdims=False)
        parts.append(along(part.astype(jnp.bfloat16), "dp", 2 * k))
    return parts


def dot(left, right, dims):
    return lax.dot_general(left, right, (dims, ((), ())), preferred_element_type=jnp.float32)


NN, NT, TN = ((1,), (0,)), ((1,), (1,)), ((0,), (0,))
ORDER = (0, 2, 1, 3)
VMEM = pl.BlockSpec(memory_space=pltpu.VMEM)
SMEM = pl.BlockSpec(memory_space=pltpu.SMEM)
HBM = pl.BlockSpec(memory_space=pltpu.HBM)
NO_COST = pl.CostEstimate(flops=0, bytes_accessed=0, transcendentals=0)


def angle_tables(length):
    half = HEAD_DIM // 2
    lane = np.arange(2 * HEAD_DIM)
    frequency = np.power(10000.0, -(lane % half).astype(np.float64) / half)
    angles = np.arange(length)[:, None] * frequency[None, :]
    sign = np.where(lane % HEAD_DIM < half, -1.0, 1.0)
    return np.cos(angles).astype(np.float32), (np.sin(angles) * sign).astype(np.float32)


def turn(values, cosine, sine):
    width = values.shape[1]
    half = HEAD_DIM // 2
    lane = lax.broadcasted_iota(jnp.int32, values.shape, 1)
    swapped = jnp.where(
        lane % HEAD_DIM < half,
        pltpu.roll(values, width - half, 1),
        pltpu.roll(values, half, 1),
    )
    repeats = width // cosine.shape[1]
    return values * jnp.concatenate([cosine] * repeats, axis=1) + swapped * jnp.concatenate(
        [sine] * repeats, axis=1
    )


def block_at(place, i):
    return place ^ ((i >> 1) | ((i & 1) << 1))


def seen(place, prefix, i, j, rows):
    query_block, key_block = block_at(place, i), block_at(place, j)
    return (key_block <= query_block) | (key_block * rows < prefix)


def mask_of(place, prefix, i, j, rows):
    key = block_at(place, j) * rows + lax.broadcasted_iota(jnp.int32, (rows, rows), 0)
    query = block_at(place, i) * rows + lax.broadcasted_iota(jnp.int32, (rows, rows), 1)
    return key <= jnp.maximum(query, prefix - 1)


def attend_kernel(where, near, far, parts, length, columns):
    rows, width = near.shape[1], near.shape[2]
    shard, lanes = parts[0].shape
    blocks = length // rows
    heads = columns // HEAD_DIM
    count = len(parts)
    gain_at = 3 * columns
    output_at = 3 * columns + 64
    bf16, f32 = jnp.bfloat16, jnp.float32
    cosine, sine = angle_tables(length)

    def body(*refs):
        spot, near_ref, far_ref = refs[:3]
        part_refs = refs[3 : 3 + count]
        cos_ref, sin_ref = refs[3 + count : 5 + count]
        (
            normed_ref,
            weight_ref,
            gain_ref,
            query_ref,
            query_t_ref,
            key_ref,
            value_ref,
            mixed_ref,
            mixed_t_ref,
            log_ref,
            sum_near_ref,
            sum_far_ref,
        ) = refs[5 + count : 17 + count]
        value_t_ref, score_ref, top_ref, total_ref, mix_ref, *keep, sems = refs[17 + count :]
        outward = [
            pltpu.make_async_copy(source, target, sems.at[n])
            for n, (source, target) in enumerate(
                zip(
                    keep,
                    (
                        normed_ref,
                        weight_ref,
                        query_ref,
                        query_t_ref,
                        key_ref,
                        value_ref,
                        mixed_ref,
                        mixed_t_ref,
                    ),
                )
            )
        ]
        (
            normed_ref,
            weight_ref,
            query_ref,
            query_t_ref,
            key_ref,
            value_ref,
            mixed_ref,
            mixed_t_ref,
        ) = keep
        place, dp_place, prefix = spot[0], spot[1], spot[2]
        for k in range(count):
            start = pl.multiple_of((dp_place ^ k) * shard, 16)
            weight_ref[pl.ds(start, shard), :] = part_refs[k][...]
        gain_tile = weight_ref[:, gain_at // 128 * 128 : gain_at // 128 * 128 + 128].astype(f32)
        gain_ref[...] = gain_tile.T[gain_at % 128 : gain_at % 128 + 8, :]
        gain = gain_ref[0:1, :]
        for i in range(blocks):
            tokens = (near_ref if i < 2 else far_ref)[i % 2].astype(f32)
            inverse = lax.rsqrt(jnp.mean(tokens * tokens, axis=-1, keepdims=True) + epsilon)
            normed = (tokens * inverse * gain).astype(bf16)
            span = pl.ds(i * rows, rows)
            normed_ref[span, :] = normed
            product = dot(normed, weight_ref[:, : 3 * columns], NN)
            spot_rows = pl.ds(pl.multiple_of(block_at(place, i) * rows, 8), rows)
            turned = turn(product[:, : 2 * columns], cos_ref[spot_rows, :], sin_ref[spot_rows, :])
            query = turned[:, :columns] * (1.0 / math.sqrt(HEAD_DIM))
            key = turned[:, columns:]
            value = product[:, 2 * columns :]
            query_t = query.T
            value_t = value.T
            for h in range(heads):
                cut = slice(h * HEAD_DIM, (h + 1) * HEAD_DIM)
                query_ref[h, span, :] = query[:, cut].astype(bf16)
                query_t_ref[h, :, span] = query_t[cut, :].astype(bf16)
                key_ref[h, span, :] = key[:, cut].astype(bf16)
                value_ref[h, span, :] = value[:, cut].astype(bf16)
                value_t_ref[h, :, span] = value_t[cut, :].astype(bf16)

        for copy in outward[:6]:
            copy.start()

        def query_block(i, carry):
            here = pl.ds(pl.multiple_of(i * rows, 128), rows)
            top_ref[...] = jnp.full(top_ref.shape, -1e30, f32)
            total_ref[...] = jnp.zeros(total_ref.shape, f32)
            mix_ref[...] = jnp.zeros(mix_ref.shape, f32)

            def scores(j, carry):
                @pl.when(seen(place, prefix, i, j, rows))
                def _():
                    there = pl.ds(pl.multiple_of(j * rows, 128), rows)
                    visible = mask_of(place, prefix, i, j, rows)
                    for h in range(heads):
                        score = dot(key_ref[h, there, :], query_t_ref[h, :, here], NN)
                        score = jnp.where(visible, score, -1e30)
                        score_ref[h, there, :] = score
                        top_ref[h : h + 1, :] = jnp.maximum(
                            top_ref[h : h + 1, :], jnp.max(score, axis=0, keepdims=True)
                        )

                return carry

            def mixing(j, carry):
                @pl.when(seen(place, prefix, i, j, rows))
                def _():
                    there = pl.ds(pl.multiple_of(j * rows, 128), rows)
                    for h in range(heads):
                        power = jnp.exp(score_ref[h, there, :] - top_ref[h : h + 1, :])
                        total_ref[h : h + 1, :] += jnp.sum(power, axis=0, keepdims=True)
                        mix_ref[h] += dot(value_t_ref[h, :, there], power.astype(bf16), NN)

                return carry

            lax.fori_loop(0, blocks, scores, 0)
            lax.fori_loop(0, blocks, mixing, 0)
            log_ref[:, here] = top_ref[...] + jnp.log(jnp.maximum(total_ref[...], 1e-30))
            mixed_t = jnp.concatenate(
                [mix_ref[h] * (1.0 / total_ref[h : h + 1, :]) for h in range(heads)], axis=0
            )
            for h in range(heads):
                mixed_t_ref[h, :, here] = mixed_t[h * HEAD_DIM : (h + 1) * HEAD_DIM, :].astype(bf16)
            mixed = mixed_t.T.astype(bf16)
            mixed_ref[here, :] = mixed
            partial = dot(mixed, weight_ref[:, output_at : output_at + columns], NT)

            @pl.when(i < 2)
            def _():
                sum_near_ref[i] = partial

            @pl.when(i >= 2)
            def _():
                sum_far_ref[i - 2] = partial.astype(bf16)

            return carry

        lax.fori_loop(0, blocks, query_block, 0)
        for copy in outward[6:]:
            copy.start()
        for copy in outward:
            copy.wait()

    per_head = (heads, length, HEAD_DIM)
    per_head_t = (heads, HEAD_DIM, length)
    out_shape = [
        jax.ShapeDtypeStruct(shape, kind)
        for shape, kind in (
            ((length, width), bf16),
            ((count * shard, lanes), bf16),
            ((8, width), f32),
            (per_head, bf16),
            (per_head_t, bf16),
            (per_head, bf16),
            (per_head, bf16),
            ((length, columns), bf16),
            (per_head_t, bf16),
            ((8, length), f32),
            ((2, rows, width), f32),
            ((2, rows, width), bf16),
        )
    ]
    return pl.pallas_call(
        body,
        out_shape=out_shape,
        in_specs=[SMEM] + [VMEM] * (4 + count),
        out_specs=[HBM] * 2 + [VMEM] + [HBM] * 6 + [VMEM] * 3,
        scratch_shapes=[
            pltpu.VMEM(per_head_t, bf16),
            pltpu.VMEM((heads, length, rows), f32),
            pltpu.VMEM((8, rows), f32),
            pltpu.VMEM((8, rows), f32),
            pltpu.VMEM((heads, HEAD_DIM, rows), f32),
        ]
        + [pltpu.VMEM(out_shape[n].shape, bf16) for n in (0, 1, 3, 4, 5, 6, 7, 8)]
        + [pltpu.SemaphoreType.DMA((8,))],
        compiler_params=pltpu.CompilerParams(vmem_limit_bytes=60 * 2**20),
        cost_estimate=NO_COST,
    )(where, near, far, *parts, cosine, sine)


def attend_back_kernel(
    where, near, far, grad_near, grad_far, saved, gain_two, length, columns
):
    normed, weight, query, query_t, key, value, mixed, mixed_t, log_total = saved
    rows, width = near.shape[1], near.shape[2]
    lanes = weight.shape[1]
    blocks = length // rows
    heads = columns // HEAD_DIM
    output_at = 3 * columns + 64
    bf16, f32 = jnp.bfloat16, jnp.float32
    cosine, sine = angle_tables(length)

    def body(*refs):
        (
            spot,
            near_ref,
            far_ref,
            grad_near_ref,
            grad_far_ref,
            normed_ref,
            weight_ref,
            query_ref,
            query_t_ref,
            key_ref,
            value_ref,
            mixed_ref,
            mixed_t_ref,
            log_ref,
            gain_two_ref,
            cos_ref,
            sin_ref,
            first_ref,
            back_near_ref,
            back_far_ref,
            grad_in,
            grad_mix,
            grad_mix_t,
            inner,
            key_t,
            grad_query_t,
            grad_key,
            grad_value,
            grad_product,
            *keep,
            sems,
        ) = refs
        place, prefix = spot[0], spot[2]
        inward = [
            pltpu.make_async_copy(source, target, sems.at[n])
            for n, (source, target) in enumerate(
                zip(
                    (
                        weight_ref,
                        mixed_t_ref,
                        key_ref,
                        query_t_ref,
                        query_ref,
                        value_ref,
                        near_ref,
                        far_ref,
                        normed_ref,
                        mixed_ref,
                        cos_ref,
                        sin_ref,
                    ),
                    keep,
                )
            )
        ]
        for copy in inward:
            copy.start()
        (
            weight_ref,
            mixed_t_ref,
            key_ref,
            query_t_ref,
            query_ref,
            value_ref,
            near_ref,
            far_ref,
            normed_ref,
            mixed_ref,
            cos_ref,
            sin_ref,
        ) = keep
        grad_key[...] = jnp.zeros(grad_key.shape, f32)
        grad_value[...] = jnp.zeros(grad_value.shape, f32)
        grad_query_t[...] = jnp.zeros(grad_query_t.shape, f32)
        for copy in inward[:3]:
            copy.wait()
        for h in range(heads):
            key_t[h] = key_ref[h].astype(f32).T.astype(bf16)
        for i in range(blocks):
            span = pl.ds(i * rows, rows)
            grad = (grad_near_ref if i < 2 else grad_far_ref)[i % 2]
            grad_in[span, :] = grad
            mix = dot(grad, weight_ref[:, output_at : output_at + columns], NN)
            mix_t = mix.T
            for h in range(heads):
                cut = slice(h * HEAD_DIM, (h + 1) * HEAD_DIM)
                low = mix_t[cut, :].astype(bf16)
                grad_mix[h, span, :] = mix[:, cut].astype(bf16)
                grad_mix_t[h, :, span] = low
                inner[h : h + 1, span] = jnp.sum(
                    low.astype(f32) * mixed_t_ref[h, :, span].astype(f32), axis=0, keepdims=True
                )

        for copy in inward[3:6]:
            copy.wait()

        def pair(step, carry):
            i, j = step // blocks, step % blocks

            @pl.when(seen(place, prefix, i, j, rows))
            def _():
                here = pl.ds(pl.multiple_of(i * rows, 128), rows)
                there = pl.ds(pl.multiple_of(j * rows, 128), rows)
                visible = mask_of(place, prefix, i, j, rows)
                for h in range(heads):
                    score = dot(key_ref[h, there, :], query_t_ref[h, :, here], NN)
                    weigh = jnp.where(visible, jnp.exp(score - log_ref[h : h + 1, here]), 0.0)
                    soft = dot(value_ref[h, there, :], grad_mix_t[h, :, here], NN)
                    low = (weigh * (soft - inner[h : h + 1, here])).astype(bf16)
                    grad_value[h, there, :] += dot(weigh.astype(bf16), grad_mix[h, here, :], NN)
                    grad_key[h, there, :] += dot(low, query_ref[h, here, :], NN)
                    grad_query_t[h, :, here] += dot(key_t[h, :, there], low, NN)

            return carry

        lax.fori_loop(0, blocks * blocks, pair, 0)
        for copy in inward[6:]:
            copy.wait()
        gain = jnp.zeros((1, width), f32)
        for i in range(blocks):
            span = pl.ds(i * rows, rows)
            spot_rows = pl.ds(pl.multiple_of(block_at(place, i) * rows, 8), rows)
            turned = jnp.concatenate(
                [grad_query_t[h, :, span].T * (1.0 / math.sqrt(HEAD_DIM)) for h in range(heads)]
                + [grad_key[h, span, :] for h in range(heads)],
                axis=1,
            )
            turned = turn(turned, cos_ref[spot_rows, :], -sin_ref[spot_rows, :])
            grads = jnp.concatenate(
                [turned] + [grad_value[h, span, :] for h in range(heads)], axis=1
            ).astype(bf16)
            grad_product[span, :] = grads
            back = dot(grads, weight_ref[:, : 3 * columns], NT)
            tokens = (near_ref if i < 2 else far_ref)[i % 2].astype(f32)
            inverse = lax.rsqrt(jnp.mean(tokens * tokens, axis=-1, keepdims=True) + epsilon)
            gain += jnp.sum(back * tokens * inverse, axis=0, keepdims=True)
            if i < 2:
                back_near_ref[i] = back
            else:
                back_far_ref[i - 2] = back.astype(bf16)
        gains = jnp.concatenate([gain, gain_two_ref[...], jnp.zeros((62, width), f32)], axis=0)
        first_ref[:, 3 * columns : output_at] = gains.T.astype(bf16)
        first_ref[:, : 3 * columns] = dot(normed_ref[...], grad_product[...], TN).astype(bf16)
        first_ref[:, output_at : output_at + columns] = dot(
            grad_in[...], mixed_ref[...], TN
        ).astype(bf16)
        if output_at + columns < lanes:
            first_ref[:, output_at + columns :] = jnp.zeros(
                (width, lanes - output_at - columns), bf16
            )

    per_head = (heads, length, HEAD_DIM)
    per_head_t = (heads, HEAD_DIM, length)
    out_shape = [
        jax.ShapeDtypeStruct(shape, kind)
        for shape, kind in (
            ((width, lanes), bf16),
            ((2, rows, width), f32),
            ((2, rows, width), bf16),
        )
    ]
    return pl.pallas_call(
        body,
        out_shape=out_shape,
        in_specs=[SMEM] + [HBM] * 2 + [VMEM] * 2 + [HBM] * 8 + [VMEM] * 2 + [HBM] * 2,
        out_specs=[VMEM] * len(out_shape),
        scratch_shapes=[
            pltpu.VMEM((length, width), bf16),
            pltpu.VMEM(per_head, bf16),
            pltpu.VMEM(per_head_t, bf16),
            pltpu.VMEM((8, length), f32),
            pltpu.VMEM(per_head_t, bf16),
            pltpu.VMEM(per_head_t, f32),
            pltpu.VMEM(per_head, f32),
            pltpu.VMEM(per_head, f32),
            pltpu.VMEM((length, 3 * columns), bf16),
        ]
        + [
            pltpu.VMEM(array.shape, array.dtype)
            for array in (
                weight,
                mixed_t,
                key,
                query_t,
                query,
                value,
                near,
                far,
                normed,
                mixed,
                cosine,
                sine,
            )
        ]
        + [pltpu.SemaphoreType.DMA((12,))],
        compiler_params=pltpu.CompilerParams(vmem_limit_bytes=60 * 2**20),
        cost_estimate=NO_COST,
    )(where, near, far, grad_near, grad_far, *saved, gain_two, cosine, sine)


def gated(gate_pre, up_pre):
    sigmoid = 1.0 / (1.0 + jnp.exp(-gate_pre))
    return gate_pre * sigmoid * up_pre


def gated_back(grad, gate_pre, up_pre):
    sigmoid = 1.0 / (1.0 + jnp.exp(-gate_pre))
    silu = gate_pre * sigmoid
    grad_gate = grad * up_pre * (sigmoid + silu * (1.0 - sigmoid))
    return silu * up_pre, grad_gate, grad * silu


def call(body, out, *args, scratch=(), scalars=0, limit=48):
    bf16_kinds = [jax.ShapeDtypeStruct(shape, kind) for shape, kind in out]
    return pl.pallas_call(
        body,
        out_shape=bf16_kinds,
        in_specs=[SMEM] * scalars + [VMEM] * (len(args) - scalars),
        out_specs=[VMEM] * len(out),
        scratch_shapes=[pltpu.VMEM(shape, kind) for shape, kind in scratch],
        compiler_params=pltpu.CompilerParams(vmem_limit_bytes=limit * 2**20),
        cost_estimate=NO_COST,
    )(*args)


def join_rows(spot, refs, target):
    rows = refs[0].shape[0]
    for k, ref in enumerate(refs):
        target[pl.ds(pl.multiple_of((spot ^ k) * rows, 16), rows), :] = ref[...]


def expert_kernel(where, rows, grads, pair_in, down_in):
    count, width = rows[0].shape
    units = down_in[0].shape[1]
    step = count // 2
    bf16, f32 = jnp.bfloat16, jnp.float32

    def body(*refs):
        spot, rows_refs, grad_refs = refs[0], refs[1:3], refs[3:5]
        down_ref, own_ref, other_ref = refs[13:16]
        act_refs, back_gate_refs, back_up_refs = refs[16:18], refs[18:20], refs[20:22]
        gate_ref, up_ref = refs[22:]
        part = down_in[0].shape[0]
        join_rows(spot[0], [ref.at[:part] for ref in refs[5:9]], gate_ref)
        join_rows(spot[0], [ref.at[part:] for ref in refs[5:9]], up_ref)
        join_rows(spot[0], refs[9:13], down_ref)
        for half in (1, 0):

            def chunk(i, carry, half=half):
                span = pl.ds(pl.multiple_of(i * step, 16), step)
                row = rows_refs[half][span, :]
                gate_pre = dot(row, gate_ref[...], NN)
                up_pre = dot(row, up_ref[...], NN)
                grad = dot(grad_refs[half][span, :], down_ref[...], NN)
                act, grad_gate, grad_up = gated_back(grad, gate_pre, up_pre)
                grad_gate, grad_up = grad_gate.astype(bf16), grad_up.astype(bf16)
                act_refs[half][span, :] = act.astype(bf16)
                back_gate_refs[half][span, :] = grad_gate
                back_up_refs[half][span, :] = grad_up
                back = dot(grad_gate, gate_ref[...], NT) + dot(grad_up, up_ref[...], NT)
                if half:
                    other_ref[span, :] = back.astype(bf16)
                else:
                    own_ref[span, :] = back
                return carry

            lax.fori_loop(0, 2, chunk, 0)

    weight = ((4 * down_in[0].shape[0], units), bf16)
    saved = ((count, units), bf16)
    outs = call(
        body,
        [weight] + [((count, width), f32), ((count, width), bf16)] + [saved] * 6,
        where,
        *rows,
        *grads,
        *pair_in,
        *down_in,
        scratch=[weight] * 2,
        scalars=1,
        limit=52,
    )
    return outs[0], outs[1], outs[2], outs[3:5], outs[5:7], outs[7:9]


def expert_grad_kernel(rows, grads, acts, back_gates, back_ups, down):
    count, width = rows[0].shape
    units = acts[0].shape[1]
    step = 256
    bf16, f32 = jnp.bfloat16, jnp.float32

    def body(*refs):
        rows_refs, grad_refs, act_refs, gate_refs, up_refs = (refs[2 * n : 2 * n + 2] for n in range(5))
        down_ref, own_ref, other_ref, gate_out, rest_out = refs[10:15]

        def chunk(i, carry):
            span = pl.ds(pl.multiple_of(i * step, 128), step)
            for left, right, target, offset in (
                (rows_refs, gate_refs, gate_out, 0),
                (rows_refs, up_refs, rest_out, 0),
                (grad_refs, act_refs, rest_out, units),
            ):
                target[:, pl.ds(pl.multiple_of(offset + i * step, 128), step)] = (
                    dot(left[0][...], right[0][:, span], TN)
                    + dot(left[1][...], right[1][:, span], TN)
                ).astype(bf16)
            return carry

        lax.fori_loop(0, units // step, chunk, 0)
        own_ref[...] = dot(act_refs[0][...], down_ref[...], NT)
        other_ref[...] = dot(act_refs[1][...], down_ref[...], NT).astype(bf16)

    return call(
        body,
        [
            ((count, width), f32),
            ((count, width), bf16),
            ((width, units), bf16),
            ((width, 2 * units), bf16),
        ],
        *rows,
        *grads,
        *acts,
        *back_gates,
        *back_ups,
        down,
        limit=52,
    )


def dense_kernel(where, normed, cotangents, parts):
    _, rows, width = normed[0].shape
    count = len(parts)
    units = parts[0].shape[1] // 3
    bf16, f32 = jnp.bfloat16, jnp.float32

    def body(*refs):
        spot, near_ref, far_ref, grad_near_ref, grad_far_ref = refs[:5]
        back_near, back_far, out_near, out_far, total_ref = refs[5 + count : 10 + count]
        weight, normed_all, grad_all, wide, act_all = refs[10 + count :]
        join_rows(spot[1], refs[5 : 5 + count], weight)
        gate, up, down = (slice(n * units, (n + 1) * units) for n in range(3))
        for i in range(4):
            row = (near_ref if i < 2 else far_ref)[i % 2]
            grad_row = (grad_near_ref if i < 2 else grad_far_ref)[i % 2]
            span = slice(i * rows, (i + 1) * rows)
            normed_all[span, :] = row
            grad_all[span, :] = grad_row
            gate_pre = dot(row, weight[:, gate], NN)
            up_pre = dot(row, weight[:, up], NN)
            grad = dot(grad_row, weight[:, down], NN)
            act, grad_gate, grad_up = gated_back(grad, gate_pre, up_pre)
            act = act.astype(bf16)
            act_all[span, :] = act
            wide[span, :units] = grad_gate.astype(bf16)
            wide[span, units:] = grad_up.astype(bf16)
            out = dot(act, weight[:, down], NT)
            back = dot(wide[span, :], weight[:, : 2 * units], NT)
            if i < 2:
                out_near[i] = out
                back_near[i] = back
            else:
                out_far[i - 2] = out.astype(bf16)
                back_far[i - 2] = back.astype(bf16)
        total_ref[:, : 2 * units] = dot(normed_all[...], wide[...], TN).astype(bf16)
        total_ref[:, down] = dot(grad_all[...], act_all[...], TN).astype(bf16)

    blocks_f, blocks_b = ((2, rows, width), f32), ((2, rows, width), bf16)
    return call(
        body,
        [blocks_f, blocks_b, blocks_f, blocks_b, ((width, 3 * units), bf16)],
        where,
        *normed,
        *cotangents,
        *parts,
        scratch=[
            ((width, 3 * units), bf16),
            ((4 * rows, width), bf16),
            ((4 * rows, width), bf16),
            ((4 * rows, 2 * units), bf16),
            ((4 * rows, units), bf16),
        ],
        scalars=1,
    )


def join_kernel(where, gate_parts, rest_parts):
    rows, cols = gate_parts[0].shape
    f32 = jnp.float32

    def body(*refs):
        place = refs[0][0]
        gate_out, up_out, down_out = refs[9:]
        for k in range(4):
            span = pl.ds(pl.multiple_of((place ^ k) * cols, 128), cols)
            gate_out[:, span] = refs[1 + k][...].astype(f32)
            up_out[:, span] = refs[5 + k][:, :cols].astype(f32)
            down_out[:, span] = refs[5 + k][:, cols:].astype(f32)

    return call(
        body,
        [((rows, 4 * cols), f32)] * 3,
        where,
        *gate_parts,
        *rest_parts,
        scalars=1,
    )


def mix_kernel(hidden, dense, gate_map, slots_out):
    bf16, f32 = jnp.bfloat16, jnp.float32

    def body(hidden_ref, dense_ref, map_ref, slots_ref, out_ref):
        weights = map_ref[...]
        high = weights.astype(bf16)
        low = (weights - high.astype(f32)).astype(bf16)
        slots = slots_ref[...]
        mixed = dot(high, slots, TN) + dot(low, slots, TN)
        out_ref[...] = (hidden_ref[...] + dense_ref[...] + mixed).astype(bf16)

    return call(body, [(hidden.shape, bf16)], hidden, dense, gate_map, slots_out)[0]


def paired(
    tokens,
    cotangent,
    gain_attn,
    w_query,
    w_key,
    w_value,
    w_output,
    gain_ffn,
    dense_gate,
    dense_up,
    dense_down,
    expert_gate,
    expert_up,
    expert_down,
    routes,
    slot_order,
    gate_values,
    prefix_len,
):
    dp_count = lax.axis_size("dp")
    tensor_count = lax.axis_size("tensor")
    place = lax.axis_index("tensor")
    local_rows, width = tokens.shape
    length = local_rows * tensor_count
    columns = w_query.shape[1]
    shard = w_query.shape[0]
    hidden_cols = dense_gate.shape[1]
    devices = dp_count * tensor_count
    slots = EXPERTS * CAP
    bf16, f32 = jnp.bfloat16, jnp.float32

    nn, tn = NN, TN

    gain_width = 64
    pad_width = -(4 * columns + gain_width) % 128
    first_shard = jnp.concatenate(
        [
            w_query,
            w_key,
            w_value,
            gain_attn[:, None],
            gain_ffn[:, None],
            jnp.zeros((shard, gain_width - 2), bf16),
            w_output.T,
            jnp.zeros((shard, pad_width), bf16),
        ],
        axis=1,
    )
    dp_place = lax.axis_index("dp")
    tokens_near = jnp.stack([tokens, to_across(tokens)])
    tokens_far = to_beside(tokens_near)
    line = gather_line(first_shard)
    parts = gather_pairs(line)

    def send_piece(k, *pieces):
        cols = pieces[0].shape[1] // tensor_count
        sent = jnp.concatenate(
            [lax.dynamic_slice_in_dim(w, (place ^ k) * cols, cols, axis=1) for w in pieces]
        )
        return along(sent, "tensor", k) if k else sent

    def send_grads(grad):
        rows = grad.shape[0] // tensor_count
        parts = [None] * tensor_count
        for k in (2, 3, 1, 0):
            part = lax.dynamic_slice_in_dim(grad, (place ^ k) * rows, rows, axis=0)
            parts[k] = along(part, "tensor", k) if k else part
        return parts

    cotangent_near = jnp.stack([cotangent, to_across(after(cotangent, tokens_near))])
    pair_in = [
        send_piece(k, after(expert_gate, cotangent_near), expert_up) for k in range(tensor_count)
    ]

    expert_ids = routes.reshape(-1)
    ranking = slot_order.reshape(-1)
    same_expert = expert_ids[:, None] == expert_ids[None, :]
    earlier = ranking[None, :] < ranking[:, None]
    placed = jnp.sum((same_expert & earlier).astype(jnp.int32), axis=1)
    targets = jnp.where(placed < CAP, expert_ids * CAP + placed, -1)
    slot_ids = jnp.arange(slots, dtype=jnp.int32)
    targets_two = targets.reshape(local_rows, TOP)
    hits = [slot_ids[:, None] == targets_two[None, :, k] for k in range(TOP)]
    token_map = sum(hit.astype(bf16) for hit in hits)
    gate_map = sum(jnp.where(hits[k], gate_values[None, :, k], 0.0) for k in range(TOP))
    slot_gate = jnp.sum(gate_map, axis=1)

    groups = [[i * tensor_count + x * 2 + c for i in range(dp_count) for x in (0, 1)] for c in (0, 1)]

    def exchange(slot_rows):
        return lax.all_to_all(
            slot_rows.reshape(EXPERTS, CAP, width),
            ("dp", "tensor"),
            split_axis=0,
            concat_axis=0,
            tiled=True,
            axis_index_groups=groups,
        ).reshape(slots, width)

    def sum_cores(own, other):
        return (own + to_beside(other.astype(bf16)).astype(f32)).astype(bf16)

    slot_cotangent = dot(token_map, cotangent, nn) * slot_gate[:, None]
    grad_own = exchange(after(slot_cotangent.astype(bf16), parts))
    second_shard = jnp.concatenate([dense_gate, dense_up, dense_down.T], axis=1)
    second_line = gather_line(after(second_shard, line[2]))

    where = jnp.stack([place, dp_place, prefix_len[0]])
    (
        *saved,
        sum_near,
        sum_far,
    ) = attend_kernel(where, tokens_near, tokens_far, parts, length, columns)
    normed_all, weights, gains_both, *saved = saved
    gain_one, gain_two = gains_both[0], gains_both[1]
    inputs = tokens.astype(f32)
    sum_far = after(sum_far, pair_in, second_line)
    second_own = jnp.stack(after(second_line, sum_far))
    second_other = along(second_own, "dp", 1)
    near = sum_near + to_beside(sum_far).astype(f32)
    hidden = inputs + near[0] + to_across(near[1].astype(bf16)).astype(f32)
    normed_two = norm_rows(after(hidden, grad_own), gain_two).astype(bf16)

    dispatched = dot(token_map, normed_two, nn).astype(bf16)
    own_rows = exchange(dispatched)
    grad_own = after(grad_own, dispatched)
    grad_rows = (grad_own, to_beside(grad_own))
    expert_down_t = after(expert_down.T, hidden)
    down_in = [send_piece(k, expert_down_t) for k in range(tensor_count)]
    normed_near = jnp.stack([normed_two, to_across(after(normed_two, dispatched))])
    normed_far = to_beside(normed_near)
    cotangent_far = to_beside(cotangent_near)
    second_parts = [part for n in range(dp_count // 2) for part in (second_own[n], second_other[n])]
    back_near, back_far, out_near, out_far, second_grad = dense_kernel(
        where,
        (normed_near, normed_far),
        (cotangent_near, cotangent_far),
        second_parts,
    )
    own_rows, back_far, out_far = after((own_rows, back_far, out_far), second_grad, down_in)
    expert_rows = (own_rows, to_beside(own_rows))
    near = back_near + to_beside(back_far).astype(f32)
    dense_back = near[0] + to_across(near[1].astype(bf16)).astype(f32)
    second_mine, second_other = pair_halves(after(second_grad, own_rows))
    piece_down_t, back_own, back_other, acts, grads_gate, grads_up = expert_kernel(
        where, expert_rows, grad_rows, pair_in, down_in
    )
    back_rows = sum_cores(back_own, back_other)
    slots_back = exchange(back_rows)

    out_own, out_other, gate_grad, rest_grad = expert_grad_kernel(
        after(expert_rows, back_rows), grad_rows, acts, grads_gate, grads_up, piece_down_t
    )
    out_rows = sum_cores(out_own, out_other)
    gate_parts = send_grads(gate_grad)
    slots_back = after(slots_back, out_rows, dense_back, gate_parts)

    expert_back = dot(token_map, slots_back, tn)
    grad_normed_two = dense_back + expert_back
    grad_hidden_norm, grad_gain_two = norm_back(hidden, gain_two, grad_normed_two)
    grad_hidden = cotangent.astype(f32) + grad_hidden_norm

    grad_attn_own = grad_hidden.astype(bf16)
    grad_near = jnp.stack([grad_attn_own, to_across(grad_attn_own)])
    grad_far = to_beside(grad_near)
    slots_out = exchange(after(out_rows, grad_attn_own))
    second_line = send_line(after((second_mine, second_other), grad_attn_own))
    rest_parts = send_grads(after(rest_grad, grad_near))
    near = out_near + to_beside(after(out_far, grad_near)).astype(f32)
    dense_out = near[0] + to_across(near[1].astype(bf16)).astype(f32)
    first_grad, back_near, back_far = attend_back_kernel(
        where,
        tokens_near,
        tokens_far,
        grad_near,
        grad_far,
        [normed_all, weights, *saved],
        grad_gain_two[None],
        length,
        columns,
    )
    first_grad = after(first_grad, slots_out, second_line, rest_parts)
    second_total = sum(part.astype(f32) for part in after(second_line, first_grad))
    first_parts = lax.all_to_all(
        first_grad.reshape(dp_count, shard, -1), "dp", split_axis=0, concat_axis=0, tiled=True
    )
    first_total = jnp.sum(first_parts.astype(f32), axis=0)
    gains = first_total[:, 3 * columns : 3 * columns + 2].T
    gains = gains + to_beside(gains)
    gains = gains + to_across(gains)
    near = back_near + to_beside(back_far).astype(f32)
    grad_normed_one = near[0] + to_across(near[1].astype(bf16)).astype(f32)
    grad_input_norm, _ = norm_back(inputs, gain_one, grad_normed_one)
    grad_tokens = grad_hidden + grad_input_norm
    slots_out, gate_parts, rest_parts, dense_out = after(
        (slots_out, gate_parts, rest_parts, dense_out), first_grad
    )
    block_out = mix_kernel(hidden, dense_out, gate_map, slots_out)
    gate_total, up_total, down_total = join_kernel(where, gate_parts, rest_parts)
    return (
        block_out,
        grad_tokens,
        gains[0],
        first_total[:, :columns],
        first_total[:, columns : 2 * columns],
        first_total[:, 2 * columns : 3 * columns],
        first_total[:, 3 * columns + gain_width :][:, :columns].T,
        gains[1],
        second_total[:, :hidden_cols],
        second_total[:, hidden_cols : 2 * hidden_cols],
        second_total[:, 2 * hidden_cols :].T,
        gate_total,
        up_total,
        down_total.T,
    )


def gather_rows(rows_in):
    return lax.all_gather(rows_in, "tensor", axis=0, tiled=True)


def sum_rows(rows_in):
    return lax.psum_scatter(rows_in, "tensor", scatter_dimension=0, tiled=True)


def gather_attn_rows(rows_in):
    return lax.all_gather(rows_in, "tensor", axis=0, tiled=True)


def sum_attn_rows(rows_in):
    return lax.psum_scatter(rows_in, "tensor", scatter_dimension=0, tiled=True)


def general(
    tokens,
    cotangent,
    gain_attn,
    w_query,
    w_key,
    w_value,
    w_output,
    gain_ffn,
    dense_gate,
    dense_up,
    dense_down,
    expert_gate,
    expert_up,
    expert_down,
    routes,
    slot_order,
    gate_values,
    prefix_len,
):
    dp_count = lax.axis_size("dp")
    tensor_count = lax.axis_size("tensor")
    local_rows = tokens.shape[0]
    model_width = tokens.shape[1]
    length = local_rows * tensor_count
    splits = max(1, dp_count // EXPERTS)
    per_device = max(1, EXPERTS // dp_count)
    inputs = tokens.astype(jnp.float32)
    dense_all = (
        lax.all_gather(gain_attn, "dp", axis=0, tiled=True),
        lax.all_gather(w_query, "dp", axis=0, tiled=True),
        lax.all_gather(w_key, "dp", axis=0, tiled=True),
        lax.all_gather(w_value, "dp", axis=0, tiled=True),
        lax.all_gather(w_output, "dp", axis=1, tiled=True),
        lax.all_gather(gain_ffn, "dp", axis=0, tiled=True),
        lax.all_gather(dense_gate, "dp", axis=0, tiled=True),
        lax.all_gather(dense_up, "dp", axis=0, tiled=True),
        lax.all_gather(dense_down, "dp", axis=1, tiled=True),
    )
    (
        gain_one,
        query_full,
        key_full,
        value_full,
        output_full,
        gain_two,
        gate_full,
        up_full,
        down_full,
    ) = dense_all
    gain_one = gain_one.astype(jnp.float32)
    gain_two = gain_two.astype(jnp.float32)
    positions = jnp.arange(length, dtype=jnp.int32)
    prefix_value = prefix_len[0]
    normed_one = norm_rows(inputs, gain_one).astype(jnp.bfloat16)
    head_count = query_full.shape[1] // HEAD_DIM
    normed_all = gather_attn_rows(normed_one)
    queries = rotary(
        jnp.dot(normed_all, query_full, preferred_element_type=jnp.float32).reshape(
            length, head_count, HEAD_DIM
        ),
        positions,
        1.0,
    ).astype(jnp.bfloat16)
    keys_all = rotary(
        jnp.dot(normed_all, key_full, preferred_element_type=jnp.float32).reshape(
            length, head_count, HEAD_DIM
        ),
        positions,
        1.0,
    ).astype(jnp.bfloat16)
    values_all = (
        jnp.dot(normed_all, value_full, preferred_element_type=jnp.float32)
        .astype(jnp.bfloat16)
        .reshape(length, head_count, HEAD_DIM)
    )
    score_scale = 1.0 / math.sqrt(HEAD_DIM)
    block_rows = min(512, length)
    blocks = length // block_rows
    query_blocks = queries.reshape(blocks, block_rows, head_count, HEAD_DIM)
    position_blocks = positions.reshape(blocks, block_rows)

    def block_scores(block_query, block_pos):
        scores = (
            jnp.einsum("qhd,khd->hqk", block_query, keys_all, preferred_element_type=jnp.float32)
            * score_scale
        )
        visible = (positions[None, :] <= block_pos[:, None]) | (positions[None, :] < prefix_value)
        return jnp.where(visible[None], scores, -1e30)

    def attend(block_item):
        block_query, block_pos = block_item
        scores = block_scores(block_query, block_pos)
        row_top = jnp.max(scores, axis=-1, keepdims=True)
        exponent = jnp.exp(scores - row_top)
        row_total = jnp.sum(exponent, axis=-1, keepdims=True)
        softmaxed = exponent / row_total
        mixture = jnp.einsum(
            "hqk,khd->qhd",
            softmaxed.astype(jnp.bfloat16),
            values_all,
            preferred_element_type=jnp.float32,
        ).astype(jnp.bfloat16)
        return (mixture, (row_top + jnp.log(row_total))[..., 0])

    attended, log_totals = lax.map(attend, (query_blocks, position_blocks))
    attended = attended.reshape(length, head_count * HEAD_DIM)
    hidden = inputs + sum_attn_rows(
        jnp.dot(attended, output_full, preferred_element_type=jnp.float32)
    )
    normed_two = norm_rows(hidden, gain_two).astype(jnp.bfloat16)
    normed_two_all = gather_rows(normed_two)
    gate_pre = jnp.dot(normed_two_all, gate_full, preferred_element_type=jnp.float32)
    up_pre = jnp.dot(normed_two_all, up_full, preferred_element_type=jnp.float32)
    activated = (jax.nn.silu(gate_pre) * up_pre).astype(jnp.bfloat16)
    dense_out = sum_rows(jnp.dot(activated, down_full, preferred_element_type=jnp.float32))
    expert_ids = routes.reshape(-1)
    ranking = slot_order.reshape(-1)
    same_expert = expert_ids[:, None] == expert_ids[None, :]
    earlier = ranking[None, :] < ranking[:, None]
    placed = jnp.sum((same_expert & earlier).astype(jnp.int32), axis=1)
    usable = placed < CAP
    targets = jnp.where(usable, expert_ids * CAP + placed, -1)
    slot_ids = jnp.arange(EXPERTS * CAP, dtype=jnp.int32)
    pair_map = (slot_ids[:, None] == targets[None, :]).astype(jnp.float32)
    token_map = jnp.sum(pair_map.reshape(EXPERTS * CAP, local_rows, TOP), axis=2).astype(
        jnp.bfloat16
    )
    dispatched = jnp.dot(token_map, normed_two, preferred_element_type=jnp.float32).astype(
        jnp.bfloat16
    )
    outgoing = jnp.broadcast_to(
        dispatched.reshape(EXPERTS, 1, CAP, model_width), (EXPERTS, splits, CAP, model_width)
    ).reshape(dp_count, per_device, CAP, model_width)
    expert_all = (
        lax.all_gather(expert_gate, "tensor", axis=0, tiled=True),
        lax.all_gather(expert_up, "tensor", axis=0, tiled=True),
        lax.all_gather(expert_down, "tensor", axis=1, tiled=True),
    )
    piece_width = expert_all[0].shape[1] // per_device
    gate_pieces = expert_all[0].reshape(model_width, per_device, piece_width)
    up_pieces = expert_all[1].reshape(model_width, per_device, piece_width)
    down_pieces = expert_all[2].reshape(per_device, piece_width, model_width)
    received = lax.all_to_all(outgoing, "dp", split_axis=0, concat_axis=0, tiled=True)
    gate_local = jnp.einsum(
        "sjnd,djp->sjnp", received, gate_pieces, preferred_element_type=jnp.float32
    )
    up_local = jnp.einsum("sjnd,djp->sjnp", received, up_pieces, preferred_element_type=jnp.float32)
    active_local = (jax.nn.silu(gate_local) * up_local).astype(jnp.bfloat16)
    result_local = jnp.einsum(
        "sjnp,jpd->sjnd", active_local, down_pieces, preferred_element_type=jnp.float32
    ).astype(jnp.bfloat16)
    returned = lax.all_to_all(result_local, "dp", split_axis=0, concat_axis=0, tiled=True)
    returned, kept_in, gate_local, up_local = (returned, received, gate_local, up_local)
    expert_sums = jnp.sum(
        returned.reshape(EXPERTS, splits, CAP, model_width).astype(jnp.float32), axis=1
    ).reshape(EXPERTS * CAP, model_width)
    pick_index = jnp.where(usable, targets, 0)
    pair_weight = jnp.where(usable, gate_values.reshape(-1), 0.0)
    picked = jnp.take(expert_sums, pick_index, axis=0) * pair_weight[:, None]
    expert_mix = jnp.sum(picked.reshape(local_rows, TOP, model_width), axis=1)
    block_out = (hidden + dense_out + expert_mix).astype(jnp.bfloat16)
    dense_back = (
        lax.all_gather(gain_attn, "dp", axis=0, tiled=True),
        lax.all_gather(w_query, "dp", axis=0, tiled=True),
        lax.all_gather(w_key, "dp", axis=0, tiled=True),
        lax.all_gather(w_value, "dp", axis=0, tiled=True),
        lax.all_gather(w_output, "dp", axis=1, tiled=True),
        lax.all_gather(gain_ffn, "dp", axis=0, tiled=True),
        lax.all_gather(dense_gate, "dp", axis=0, tiled=True),
        lax.all_gather(dense_up, "dp", axis=0, tiled=True),
        lax.all_gather(dense_down, "dp", axis=1, tiled=True),
    )
    (
        gain_one,
        query_full,
        key_full,
        value_full,
        output_full,
        gain_two,
        gate_full,
        up_full,
        down_full,
    ) = dense_back
    gain_one = gain_one.astype(jnp.float32)
    gain_two = gain_two.astype(jnp.float32)
    grad_out = cotangent.astype(jnp.float32)
    cotangent_all = gather_rows(cotangent)
    grad_down = jnp.einsum(
        "lf,ld->fd", activated, cotangent_all, preferred_element_type=jnp.float32
    )
    grad_act = jnp.einsum("ld,fd->lf", cotangent_all, down_full, preferred_element_type=jnp.float32)
    grad_gate_pre, grad_up_pre = swiglu_back(grad_act, gate_pre, up_pre)
    grad_gate = jnp.einsum(
        "ld,lf->df", normed_two_all, grad_gate_pre, preferred_element_type=jnp.float32
    )
    grad_up = jnp.einsum(
        "ld,lf->df", normed_two_all, grad_up_pre, preferred_element_type=jnp.float32
    )
    dense_back_in = jnp.einsum(
        "lf,df->ld", grad_gate_pre, gate_full, preferred_element_type=jnp.float32
    ) + jnp.einsum("lf,df->ld", grad_up_pre, up_full, preferred_element_type=jnp.float32)
    slot_gate = jnp.dot(pair_map, gate_values.reshape(-1), precision=lax.Precision.HIGHEST)
    slot_cotangent = jnp.dot(token_map, cotangent, preferred_element_type=jnp.float32)
    grad_slots = (slot_cotangent * slot_gate[:, None]).astype(jnp.bfloat16)
    grad_outgoing = jnp.broadcast_to(
        grad_slots.reshape(EXPERTS, 1, CAP, model_width), (EXPERTS, splits, CAP, model_width)
    ).reshape(dp_count, per_device, CAP, model_width)
    grad_received = lax.all_to_all(grad_outgoing, "dp", split_axis=0, concat_axis=0, tiled=True)
    active_local = (jax.nn.silu(gate_local) * up_local).astype(jnp.bfloat16)
    grad_down_expert = jnp.einsum(
        "sjnp,sjnd->jpd", active_local, grad_received, preferred_element_type=jnp.float32
    ).reshape(per_device * piece_width, model_width)
    grad_act_expert = jnp.einsum(
        "sjnd,jpd->sjnp", grad_received, down_pieces, preferred_element_type=jnp.float32
    )
    grad_gate_local, grad_up_local = swiglu_back(grad_act_expert, gate_local, up_local)
    grad_gate_expert = jnp.einsum(
        "sjnd,sjnp->djp", kept_in, grad_gate_local, preferred_element_type=jnp.float32
    ).reshape(model_width, per_device * piece_width)
    grad_up_expert = jnp.einsum(
        "sjnd,sjnp->djp", kept_in, grad_up_local, preferred_element_type=jnp.float32
    ).reshape(model_width, per_device * piece_width)
    grad_in_expert = (
        jnp.einsum(
            "sjnp,djp->sjnd", grad_gate_local, gate_pieces, preferred_element_type=jnp.float32
        )
        + jnp.einsum("sjnp,djp->sjnd", grad_up_local, up_pieces, preferred_element_type=jnp.float32)
    ).astype(jnp.bfloat16)
    grad_back = lax.all_to_all(grad_in_expert, "dp", split_axis=0, concat_axis=0, tiled=True)
    grad_slots_in = jnp.sum(
        grad_back.reshape(EXPERTS, splits, CAP, model_width).astype(jnp.float32), axis=1
    ).reshape(EXPERTS * CAP, model_width)
    grad_pairs = jnp.where(usable[:, None], jnp.take(grad_slots_in, pick_index, axis=0), 0.0)
    expert_back = jnp.sum(grad_pairs.reshape(local_rows, TOP, model_width), axis=1)
    grad_normed_two = sum_rows(dense_back_in) + expert_back
    grad_hidden_norm, grad_gain_two_part = norm_back(hidden, gain_two, grad_normed_two)
    grad_hidden = grad_out + grad_hidden_norm
    query_use, key_use, value_use, output_use = (query_full, key_full, value_full, output_full)
    grad_attn_in = gather_attn_rows(grad_hidden.astype(jnp.bfloat16))
    grad_output_w = jnp.einsum(
        "lc,ld->cd", attended, grad_attn_in, preferred_element_type=jnp.float32
    )
    grad_attended = (
        jnp.einsum("ld,cd->lc", grad_attn_in, output_use, preferred_element_type=jnp.float32)
        .astype(jnp.bfloat16)
        .reshape(blocks, block_rows, head_count, HEAD_DIM)
    )

    def attend_back(running, block_item):
        grad_keys, grad_values = running
        block_query, block_pos, block_grad, block_total = block_item
        scores = block_scores(block_query, block_pos)
        softmaxed = jnp.exp(scores - block_total[..., None])
        grad_soft = jnp.einsum(
            "qhd,khd->hqk", block_grad, values_all, preferred_element_type=jnp.float32
        )
        inner_sum = jnp.sum(softmaxed * grad_soft, axis=-1, keepdims=True)
        grad_scores = (softmaxed * (grad_soft - inner_sum)).astype(jnp.bfloat16)
        grad_block = (
            jnp.einsum("hqk,khd->qhd", grad_scores, keys_all, preferred_element_type=jnp.float32)
            * score_scale
        )
        grad_keys = (
            grad_keys
            + jnp.einsum(
                "hqk,qhd->khd", grad_scores, block_query, preferred_element_type=jnp.float32
            )
            * score_scale
        )
        grad_values = grad_values + jnp.einsum(
            "hqk,qhd->khd",
            softmaxed.astype(jnp.bfloat16),
            block_grad,
            preferred_element_type=jnp.float32,
        )
        return ((grad_keys, grad_values), grad_block)

    zero_start = (
        jnp.zeros((length, head_count, HEAD_DIM), jnp.float32),
        jnp.zeros((length, head_count, HEAD_DIM), jnp.float32),
    )
    (grad_keys, grad_values), grad_queries = lax.scan(
        attend_back, zero_start, (query_blocks, position_blocks, grad_attended, log_totals)
    )
    grad_queries = (
        rotary(grad_queries.reshape(length, head_count, HEAD_DIM), positions, -1.0)
        .astype(jnp.bfloat16)
        .reshape(length, head_count * HEAD_DIM)
    )
    grad_keys = (
        rotary(grad_keys, positions, -1.0)
        .astype(jnp.bfloat16)
        .reshape(length, head_count * HEAD_DIM)
    )
    grad_values = grad_values.astype(jnp.bfloat16).reshape(length, head_count * HEAD_DIM)
    grad_query_w = jnp.einsum(
        "ld,lc->dc", normed_all, grad_queries, preferred_element_type=jnp.float32
    )
    grad_key_w = jnp.einsum("ld,lc->dc", normed_all, grad_keys, preferred_element_type=jnp.float32)
    grad_value_w = jnp.einsum(
        "ld,lc->dc", normed_all, grad_values, preferred_element_type=jnp.float32
    )
    normed_back_part = (
        jnp.einsum("lc,dc->ld", grad_queries, query_use, preferred_element_type=jnp.float32)
        + jnp.einsum("lc,dc->ld", grad_keys, key_use, preferred_element_type=jnp.float32)
        + jnp.einsum("lc,dc->ld", grad_values, value_use, preferred_element_type=jnp.float32)
    )
    grad_normed_one = sum_attn_rows(normed_back_part)
    grad_input_norm, grad_gain_one_part = norm_back(inputs, gain_one, grad_normed_one)
    grad_tokens = grad_hidden + grad_input_norm
    dense_grads = (
        lax.psum_scatter(grad_gain_one_part, "dp", scatter_dimension=0, tiled=True),
        lax.psum_scatter(grad_query_w, "dp", scatter_dimension=0, tiled=True),
        lax.psum_scatter(grad_key_w, "dp", scatter_dimension=0, tiled=True),
        lax.psum_scatter(grad_value_w, "dp", scatter_dimension=0, tiled=True),
        lax.psum_scatter(grad_output_w, "dp", scatter_dimension=1, tiled=True),
        lax.psum_scatter(grad_gain_two_part, "dp", scatter_dimension=0, tiled=True),
        lax.psum_scatter(grad_gate, "dp", scatter_dimension=0, tiled=True),
        lax.psum_scatter(grad_up, "dp", scatter_dimension=0, tiled=True),
        lax.psum_scatter(grad_down, "dp", scatter_dimension=1, tiled=True),
    )
    gain_totals = lax.psum((dense_grads[0], dense_grads[5]), "tensor")
    expert_grads = (
        lax.psum_scatter(
            grad_gate_expert.astype(jnp.bfloat16), "tensor", scatter_dimension=0, tiled=True
        ).astype(jnp.float32),
        lax.psum_scatter(
            grad_up_expert.astype(jnp.bfloat16), "tensor", scatter_dimension=0, tiled=True
        ).astype(jnp.float32),
        lax.psum_scatter(
            grad_down_expert.astype(jnp.bfloat16), "tensor", scatter_dimension=1, tiled=True
        ).astype(jnp.float32),
    )
    return (
        block_out,
        grad_tokens,
        gain_totals[0],
        dense_grads[1],
        dense_grads[2],
        dense_grads[3],
        dense_grads[4],
        gain_totals[1],
        dense_grads[6],
        dense_grads[7],
        dense_grads[8],
        expert_grads[0],
        expert_grads[1],
        expert_grads[2],
    )


def solution(mesh):
    sizes = mesh.shape
    in_pairs = sizes["tensor"] == 4 and sizes["dp"] * 2 == EXPERTS
    local = paired if in_pairs else general
    return jax.shard_map(
        local,
        mesh=mesh,
        in_specs=(
            P(("dp", "tensor"), None),
            P(("dp", "tensor"), None),
            P("dp"),
            P("dp", "tensor"),
            P("dp", "tensor"),
            P("dp", "tensor"),
            P("tensor", "dp"),
            P("dp"),
            P("dp", "tensor"),
            P("dp", "tensor"),
            P("tensor", "dp"),
            P("tensor", "dp"),
            P("tensor", "dp"),
            P("dp", "tensor"),
            P(("dp", "tensor"), None),
            P(("dp", "tensor"), None),
            P(("dp", "tensor"), None),
            P("dp"),
        ),
        out_specs=(
            P(("dp", "tensor"), None),
            P(("dp", "tensor"), None),
            P("dp"),
            P("dp", "tensor"),
            P("dp", "tensor"),
            P("dp", "tensor"),
            P("tensor", "dp"),
            P("dp"),
            P("dp", "tensor"),
            P("dp", "tensor"),
            P("tensor", "dp"),
            P("tensor", "dp"),
            P("tensor", "dp"),
            P("dp", "tensor"),
        ),
        check_vma=False,
    )
```

```python
import math

import jax
import jax.numpy as jnp
import numpy as np
from jax import lax
from jax.experimental import pallas as pl
from jax.experimental.pallas import tpu as pltpu
from jax.sharding import PartitionSpec as P

HEAD_DIM = 64
EXPERTS = 16
TOP = 2
CAP = 40


epsilon = 1e-06


def norm_rows(rows_in, gain_row):
    return (
        rows_in
        * lax.rsqrt(jnp.mean(rows_in * rows_in, axis=-1, keepdims=True) + epsilon)
        * gain_row
    )


def norm_back(rows_in, gain_row, grad_out):
    inverse = lax.rsqrt(jnp.mean(rows_in * rows_in, axis=-1, keepdims=True) + epsilon)
    scaled = grad_out * gain_row
    grad_rows = inverse * scaled - rows_in * inverse**3 * jnp.mean(
        scaled * rows_in, axis=-1, keepdims=True
    )
    grad_gain = jnp.sum(grad_out * rows_in * inverse, axis=0)
    return (grad_rows, grad_gain)


def rotary(values, positions, direction):
    half_width = values.shape[-1] // 2
    frequency = jnp.power(10000.0, -jnp.arange(half_width).astype(jnp.float32) / half_width)
    angles = positions[:, None].astype(jnp.float32) * frequency[None, :]
    cosine = jnp.cos(angles)[:, None, :]
    sine_part = direction * jnp.sin(angles)[:, None, :]
    first_half = values[..., :half_width]
    second_half = values[..., half_width:]
    return jnp.concatenate(
        [
            first_half * cosine - second_half * sine_part,
            second_half * cosine + first_half * sine_part,
        ],
        axis=-1,
    )


def swiglu_back(grad_act, gate_pre, up_pre):
    sigmoid = jax.nn.sigmoid(gate_pre)
    silu_value = gate_pre * sigmoid
    grad_gate = grad_act * up_pre * sigmoid * (1.0 + gate_pre * (1.0 - sigmoid))
    grad_up = grad_act * silu_value
    return (grad_gate.astype(jnp.bfloat16), grad_up.astype(jnp.bfloat16))


def to_across(values):
    return lax.ppermute(values, "tensor", [(i, i ^ 2) for i in range(4)])


def to_beside(values):
    return lax.ppermute(values, "tensor", [(i, i ^ 1) for i in range(4)])


def gather_blocks(rows_in):
    near = jnp.stack([rows_in, to_across(rows_in)])
    return jnp.concatenate([near, to_beside(near)]).reshape(-1, rows_in.shape[-1])


def sum_across(own, near, far, *before):
    beside = to_beside(far)
    beside = [part.astype(jnp.float32) for part in after((beside[0], beside[1]))]
    sent = (near + beside[1]).astype(jnp.bfloat16)
    return own + beside[0] + to_across(after(sent, *before) if before else sent).astype(jnp.float32)


def after(value, *before):
    if not before:
        return lax.optimization_barrier(value)
    return lax.optimization_barrier((value,) + before)[0]


def sum_blocks(partial):
    blocks = partial.reshape(4, -1, partial.shape[-1])
    near = blocks[:2] + to_beside(blocks[2:].astype(jnp.bfloat16)).astype(jnp.float32)
    return near[0] + to_across(near[1].astype(jnp.bfloat16)).astype(jnp.float32)


def along(values, axis, k):
    return lax.ppermute(values, axis, [(i, i ^ k) for i in range(lax.axis_size(axis))])


def gather_line(rows_in):
    return [along(rows_in, "dp", k) if k else rows_in for k in range(0, lax.axis_size("dp"), 2)]


def gather_pairs(line):
    return [part for own in line for part in (own, along(own, "dp", 1))]


def dot(left, right, dims):
    return lax.dot_general(left, right, (dims, ((), ())), preferred_element_type=jnp.float32)


NN, NT, TN = ((1,), (0,)), ((1,), (1,)), ((0,), (0,))
ORDER = (0, 2, 1, 3)
VMEM = pl.BlockSpec(memory_space=pltpu.VMEM)
SMEM = pl.BlockSpec(memory_space=pltpu.SMEM)
HBM = pl.BlockSpec(memory_space=pltpu.HBM)
NO_COST = pl.CostEstimate(flops=0, bytes_accessed=0, transcendentals=0)


def angle_tables(length):
    half = HEAD_DIM // 2
    lane = np.arange(2 * HEAD_DIM)
    frequency = np.power(10000.0, -(lane % half).astype(np.float64) / half)
    angles = np.arange(length)[:, None] * frequency[None, :]
    sign = np.where(lane % HEAD_DIM < half, -1.0, 1.0)
    return np.cos(angles).astype(np.float32), (np.sin(angles) * sign).astype(np.float32)


def turn(values, cosine, sine):
    width = values.shape[1]
    half = HEAD_DIM // 2
    lane = lax.broadcasted_iota(jnp.int32, values.shape, 1)
    swapped = jnp.where(
        lane % HEAD_DIM < half,
        pltpu.roll(values, width - half, 1),
        pltpu.roll(values, half, 1),
    )
    repeats = width // cosine.shape[1]
    return values * jnp.concatenate([cosine] * repeats, axis=1) + swapped * jnp.concatenate(
        [sine] * repeats, axis=1
    )


def block_at(place, i):
    return place ^ ((i >> 1) | ((i & 1) << 1))


def pack_views(own, near, far, n):
    return own, near.at[n], far.at[0, n], far.at[1, n]


def seen(place, prefix, i, j, rows):
    query_block, key_block = block_at(place, i), block_at(place, j)
    return (key_block <= query_block) | (key_block * rows < prefix)


def mask_of(place, prefix, i, j, rows):
    key = block_at(place, j) * rows + lax.broadcasted_iota(jnp.int32, (rows, rows), 0)
    query = block_at(place, i) * rows + lax.broadcasted_iota(jnp.int32, (rows, rows), 1)
    return key <= jnp.maximum(query, prefix - 1)


def attend_kernel(where, blocks_in, parts, length, columns):
    rows, width = blocks_in[0].shape
    shard, lanes = parts[0].shape
    blocks = length // rows
    heads = columns // HEAD_DIM
    count = len(parts)
    gain_at = 3 * columns
    output_at = 3 * columns + 64
    bf16, f32 = jnp.bfloat16, jnp.float32
    cosine, sine = angle_tables(length)

    def body(*refs):
        spot, token_refs = refs[0], pack_views(*refs[1:4], 0)
        part_refs = refs[4 : 4 + count]
        cos_ref, sin_ref = refs[4 + count : 6 + count]
        (
            normed_ref,
            weight_ref,
            gain_ref,
            query_ref,
            query_t_ref,
            key_ref,
            value_ref,
            mixed_ref,
            mixed_t_ref,
            log_ref,
            sum_own_ref,
            sum_near_ref,
            sum_far_ref,
        ) = refs[6 + count : 19 + count]
        value_t_ref, score_ref, top_ref, total_ref, mix_ref, *keep, sems = refs[19 + count :]
        outward = [
            pltpu.make_async_copy(source, target, sems.at[n])
            for n, (source, target) in enumerate(
                zip(
                    keep,
                    (
                        normed_ref,
                        weight_ref,
                        query_ref,
                        query_t_ref,
                        key_ref,
                        value_ref,
                        mixed_ref,
                        mixed_t_ref,
                    ),
                )
            )
        ]
        (
            normed_ref,
            weight_ref,
            query_ref,
            query_t_ref,
            key_ref,
            value_ref,
            mixed_ref,
            mixed_t_ref,
        ) = keep
        place, dp_place, prefix = spot[0], spot[1], spot[2]
        for k in range(count):
            start = pl.multiple_of((dp_place ^ k) * shard, 16)
            weight_ref[pl.ds(start, shard), :] = part_refs[k][...]
        gain_tile = weight_ref[:, gain_at // 128 * 128 : gain_at // 128 * 128 + 128].astype(f32)
        gain_ref[...] = gain_tile.T[gain_at % 128 : gain_at % 128 + 8, :]
        gain = gain_ref[0:1, :]
        for i in range(blocks):
            tokens = token_refs[i][...].astype(f32)
            inverse = lax.rsqrt(jnp.mean(tokens * tokens, axis=-1, keepdims=True) + epsilon)
            normed = (tokens * inverse * gain).astype(bf16)
            span = pl.ds(i * rows, rows)
            normed_ref[span, :] = normed
            product = dot(normed, weight_ref[:, : 3 * columns], NN)
            spot_rows = pl.ds(pl.multiple_of(block_at(place, i) * rows, 8), rows)
            turned = turn(product[:, : 2 * columns], cos_ref[spot_rows, :], sin_ref[spot_rows, :])
            query = turned[:, :columns] * (1.0 / math.sqrt(HEAD_DIM))
            key = turned[:, columns:]
            value = product[:, 2 * columns :]
            query_t = query.T
            value_t = value.T
            for h in range(heads):
                cut = slice(h * HEAD_DIM, (h + 1) * HEAD_DIM)
                query_ref[h, span, :] = query[:, cut].astype(bf16)
                query_t_ref[h, :, span] = query_t[cut, :].astype(bf16)
                key_ref[h, span, :] = key[:, cut].astype(bf16)
                value_ref[h, span, :] = value[:, cut].astype(bf16)
                value_t_ref[h, :, span] = value_t[cut, :].astype(bf16)

        for copy in outward[:6]:
            copy.start()

        def query_block(i, carry):
            here = pl.ds(pl.multiple_of(i * rows, 128), rows)
            top_ref[...] = jnp.full(top_ref.shape, -1e30, f32)
            total_ref[...] = jnp.zeros(total_ref.shape, f32)
            mix_ref[...] = jnp.zeros(mix_ref.shape, f32)

            def scores(j, carry):
                @pl.when(seen(place, prefix, i, j, rows))
                def _():
                    there = pl.ds(pl.multiple_of(j * rows, 128), rows)
                    visible = mask_of(place, prefix, i, j, rows)
                    for h in range(heads):
                        score = dot(key_ref[h, there, :], query_t_ref[h, :, here], NN)
                        score = jnp.where(visible, score, -1e30)
                        score_ref[h, there, :] = score
                        top_ref[h : h + 1, :] = jnp.maximum(
                            top_ref[h : h + 1, :], jnp.max(score, axis=0, keepdims=True)
                        )

                return carry

            def mixing(j, carry):
                @pl.when(seen(place, prefix, i, j, rows))
                def _():
                    there = pl.ds(pl.multiple_of(j * rows, 128), rows)
                    for h in range(heads):
                        power = jnp.exp(score_ref[h, there, :] - top_ref[h : h + 1, :])
                        total_ref[h : h + 1, :] += jnp.sum(power, axis=0, keepdims=True)
                        mix_ref[h] += dot(value_t_ref[h, :, there], power.astype(bf16), NN)

                return carry

            lax.fori_loop(0, blocks, scores, 0)
            lax.fori_loop(0, blocks, mixing, 0)
            log_ref[:, here] = top_ref[...] + jnp.log(jnp.maximum(total_ref[...], 1e-30))
            mixed_t = jnp.concatenate(
                [mix_ref[h] * (1.0 / total_ref[h : h + 1, :]) for h in range(heads)], axis=0
            )
            for h in range(heads):
                mixed_t_ref[h, :, here] = mixed_t[h * HEAD_DIM : (h + 1) * HEAD_DIM, :].astype(bf16)
            mixed = mixed_t.T.astype(bf16)
            mixed_ref[here, :] = mixed
            partial = dot(mixed, weight_ref[:, output_at : output_at + columns], NT)

            @pl.when(i == 0)
            def _():
                sum_own_ref[...] = partial

            @pl.when(i == 1)
            def _():
                sum_near_ref[...] = partial

            @pl.when(i >= 2)
            def _():
                sum_far_ref[i - 2] = partial.astype(bf16)

            return carry

        lax.fori_loop(0, blocks, query_block, 0)
        for copy in outward[6:]:
            copy.start()
        for copy in outward:
            copy.wait()

    per_head = (heads, length, HEAD_DIM)
    per_head_t = (heads, HEAD_DIM, length)
    out_shape = [
        jax.ShapeDtypeStruct(shape, kind)
        for shape, kind in (
            ((length, width), bf16),
            ((count * shard, lanes), bf16),
            ((8, width), f32),
            (per_head, bf16),
            (per_head_t, bf16),
            (per_head, bf16),
            (per_head, bf16),
            ((length, columns), bf16),
            (per_head_t, bf16),
            ((8, length), f32),
            ((rows, width), f32),
            ((rows, width), f32),
            ((2, rows, width), bf16),
        )
    ]
    return pl.pallas_call(
        body,
        out_shape=out_shape,
        in_specs=[SMEM] + [VMEM] * (5 + count),
        out_specs=[HBM] * 2 + [VMEM] + [HBM] * 6 + [VMEM] * 4,
        scratch_shapes=[
            pltpu.VMEM(per_head_t, bf16),
            pltpu.VMEM((heads, length, rows), f32),
            pltpu.VMEM((8, rows), f32),
            pltpu.VMEM((8, rows), f32),
            pltpu.VMEM((heads, HEAD_DIM, rows), f32),
        ]
        + [pltpu.VMEM(out_shape[n].shape, bf16) for n in (0, 1, 3, 4, 5, 6, 7, 8)]
        + [pltpu.SemaphoreType.DMA((8,))],
        compiler_params=pltpu.CompilerParams(vmem_limit_bytes=60 * 2**20),
        cost_estimate=NO_COST,
    )(where, *blocks_in, *parts, cosine, sine)


def attend_back_kernel(
    where, blocks_in, grads_in, saved, gain_two, length, columns
):
    normed, weight, query, query_t, key, value, mixed, mixed_t, log_total = saved
    rows, width = blocks_in[0].shape
    lanes = weight.shape[1]
    blocks = length // rows
    heads = columns // HEAD_DIM
    output_at = 3 * columns + 64
    bf16, f32 = jnp.bfloat16, jnp.float32
    cosine, sine = angle_tables(length)

    def body(*refs):
        (
            spot,
            own_ref,
            near_ref,
            far_ref,
            grad_own_ref,
            grad_near_ref,
            grad_far_ref,
            normed_ref,
            weight_ref,
            query_ref,
            query_t_ref,
            key_ref,
            value_ref,
            mixed_ref,
            mixed_t_ref,
            log_ref,
            gain_two_ref,
            cos_ref,
            sin_ref,
            first_ref,
            back_own_ref,
            back_near_ref,
            back_far_ref,
            grad_in,
            grad_mix,
            grad_mix_t,
            inner,
            key_t,
            grad_query_t,
            grad_key,
            grad_value,
            grad_product,
            *keep,
            sems,
        ) = refs
        place, prefix = spot[0], spot[2]
        inward = [
            pltpu.make_async_copy(source, target, sems.at[n])
            for n, (source, target) in enumerate(
                zip(
                    (
                        weight_ref,
                        mixed_t_ref,
                        key_ref,
                        query_t_ref,
                        query_ref,
                        value_ref,
                        own_ref,
                        near_ref.at[0],
                        far_ref.at[0, 0],
                        far_ref.at[1, 0],
                        normed_ref,
                        mixed_ref,
                        cos_ref,
                        sin_ref,
                    ),
                    keep,
                )
            )
        ]
        for copy in inward:
            copy.start()
        (
            weight_ref,
            mixed_t_ref,
            key_ref,
            query_t_ref,
            query_ref,
            value_ref,
            *token_refs,
            normed_ref,
            mixed_ref,
            cos_ref,
            sin_ref,
        ) = keep
        grad_refs = (grad_own_ref, grad_near_ref, grad_far_ref.at[0], grad_far_ref.at[1])
        grad_key[...] = jnp.zeros(grad_key.shape, f32)
        grad_value[...] = jnp.zeros(grad_value.shape, f32)
        grad_query_t[...] = jnp.zeros(grad_query_t.shape, f32)
        for copy in inward[:3]:
            copy.wait()
        for h in range(heads):
            key_t[h] = key_ref[h].astype(f32).T.astype(bf16)
        for i in range(blocks):
            span = pl.ds(i * rows, rows)
            grad = grad_refs[i][...]
            grad_in[span, :] = grad
            mix = dot(grad, weight_ref[:, output_at : output_at + columns], NN)
            mix_t = mix.T
            for h in range(heads):
                cut = slice(h * HEAD_DIM, (h + 1) * HEAD_DIM)
                low = mix_t[cut, :].astype(bf16)
                grad_mix[h, span, :] = mix[:, cut].astype(bf16)
                grad_mix_t[h, :, span] = low
                inner[h : h + 1, span] = jnp.sum(
                    low.astype(f32) * mixed_t_ref[h, :, span].astype(f32), axis=0, keepdims=True
                )

        for copy in inward[3:6]:
            copy.wait()

        def pair(step, carry):
            i, j = step // blocks, step % blocks

            @pl.when(seen(place, prefix, i, j, rows))
            def _():
                here = pl.ds(pl.multiple_of(i * rows, 128), rows)
                there = pl.ds(pl.multiple_of(j * rows, 128), rows)
                visible = mask_of(place, prefix, i, j, rows)
                for h in range(heads):
                    score = dot(key_ref[h, there, :], query_t_ref[h, :, here], NN)
                    weigh = jnp.where(visible, jnp.exp(score - log_ref[h : h + 1, here]), 0.0)
                    soft = dot(value_ref[h, there, :], grad_mix_t[h, :, here], NN)
                    low = (weigh * (soft - inner[h : h + 1, here])).astype(bf16)
                    grad_value[h, there, :] += dot(weigh.astype(bf16), grad_mix[h, here, :], NN)
                    grad_key[h, there, :] += dot(low, query_ref[h, here, :], NN)
                    grad_query_t[h, :, here] += dot(key_t[h, :, there], low, NN)

            return carry

        lax.fori_loop(0, blocks * blocks, pair, 0)
        for copy in inward[6:]:
            copy.wait()
        gain = jnp.zeros((1, width), f32)
        for i in range(blocks):
            span = pl.ds(i * rows, rows)
            spot_rows = pl.ds(pl.multiple_of(block_at(place, i) * rows, 8), rows)
            turned = jnp.concatenate(
                [grad_query_t[h, :, span].T * (1.0 / math.sqrt(HEAD_DIM)) for h in range(heads)]
                + [grad_key[h, span, :] for h in range(heads)],
                axis=1,
            )
            turned = turn(turned, cos_ref[spot_rows, :], -sin_ref[spot_rows, :])
            grads = jnp.concatenate(
                [turned] + [grad_value[h, span, :] for h in range(heads)], axis=1
            ).astype(bf16)
            grad_product[span, :] = grads
            back = dot(grads, weight_ref[:, : 3 * columns], NT)
            tokens = token_refs[i][...].astype(f32)
            inverse = lax.rsqrt(jnp.mean(tokens * tokens, axis=-1, keepdims=True) + epsilon)
            gain += jnp.sum(back * tokens * inverse, axis=0, keepdims=True)
            if i < 2:
                (back_own_ref, back_near_ref)[i][...] = back
            else:
                back_far_ref[i - 2] = back.astype(bf16)
        gains = jnp.concatenate([gain, gain_two_ref[...], jnp.zeros((62, width), f32)], axis=0)
        first_ref[:, 3 * columns : output_at] = gains.T.astype(bf16)
        first_ref[:, : 3 * columns] = dot(normed_ref[...], grad_product[...], TN).astype(bf16)
        first_ref[:, output_at : output_at + columns] = dot(
            grad_in[...], mixed_ref[...], TN
        ).astype(bf16)
        if output_at + columns < lanes:
            first_ref[:, output_at + columns :] = jnp.zeros(
                (width, lanes - output_at - columns), bf16
            )

    per_head = (heads, length, HEAD_DIM)
    per_head_t = (heads, HEAD_DIM, length)
    out_shape = [
        jax.ShapeDtypeStruct(shape, kind)
        for shape, kind in (
            ((width, lanes), bf16),
            ((rows, width), f32),
            ((rows, width), f32),
            ((2, rows, width), bf16),
        )
    ]
    return pl.pallas_call(
        body,
        out_shape=out_shape,
        in_specs=[SMEM] + [HBM] * 3 + [VMEM] * 3 + [HBM] * 8 + [VMEM] * 2 + [HBM] * 2,
        out_specs=[VMEM] * len(out_shape),
        scratch_shapes=[
            pltpu.VMEM((length, width), bf16),
            pltpu.VMEM(per_head, bf16),
            pltpu.VMEM(per_head_t, bf16),
            pltpu.VMEM((8, length), f32),
            pltpu.VMEM(per_head_t, bf16),
            pltpu.VMEM(per_head_t, f32),
            pltpu.VMEM(per_head, f32),
            pltpu.VMEM(per_head, f32),
            pltpu.VMEM((length, 3 * columns), bf16),
        ]
        + [
            pltpu.VMEM(array.shape, array.dtype)
            for array in (
                weight,
                mixed_t,
                key,
                query_t,
                query,
                value,
                *[blocks_in[0]] * 4,
                normed,
                mixed,
                cosine,
                sine,
            )
        ]
        + [pltpu.SemaphoreType.DMA((14,))],
        compiler_params=pltpu.CompilerParams(vmem_limit_bytes=60 * 2**20),
        cost_estimate=NO_COST,
    )(where, *blocks_in, *grads_in, *saved, gain_two, cosine, sine)


def gated(gate_pre, up_pre):
    sigmoid = 1.0 / (1.0 + jnp.exp(-gate_pre))
    return gate_pre * sigmoid * up_pre


def gated_back(grad, gate_pre, up_pre):
    sigmoid = 1.0 / (1.0 + jnp.exp(-gate_pre))
    silu = gate_pre * sigmoid
    grad_gate = grad * up_pre * (sigmoid + silu * (1.0 - sigmoid))
    return silu * up_pre, grad_gate, grad * silu


def call(body, out, *args, scratch=(), scalars=0, limit=48):
    bf16_kinds = [jax.ShapeDtypeStruct(shape, kind) for shape, kind in out]
    return pl.pallas_call(
        body,
        out_shape=bf16_kinds,
        in_specs=[SMEM] * scalars + [VMEM] * (len(args) - scalars),
        out_specs=[VMEM] * len(out),
        scratch_shapes=[pltpu.VMEM(shape, kind) for shape, kind in scratch],
        compiler_params=pltpu.CompilerParams(vmem_limit_bytes=limit * 2**20),
        cost_estimate=NO_COST,
    )(*args)


def join_rows(spot, refs, target):
    rows = refs[0].shape[0]
    for k, ref in enumerate(refs):
        target[pl.ds(pl.multiple_of((spot ^ k) * rows, 16), rows), :] = ref[...]


def expert_kernel(where, rows, grads, pair_in, down_in):
    part = down_in[0].shape[1]
    count, width = rows[0].shape
    units = down_in[0].shape[2]
    step = count // 2
    bf16, f32 = jnp.bfloat16, jnp.float32

    def body(*refs):
        spot, rows_refs, grad_refs = refs[0], refs[1:3], refs[3:5]
        pair_refs, down_refs = refs[5:7], refs[7:9]
        down_ref, own_ref, other_ref = refs[9:12]
        act_refs, back_gate_refs, back_up_refs = refs[12:14], refs[14:16], refs[16:18]
        gate_ref, up_ref = refs[18:]
        for target, views in (
            (gate_ref, [ref.at[n, 0] for n in (0, 1) for ref in pair_refs]),
            (up_ref, [ref.at[n, 1] for n in (0, 1) for ref in pair_refs]),
            (down_ref, [ref.at[n] for n in (0, 1) for ref in down_refs]),
        ):
            join_rows(spot[0], views, target)
        for half in (1, 0):

            def chunk(i, carry, half=half):
                span = pl.ds(pl.multiple_of(i * step, 16), step)
                row = rows_refs[half][span, :]
                gate_pre = dot(row, gate_ref[...], NN)
                up_pre = dot(row, up_ref[...], NN)
                grad = dot(grad_refs[half][span, :], down_ref[...], NN)
                act, grad_gate, grad_up = gated_back(grad, gate_pre, up_pre)
                grad_gate, grad_up = grad_gate.astype(bf16), grad_up.astype(bf16)
                act_refs[half][span, :] = act.astype(bf16)
                back_gate_refs[half][span, :] = grad_gate
                back_up_refs[half][span, :] = grad_up
                back = dot(grad_gate, gate_ref[...], NT) + dot(grad_up, up_ref[...], NT)
                if half:
                    other_ref[span, :] = back.astype(bf16)
                else:
                    own_ref[span, :] = back
                return carry

            lax.fori_loop(0, 2, chunk, 0)

    weight = ((4 * part, units), bf16)
    saved = ((count, units), bf16)
    outs = call(
        body,
        [weight] + [((count, width), f32), ((count, width), bf16)] + [saved] * 6,
        where,
        *rows,
        *grads,
        *pair_in,
        *down_in,
        scratch=[weight] * 2,
        scalars=1,
        limit=52,
    )
    return outs[0], outs[1], outs[2], outs[3:5], outs[5:7], outs[7:9]


def expert_grad_kernel(rows, grads, acts, back_gates, back_ups, down):
    count, width = rows[0].shape
    units = acts[0].shape[1]
    step = 256
    bf16, f32 = jnp.bfloat16, jnp.float32

    def body(*refs):
        rows_refs, grad_refs, act_refs, gate_refs, up_refs = (refs[2 * n : 2 * n + 2] for n in range(5))
        down_ref, own_ref, other_ref, gate_out, up_out, down_out = refs[10:16]

        def chunk(i, carry):
            span = pl.ds(pl.multiple_of(i * step, 128), step)
            for left, right, target in (
                (rows_refs, gate_refs, gate_out),
                (rows_refs, up_refs, up_out),
                (grad_refs, act_refs, down_out),
            ):
                target[:, span] = (
                    dot(left[0][...], right[0][:, span], TN)
                    + dot(left[1][...], right[1][:, span], TN)
                ).astype(bf16)
            return carry

        lax.fori_loop(0, units // step, chunk, 0)
        own_ref[...] = dot(act_refs[0][...], down_ref[...], NT)
        other_ref[...] = dot(act_refs[1][...], down_ref[...], NT).astype(bf16)

    return call(
        body,
        [
            ((count, width), f32),
            ((count, width), bf16),
            *[((width, units), bf16)] * 3,
        ],
        *rows,
        *grads,
        *acts,
        *back_gates,
        *back_ups,
        down,
        limit=52,
    )


def dense_kernel(normed, pack, weight):
    rows, width = normed[0].shape
    units = weight.shape[1] // 3
    bf16, f32 = jnp.bfloat16, jnp.float32

    def body(*refs):
        normed_refs = (refs[0], refs[1], refs[2].at[0], refs[2].at[1])
        grad_refs = pack_views(*refs[3:6], 1)
        weight, back_own, back_near, back_far, out_own, out_near, out_far, total_ref = refs[6:14]
        normed_all, grad_all, wide, act_all = refs[14:]
        gate, up, down = (slice(n * units, (n + 1) * units) for n in range(3))
        for i in range(4):
            row = normed_refs[i][...]
            grad_row = grad_refs[i][...]
            span = slice(i * rows, (i + 1) * rows)
            normed_all[span, :] = row
            grad_all[span, :] = grad_row
            gate_pre = dot(row, weight[:, gate], NN)
            up_pre = dot(row, weight[:, up], NN)
            grad = dot(grad_row, weight[:, down], NN)
            act, grad_gate, grad_up = gated_back(grad, gate_pre, up_pre)
            act = act.astype(bf16)
            act_all[span, :] = act
            wide[span, :units] = grad_gate.astype(bf16)
            wide[span, units:] = grad_up.astype(bf16)
            out = dot(act, weight[:, down], NT)
            back = dot(wide[span, :], weight[:, : 2 * units], NT)
            if i < 2:
                (out_own, out_near)[i][...] = out
                (back_own, back_near)[i][...] = back
            else:
                out_far[i - 2] = out.astype(bf16)
                back_far[i - 2] = back.astype(bf16)
        total_ref[:, : 2 * units] = dot(normed_all[...], wide[...], TN).astype(bf16)
        total_ref[:, down] = dot(grad_all[...], act_all[...], TN).astype(bf16)

    blocks = [((rows, width), f32)] * 2 + [((2, rows, width), bf16)]
    return call(
        body,
        [*blocks, *blocks, ((width, 3 * units), bf16)],
        *normed,
        *pack,
        weight,
        scratch=[
            ((4 * rows, width), bf16),
            ((4 * rows, width), bf16),
            ((4 * rows, 2 * units), bf16),
            ((4 * rows, units), bf16),
        ],
    )


def join_kernel(where, *grads):
    _, rows, cols = grads[0][0].shape
    f32 = jnp.float32

    def body(*refs):
        place = refs[0][0]
        for k in range(4):
            span = pl.ds(pl.multiple_of((place ^ k) * cols, 128), cols)
            for n in range(3):
                half = refs[1 + 3 * n + min(k, 2)].at[place >> 1 if k < 2 else k - 2]
                refs[10 + n][:, span] = half[...].astype(f32)

    return call(
        body,
        [((rows, 4 * cols), f32)] * 3,
        where,
        *(part for grad in grads for part in grad),
        scalars=1,
    )


def mix_kernel(hidden, dense, gate_map, slots_out):
    bf16, f32 = jnp.bfloat16, jnp.float32

    def body(hidden_ref, dense_ref, map_ref, slots_ref, out_ref):
        weights = map_ref[...]
        high = weights.astype(bf16)
        low = (weights - high.astype(f32)).astype(bf16)
        slots = slots_ref[...]
        mixed = dot(high, slots, TN) + dot(low, slots, TN)
        out_ref[...] = (hidden_ref[...] + dense_ref[...] + mixed).astype(bf16)

    return call(body, [(hidden.shape, bf16)], hidden, dense, gate_map, slots_out)[0]


def paired(
    tokens,
    cotangent,
    gain_attn,
    w_query,
    w_key,
    w_value,
    w_output,
    gain_ffn,
    dense_gate,
    dense_up,
    dense_down,
    expert_gate,
    expert_up,
    expert_down,
    routes,
    slot_order,
    gate_values,
    prefix_len,
):
    dp_count = lax.axis_size("dp")
    tensor_count = lax.axis_size("tensor")
    place = lax.axis_index("tensor")
    local_rows, width = tokens.shape
    length = local_rows * tensor_count
    columns = w_query.shape[1]
    shard = w_query.shape[0]
    hidden_cols = dense_gate.shape[1]
    devices = dp_count * tensor_count
    slots = EXPERTS * CAP
    bf16, f32 = jnp.bfloat16, jnp.float32

    nn, tn = NN, TN

    gain_width = 64
    pad_width = -(4 * columns + gain_width) % 128
    first_shard = jnp.concatenate(
        [
            w_query,
            w_key,
            w_value,
            gain_attn[:, None],
            gain_ffn[:, None],
            jnp.zeros((shard, gain_width - 2), bf16),
            w_output.T,
            jnp.zeros((shard, pad_width), bf16),
        ],
        axis=1,
    )
    dp_place = lax.axis_index("dp")
    pack = jnp.stack([tokens, cotangent])
    pack_near = to_across(after(pack, first_shard))
    row, core = place // 2, place % 2

    def split(values, axis, spot):
        size = values.shape[axis] // 2
        return (
            lax.dynamic_slice_in_dim(values, spot * size, size, axis=axis),
            lax.dynamic_slice_in_dim(values, (1 - spot) * size, size, axis=axis),
        )

    def cut_pieces(pieces):
        halves = [split(piece, 1, row) for piece in pieces]
        return [jnp.stack([half[n] for half in halves]) for n in (0, 1)]

    def share_beside(own, across):
        mine, other = split(jnp.stack([own, across]), 3, core)
        return mine, to_beside(other)

    def send_grads(grad):
        blocks = grad.reshape(2, 2, -1, grad.shape[1])
        mine = lax.dynamic_index_in_dim(blocks, core, 1, keepdims=False)
        beside = to_beside(lax.dynamic_index_in_dim(blocks, 1 - core, 1, keepdims=False))
        return mine, beside

    def cross_grads(mine, beside):
        halves = [lax.dynamic_index_in_dim(half, 1 - row, 0, keepdims=False) for half in (mine, beside)]
        return to_across(jnp.stack(halves))


    expert_ids = routes.reshape(-1)
    ranking = slot_order.reshape(-1)
    same_expert = expert_ids[:, None] == expert_ids[None, :]
    earlier = ranking[None, :] < ranking[:, None]
    placed = jnp.sum((same_expert & earlier).astype(jnp.int32), axis=1)
    targets = jnp.where(placed < CAP, expert_ids * CAP + placed, -1)
    slot_ids = jnp.arange(slots, dtype=jnp.int32)
    targets_two = targets.reshape(local_rows, TOP)
    hits = [slot_ids[:, None] == targets_two[None, :, k] for k in range(TOP)]
    token_map = sum(hit.astype(bf16) for hit in hits)
    gate_map = sum(jnp.where(hits[k], gate_values[None, :, k], 0.0) for k in range(TOP))
    slot_gate = jnp.sum(gate_map, axis=1)

    groups = [[i * tensor_count + x * 2 + c for i in range(dp_count) for x in (0, 1)] for c in (0, 1)]

    def exchange(slot_rows):
        return lax.all_to_all(
            slot_rows.reshape(EXPERTS, CAP, width),
            ("dp", "tensor"),
            split_axis=0,
            concat_axis=0,
            tiled=True,
            axis_index_groups=groups,
        ).reshape(slots, width)

    def sum_cores(own, other):
        return (own + to_beside(other.astype(bf16)).astype(f32)).astype(bf16)

    slot_cotangent = (dot(token_map, cotangent, nn) * slot_gate[:, None]).astype(bf16)
    pair_own, pair_sent = cut_pieces([expert_gate, expert_up])
    line = gather_line(first_shard)
    line[2:], slot_cotangent, pair_own, pair_sent = after(
        (line[2:], slot_cotangent, pair_own, pair_sent)
    )
    parts = gather_pairs(line)
    pair_across = to_across(after(pair_sent, pack_near))
    pack_far = to_beside(after(jnp.stack([pack, pack_near]), parts))
    token_blocks = (tokens, pack_near, pack_far)
    grad_own = exchange(after(slot_cotangent, parts))
    second_shard = jnp.concatenate([dense_gate, dense_up, dense_down.T], axis=1)
    second = lax.all_gather(after(second_shard, line[1:]), "dp", axis=0, tiled=True)

    where = jnp.stack([place, dp_place, prefix_len[0]])
    (
        *saved,
        sum_own,
        sum_near,
        sum_far,
    ) = attend_kernel(where, token_blocks, parts, length, columns)
    normed_all, weights, gains_both, *saved = saved
    gain_one, gain_two = gains_both[0], gains_both[1]
    inputs = tokens.astype(f32)
    hidden = inputs + sum_across(sum_own, sum_near, sum_far, pair_across)
    grad_rows = (grad_own, to_beside(grad_own))
    hidden = after(hidden, grad_rows)
    normed_two = norm_rows(hidden, gain_two).astype(bf16)

    dispatched = dot(token_map, normed_two, nn).astype(bf16)
    own_rows = exchange(dispatched)
    normed_near = to_across(after(normed_two, dispatched))
    down_own, down_sent = cut_pieces([expert_down.T])
    down_across = to_across(after(down_sent, normed_near))
    normed_far = to_beside(jnp.stack([normed_two, normed_near]))
    back_own, back_near, back_far, out_own, out_near, out_far, second_grad = dense_kernel(
        (normed_two, normed_near, normed_far), (cotangent, pack_near, pack_far), second
    )
    second_total = lax.psum_scatter(second_grad, "dp", scatter_dimension=0, tiled=True)
    down_across = after(down_across, second_grad)
    pair_in = share_beside(pair_own, pair_across)
    down_in = [part[:, 0] for part in share_beside(down_own, down_across)]
    own_rows, back_far, out_far = after((own_rows, back_far, out_far), second_grad, down_in, pair_in)
    expert_rows = (own_rows, to_beside(own_rows))
    dense_back = sum_across(back_own, back_near, back_far)
    piece_down_t, slots_own, slots_other, acts, grads_gate, grads_up = expert_kernel(
        where, expert_rows, grad_rows, pair_in, down_in
    )
    back_rows = sum_cores(slots_own, slots_other)
    slots_back = exchange(back_rows)

    mixed_own, mixed_other, gate_grad, up_grad, down_grad = expert_grad_kernel(
        after(expert_rows, back_rows), grad_rows, acts, grads_gate, grads_up, piece_down_t
    )
    out_rows = sum_cores(mixed_own, mixed_other)
    gate_parts = send_grads(gate_grad)
    up_parts, down_parts = send_grads(up_grad), send_grads(down_grad)
    slots_back = after(slots_back, out_rows, dense_back, gate_parts, up_parts, down_parts)

    expert_back = dot(token_map, slots_back, tn)
    grad_normed_two = dense_back + expert_back
    grad_hidden_norm, grad_gain_two = norm_back(hidden, gain_two, grad_normed_two)
    grad_hidden = cotangent.astype(f32) + grad_hidden_norm

    grad_attn_own = grad_hidden.astype(bf16)
    grad_near = to_across(grad_attn_own)
    grad_far = to_beside(jnp.stack([grad_attn_own, grad_near]))
    slots_out = exchange(after(out_rows, grad_attn_own))
    gate_parts += (cross_grads(*after(gate_parts, grad_near)),)
    up_parts += (cross_grads(*after(up_parts, grad_near)),)
    first_grad, back_own, back_near, back_far = attend_back_kernel(
        where,
        token_blocks,
        (grad_attn_own, grad_near, grad_far),
        [normed_all, weights, *saved],
        grad_gain_two[None],
        length,
        columns,
    )
    first_grad = after(first_grad, slots_out, gate_parts)
    first_parts = lax.all_to_all(
        first_grad.reshape(dp_count, shard, -1), "dp", split_axis=0, concat_axis=0, tiled=True
    )
    grad_normed_one = sum_across(back_own, back_near, back_far, up_parts)
    grad_input_norm, _ = norm_back(inputs, gain_one, grad_normed_one)
    grad_tokens = grad_hidden + grad_input_norm
    down_parts, out_far = after((down_parts, out_far), first_grad)
    down_parts += (cross_grads(*down_parts),)
    dense_out = sum_across(out_own, out_near, out_far)
    slots_out, gate_parts, up_parts = after((slots_out, gate_parts, up_parts), first_grad)
    block_out = mix_kernel(hidden, dense_out, gate_map, slots_out)
    gate_total, up_total, down_total = join_kernel(where, gate_parts, up_parts, down_parts)
    second_total = after(second_total, block_out).astype(f32)
    first_parts = after(first_parts, block_out, gate_total)
    first_total = jnp.sum(first_parts.astype(f32), axis=0)
    gains = first_total[:, 3 * columns : 3 * columns + 2].T
    gains = gains + to_beside(gains)
    gains = gains + to_across(gains)
    return (
        block_out,
        grad_tokens,
        gains[0],
        first_total[:, :columns],
        first_total[:, columns : 2 * columns],
        first_total[:, 2 * columns : 3 * columns],
        first_total[:, 3 * columns + gain_width :][:, :columns].T,
        gains[1],
        second_total[:, :hidden_cols],
        second_total[:, hidden_cols : 2 * hidden_cols],
        second_total[:, 2 * hidden_cols :].T,
        gate_total,
        up_total,
        down_total.T,
    )


def gather_rows(rows_in):
    return lax.all_gather(rows_in, "tensor", axis=0, tiled=True)


def sum_rows(rows_in):
    return lax.psum_scatter(rows_in, "tensor", scatter_dimension=0, tiled=True)


def gather_attn_rows(rows_in):
    return lax.all_gather(rows_in, "tensor", axis=0, tiled=True)


def sum_attn_rows(rows_in):
    return lax.psum_scatter(rows_in, "tensor", scatter_dimension=0, tiled=True)


def general(
    tokens,
    cotangent,
    gain_attn,
    w_query,
    w_key,
    w_value,
    w_output,
    gain_ffn,
    dense_gate,
    dense_up,
    dense_down,
    expert_gate,
    expert_up,
    expert_down,
    routes,
    slot_order,
    gate_values,
    prefix_len,
):
    dp_count = lax.axis_size("dp")
    tensor_count = lax.axis_size("tensor")
    local_rows = tokens.shape[0]
    model_width = tokens.shape[1]
    length = local_rows * tensor_count
    splits = max(1, dp_count // EXPERTS)
    per_device = max(1, EXPERTS // dp_count)
    inputs = tokens.astype(jnp.float32)
    dense_all = (
        lax.all_gather(gain_attn, "dp", axis=0, tiled=True),
        lax.all_gather(w_query, "dp", axis=0, tiled=True),
        lax.all_gather(w_key, "dp", axis=0, tiled=True),
        lax.all_gather(w_value, "dp", axis=0, tiled=True),
        lax.all_gather(w_output, "dp", axis=1, tiled=True),
        lax.all_gather(gain_ffn, "dp", axis=0, tiled=True),
        lax.all_gather(dense_gate, "dp", axis=0, tiled=True),
        lax.all_gather(dense_up, "dp", axis=0, tiled=True),
        lax.all_gather(dense_down, "dp", axis=1, tiled=True),
    )
    (
        gain_one,
        query_full,
        key_full,
        value_full,
        output_full,
        gain_two,
        gate_full,
        up_full,
        down_full,
    ) = dense_all
    gain_one = gain_one.astype(jnp.float32)
    gain_two = gain_two.astype(jnp.float32)
    positions = jnp.arange(length, dtype=jnp.int32)
    prefix_value = prefix_len[0]
    normed_one = norm_rows(inputs, gain_one).astype(jnp.bfloat16)
    head_count = query_full.shape[1] // HEAD_DIM
    normed_all = gather_attn_rows(normed_one)
    queries = rotary(
        jnp.dot(normed_all, query_full, preferred_element_type=jnp.float32).reshape(
            length, head_count, HEAD_DIM
        ),
        positions,
        1.0,
    ).astype(jnp.bfloat16)
    keys_all = rotary(
        jnp.dot(normed_all, key_full, preferred_element_type=jnp.float32).reshape(
            length, head_count, HEAD_DIM
        ),
        positions,
        1.0,
    ).astype(jnp.bfloat16)
    values_all = (
        jnp.dot(normed_all, value_full, preferred_element_type=jnp.float32)
        .astype(jnp.bfloat16)
        .reshape(length, head_count, HEAD_DIM)
    )
    score_scale = 1.0 / math.sqrt(HEAD_DIM)
    block_rows = min(512, length)
    blocks = length // block_rows
    query_blocks = queries.reshape(blocks, block_rows, head_count, HEAD_DIM)
    position_blocks = positions.reshape(blocks, block_rows)

    def block_scores(block_query, block_pos):
        scores = (
            jnp.einsum("qhd,khd->hqk", block_query, keys_all, preferred_element_type=jnp.float32)
            * score_scale
        )
        visible = (positions[None, :] <= block_pos[:, None]) | (positions[None, :] < prefix_value)
        return jnp.where(visible[None], scores, -1e30)

    def attend(block_item):
        block_query, block_pos = block_item
        scores = block_scores(block_query, block_pos)
        row_top = jnp.max(scores, axis=-1, keepdims=True)
        exponent = jnp.exp(scores - row_top)
        row_total = jnp.sum(exponent, axis=-1, keepdims=True)
        softmaxed = exponent / row_total
        mixture = jnp.einsum(
            "hqk,khd->qhd",
            softmaxed.astype(jnp.bfloat16),
            values_all,
            preferred_element_type=jnp.float32,
        ).astype(jnp.bfloat16)
        return (mixture, (row_top + jnp.log(row_total))[..., 0])

    attended, log_totals = lax.map(attend, (query_blocks, position_blocks))
    attended = attended.reshape(length, head_count * HEAD_DIM)
    hidden = inputs + sum_attn_rows(
        jnp.dot(attended, output_full, preferred_element_type=jnp.float32)
    )
    normed_two = norm_rows(hidden, gain_two).astype(jnp.bfloat16)
    normed_two_all = gather_rows(normed_two)
    gate_pre = jnp.dot(normed_two_all, gate_full, preferred_element_type=jnp.float32)
    up_pre = jnp.dot(normed_two_all, up_full, preferred_element_type=jnp.float32)
    activated = (jax.nn.silu(gate_pre) * up_pre).astype(jnp.bfloat16)
    dense_out = sum_rows(jnp.dot(activated, down_full, preferred_element_type=jnp.float32))
    expert_ids = routes.reshape(-1)
    ranking = slot_order.reshape(-1)
    same_expert = expert_ids[:, None] == expert_ids[None, :]
    earlier = ranking[None, :] < ranking[:, None]
    placed = jnp.sum((same_expert & earlier).astype(jnp.int32), axis=1)
    usable = placed < CAP
    targets = jnp.where(usable, expert_ids * CAP + placed, -1)
    slot_ids = jnp.arange(EXPERTS * CAP, dtype=jnp.int32)
    pair_map = (slot_ids[:, None] == targets[None, :]).astype(jnp.float32)
    token_map = jnp.sum(pair_map.reshape(EXPERTS * CAP, local_rows, TOP), axis=2).astype(
        jnp.bfloat16
    )
    dispatched = jnp.dot(token_map, normed_two, preferred_element_type=jnp.float32).astype(
        jnp.bfloat16
    )
    outgoing = jnp.broadcast_to(
        dispatched.reshape(EXPERTS, 1, CAP, model_width), (EXPERTS, splits, CAP, model_width)
    ).reshape(dp_count, per_device, CAP, model_width)
    expert_all = (
        lax.all_gather(expert_gate, "tensor", axis=0, tiled=True),
        lax.all_gather(expert_up, "tensor", axis=0, tiled=True),
        lax.all_gather(expert_down, "tensor", axis=1, tiled=True),
    )
    piece_width = expert_all[0].shape[1] // per_device
    gate_pieces = expert_all[0].reshape(model_width, per_device, piece_width)
    up_pieces = expert_all[1].reshape(model_width, per_device, piece_width)
    down_pieces = expert_all[2].reshape(per_device, piece_width, model_width)
    received = lax.all_to_all(outgoing, "dp", split_axis=0, concat_axis=0, tiled=True)
    gate_local = jnp.einsum(
        "sjnd,djp->sjnp", received, gate_pieces, preferred_element_type=jnp.float32
    )
    up_local = jnp.einsum("sjnd,djp->sjnp", received, up_pieces, preferred_element_type=jnp.float32)
    active_local = (jax.nn.silu(gate_local) * up_local).astype(jnp.bfloat16)
    result_local = jnp.einsum(
        "sjnp,jpd->sjnd", active_local, down_pieces, preferred_element_type=jnp.float32
    ).astype(jnp.bfloat16)
    returned = lax.all_to_all(result_local, "dp", split_axis=0, concat_axis=0, tiled=True)
    returned, kept_in, gate_local, up_local = (returned, received, gate_local, up_local)
    expert_sums = jnp.sum(
        returned.reshape(EXPERTS, splits, CAP, model_width).astype(jnp.float32), axis=1
    ).reshape(EXPERTS * CAP, model_width)
    pick_index = jnp.where(usable, targets, 0)
    pair_weight = jnp.where(usable, gate_values.reshape(-1), 0.0)
    picked = jnp.take(expert_sums, pick_index, axis=0) * pair_weight[:, None]
    expert_mix = jnp.sum(picked.reshape(local_rows, TOP, model_width), axis=1)
    block_out = (hidden + dense_out + expert_mix).astype(jnp.bfloat16)
    dense_back = (
        lax.all_gather(gain_attn, "dp", axis=0, tiled=True),
        lax.all_gather(w_query, "dp", axis=0, tiled=True),
        lax.all_gather(w_key, "dp", axis=0, tiled=True),
        lax.all_gather(w_value, "dp", axis=0, tiled=True),
        lax.all_gather(w_output, "dp", axis=1, tiled=True),
        lax.all_gather(gain_ffn, "dp", axis=0, tiled=True),
        lax.all_gather(dense_gate, "dp", axis=0, tiled=True),
        lax.all_gather(dense_up, "dp", axis=0, tiled=True),
        lax.all_gather(dense_down, "dp", axis=1, tiled=True),
    )
    (
        gain_one,
        query_full,
        key_full,
        value_full,
        output_full,
        gain_two,
        gate_full,
        up_full,
        down_full,
    ) = dense_back
    gain_one = gain_one.astype(jnp.float32)
    gain_two = gain_two.astype(jnp.float32)
    grad_out = cotangent.astype(jnp.float32)
    cotangent_all = gather_rows(cotangent)
    grad_down = jnp.einsum(
        "lf,ld->fd", activated, cotangent_all, preferred_element_type=jnp.float32
    )
    grad_act = jnp.einsum("ld,fd->lf", cotangent_all, down_full, preferred_element_type=jnp.float32)
    grad_gate_pre, grad_up_pre = swiglu_back(grad_act, gate_pre, up_pre)
    grad_gate = jnp.einsum(
        "ld,lf->df", normed_two_all, grad_gate_pre, preferred_element_type=jnp.float32
    )
    grad_up = jnp.einsum(
        "ld,lf->df", normed_two_all, grad_up_pre, preferred_element_type=jnp.float32
    )
    dense_back_in = jnp.einsum(
        "lf,df->ld", grad_gate_pre, gate_full, preferred_element_type=jnp.float32
    ) + jnp.einsum("lf,df->ld", grad_up_pre, up_full, preferred_element_type=jnp.float32)
    slot_gate = jnp.dot(pair_map, gate_values.reshape(-1), precision=lax.Precision.HIGHEST)
    slot_cotangent = jnp.dot(token_map, cotangent, preferred_element_type=jnp.float32)
    grad_slots = (slot_cotangent * slot_gate[:, None]).astype(jnp.bfloat16)
    grad_outgoing = jnp.broadcast_to(
        grad_slots.reshape(EXPERTS, 1, CAP, model_width), (EXPERTS, splits, CAP, model_width)
    ).reshape(dp_count, per_device, CAP, model_width)
    grad_received = lax.all_to_all(grad_outgoing, "dp", split_axis=0, concat_axis=0, tiled=True)
    active_local = (jax.nn.silu(gate_local) * up_local).astype(jnp.bfloat16)
    grad_down_expert = jnp.einsum(
        "sjnp,sjnd->jpd", active_local, grad_received, preferred_element_type=jnp.float32
    ).reshape(per_device * piece_width, model_width)
    grad_act_expert = jnp.einsum(
        "sjnd,jpd->sjnp", grad_received, down_pieces, preferred_element_type=jnp.float32
    )
    grad_gate_local, grad_up_local = swiglu_back(grad_act_expert, gate_local, up_local)
    grad_gate_expert = jnp.einsum(
        "sjnd,sjnp->djp", kept_in, grad_gate_local, preferred_element_type=jnp.float32
    ).reshape(model_width, per_device * piece_width)
    grad_up_expert = jnp.einsum(
        "sjnd,sjnp->djp", kept_in, grad_up_local, preferred_element_type=jnp.float32
    ).reshape(model_width, per_device * piece_width)
    grad_in_expert = (
        jnp.einsum(
            "sjnp,djp->sjnd", grad_gate_local, gate_pieces, preferred_element_type=jnp.float32
        )
        + jnp.einsum("sjnp,djp->sjnd", grad_up_local, up_pieces, preferred_element_type=jnp.float32)
    ).astype(jnp.bfloat16)
    grad_back = lax.all_to_all(grad_in_expert, "dp", split_axis=0, concat_axis=0, tiled=True)
    grad_slots_in = jnp.sum(
        grad_back.reshape(EXPERTS, splits, CAP, model_width).astype(jnp.float32), axis=1
    ).reshape(EXPERTS * CAP, model_width)
    grad_pairs = jnp.where(usable[:, None], jnp.take(grad_slots_in, pick_index, axis=0), 0.0)
    expert_back = jnp.sum(grad_pairs.reshape(local_rows, TOP, model_width), axis=1)
    grad_normed_two = sum_rows(dense_back_in) + expert_back
    grad_hidden_norm, grad_gain_two_part = norm_back(hidden, gain_two, grad_normed_two)
    grad_hidden = grad_out + grad_hidden_norm
    query_use, key_use, value_use, output_use = (query_full, key_full, value_full, output_full)
    grad_attn_in = gather_attn_rows(grad_hidden.astype(jnp.bfloat16))
    grad_output_w = jnp.einsum(
        "lc,ld->cd", attended, grad_attn_in, preferred_element_type=jnp.float32
    )
    grad_attended = (
        jnp.einsum("ld,cd->lc", grad_attn_in, output_use, preferred_element_type=jnp.float32)
        .astype(jnp.bfloat16)
        .reshape(blocks, block_rows, head_count, HEAD_DIM)
    )

    def attend_back(running, block_item):
        grad_keys, grad_values = running
        block_query, block_pos, block_grad, block_total = block_item
        scores = block_scores(block_query, block_pos)
        softmaxed = jnp.exp(scores - block_total[..., None])
        grad_soft = jnp.einsum(
            "qhd,khd->hqk", block_grad, values_all, preferred_element_type=jnp.float32
        )
        inner_sum = jnp.sum(softmaxed * grad_soft, axis=-1, keepdims=True)
        grad_scores = (softmaxed * (grad_soft - inner_sum)).astype(jnp.bfloat16)
        grad_block = (
            jnp.einsum("hqk,khd->qhd", grad_scores, keys_all, preferred_element_type=jnp.float32)
            * score_scale
        )
        grad_keys = (
            grad_keys
            + jnp.einsum(
                "hqk,qhd->khd", grad_scores, block_query, preferred_element_type=jnp.float32
            )
            * score_scale
        )
        grad_values = grad_values + jnp.einsum(
            "hqk,qhd->khd",
            softmaxed.astype(jnp.bfloat16),
            block_grad,
            preferred_element_type=jnp.float32,
        )
        return ((grad_keys, grad_values), grad_block)

    zero_start = (
        jnp.zeros((length, head_count, HEAD_DIM), jnp.float32),
        jnp.zeros((length, head_count, HEAD_DIM), jnp.float32),
    )
    (grad_keys, grad_values), grad_queries = lax.scan(
        attend_back, zero_start, (query_blocks, position_blocks, grad_attended, log_totals)
    )
    grad_queries = (
        rotary(grad_queries.reshape(length, head_count, HEAD_DIM), positions, -1.0)
        .astype(jnp.bfloat16)
        .reshape(length, head_count * HEAD_DIM)
    )
    grad_keys = (
        rotary(grad_keys, positions, -1.0)
        .astype(jnp.bfloat16)
        .reshape(length, head_count * HEAD_DIM)
    )
    grad_values = grad_values.astype(jnp.bfloat16).reshape(length, head_count * HEAD_DIM)
    grad_query_w = jnp.einsum(
        "ld,lc->dc", normed_all, grad_queries, preferred_element_type=jnp.float32
    )
    grad_key_w = jnp.einsum("ld,lc->dc", normed_all, grad_keys, preferred_element_type=jnp.float32)
    grad_value_w = jnp.einsum(
        "ld,lc->dc", normed_all, grad_values, preferred_element_type=jnp.float32
    )
    normed_back_part = (
        jnp.einsum("lc,dc->ld", grad_queries, query_use, preferred_element_type=jnp.float32)
        + jnp.einsum("lc,dc->ld", grad_keys, key_use, preferred_element_type=jnp.float32)
        + jnp.einsum("lc,dc->ld", grad_values, value_use, preferred_element_type=jnp.float32)
    )
    grad_normed_one = sum_attn_rows(normed_back_part)
    grad_input_norm, grad_gain_one_part = norm_back(inputs, gain_one, grad_normed_one)
    grad_tokens = grad_hidden + grad_input_norm
    dense_grads = (
        lax.psum_scatter(grad_gain_one_part, "dp", scatter_dimension=0, tiled=True),
        lax.psum_scatter(grad_query_w, "dp", scatter_dimension=0, tiled=True),
        lax.psum_scatter(grad_key_w, "dp", scatter_dimension=0, tiled=True),
        lax.psum_scatter(grad_value_w, "dp", scatter_dimension=0, tiled=True),
        lax.psum_scatter(grad_output_w, "dp", scatter_dimension=1, tiled=True),
        lax.psum_scatter(grad_gain_two_part, "dp", scatter_dimension=0, tiled=True),
        lax.psum_scatter(grad_gate, "dp", scatter_dimension=0, tiled=True),
        lax.psum_scatter(grad_up, "dp", scatter_dimension=0, tiled=True),
        lax.psum_scatter(grad_down, "dp", scatter_dimension=1, tiled=True),
    )
    gain_totals = lax.psum((dense_grads[0], dense_grads[5]), "tensor")
    expert_grads = (
        lax.psum_scatter(
            grad_gate_expert.astype(jnp.bfloat16), "tensor", scatter_dimension=0, tiled=True
        ).astype(jnp.float32),
        lax.psum_scatter(
            grad_up_expert.astype(jnp.bfloat16), "tensor", scatter_dimension=0, tiled=True
        ).astype(jnp.float32),
        lax.psum_scatter(
            grad_down_expert.astype(jnp.bfloat16), "tensor", scatter_dimension=1, tiled=True
        ).astype(jnp.float32),
    )
    return (
        block_out,
        grad_tokens,
        gain_totals[0],
        dense_grads[1],
        dense_grads[2],
        dense_grads[3],
        dense_grads[4],
        gain_totals[1],
        dense_grads[6],
        dense_grads[7],
        dense_grads[8],
        expert_grads[0],
        expert_grads[1],
        expert_grads[2],
    )


def solution(mesh):
    sizes = mesh.shape
    in_pairs = sizes["tensor"] == 4 and sizes["dp"] * 2 == EXPERTS
    local = paired if in_pairs else general
    return jax.shard_map(
        local,
        mesh=mesh,
        in_specs=(
            P(("dp", "tensor"), None),
            P(("dp", "tensor"), None),
            P("dp"),
            P("dp", "tensor"),
            P("dp", "tensor"),
            P("dp", "tensor"),
            P("tensor", "dp"),
            P("dp"),
            P("dp", "tensor"),
            P("dp", "tensor"),
            P("tensor", "dp"),
            P("tensor", "dp"),
            P("tensor", "dp"),
            P("dp", "tensor"),
            P(("dp", "tensor"), None),
            P(("dp", "tensor"), None),
            P(("dp", "tensor"), None),
            P("dp"),
        ),
        out_specs=(
            P(("dp", "tensor"), None),
            P(("dp", "tensor"), None),
            P("dp"),
            P("dp", "tensor"),
            P("dp", "tensor"),
            P("dp", "tensor"),
            P("tensor", "dp"),
            P("dp"),
            P("dp", "tensor"),
            P("dp", "tensor"),
            P("tensor", "dp"),
            P("tensor", "dp"),
            P("tensor", "dp"),
            P("dp", "tensor"),
        ),
        check_vma=False,
    )
```

```python
import math

import jax
import jax.numpy as jnp
import numpy as np
from jax import lax
from jax.experimental import pallas as pl
from jax.experimental.pallas import tpu as pltpu
from jax.sharding import PartitionSpec as P

HEAD_DIM = 64
EXPERTS = 16
TOP = 2
CAP = 40


epsilon = 1e-06


def norm_rows(rows_in, gain_row):
    return (
        rows_in
        * lax.rsqrt(jnp.mean(rows_in * rows_in, axis=-1, keepdims=True) + epsilon)
        * gain_row
    )


def norm_back(rows_in, gain_row, grad_out):
    inverse = lax.rsqrt(jnp.mean(rows_in * rows_in, axis=-1, keepdims=True) + epsilon)
    scaled = grad_out * gain_row
    grad_rows = inverse * scaled - rows_in * inverse**3 * jnp.mean(
        scaled * rows_in, axis=-1, keepdims=True
    )
    grad_gain = jnp.sum(grad_out * rows_in * inverse, axis=0)
    return (grad_rows, grad_gain)


def rotary(values, positions, direction):
    half_width = values.shape[-1] // 2
    frequency = jnp.power(10000.0, -jnp.arange(half_width).astype(jnp.float32) / half_width)
    angles = positions[:, None].astype(jnp.float32) * frequency[None, :]
    cosine = jnp.cos(angles)[:, None, :]
    sine_part = direction * jnp.sin(angles)[:, None, :]
    first_half = values[..., :half_width]
    second_half = values[..., half_width:]
    return jnp.concatenate(
        [
            first_half * cosine - second_half * sine_part,
            second_half * cosine + first_half * sine_part,
        ],
        axis=-1,
    )


def swiglu_back(grad_act, gate_pre, up_pre):
    sigmoid = jax.nn.sigmoid(gate_pre)
    silu_value = gate_pre * sigmoid
    grad_gate = grad_act * up_pre * sigmoid * (1.0 + gate_pre * (1.0 - sigmoid))
    grad_up = grad_act * silu_value
    return (grad_gate.astype(jnp.bfloat16), grad_up.astype(jnp.bfloat16))


def to_across(values):
    return lax.ppermute(values, "tensor", [(i, i ^ 2) for i in range(4)])


def to_beside(values):
    return lax.ppermute(values, "tensor", [(i, i ^ 1) for i in range(4)])


def gather_blocks(rows_in):
    near = jnp.stack([rows_in, to_across(rows_in)])
    return jnp.concatenate([near, to_beside(near)]).reshape(-1, rows_in.shape[-1])


def sum_across(own, near, far, *before):
    beside = to_beside(far)
    beside = [part.astype(jnp.float32) for part in after((beside[0], beside[1]))]
    sent = (near + beside[1]).astype(jnp.bfloat16)
    return own + beside[0] + to_across(after(sent, *before) if before else sent).astype(jnp.float32)


def after(value, *before):
    if not before:
        return lax.optimization_barrier(value)
    return lax.optimization_barrier((value,) + before)[0]


def sum_blocks(partial):
    blocks = partial.reshape(4, -1, partial.shape[-1])
    near = blocks[:2] + to_beside(blocks[2:].astype(jnp.bfloat16)).astype(jnp.float32)
    return near[0] + to_across(near[1].astype(jnp.bfloat16)).astype(jnp.float32)


def along(values, axis, k):
    return lax.ppermute(values, axis, [(i, i ^ k) for i in range(lax.axis_size(axis))])


def gather_line(rows_in):
    return [along(rows_in, "dp", k) if k else rows_in for k in range(0, lax.axis_size("dp"), 2)]


def gather_pairs(line):
    return [part for own in line for part in (own, along(own, "dp", 1))]


def dot(left, right, dims):
    return lax.dot_general(left, right, (dims, ((), ())), preferred_element_type=jnp.float32)


NN, NT, TN = ((1,), (0,)), ((1,), (1,)), ((0,), (0,))
ORDER = (0, 2, 1, 3)
VMEM = pl.BlockSpec(memory_space=pltpu.VMEM)
SMEM = pl.BlockSpec(memory_space=pltpu.SMEM)
HBM = pl.BlockSpec(memory_space=pltpu.HBM)
NO_COST = pl.CostEstimate(flops=0, bytes_accessed=0, transcendentals=0)


def angle_tables(length):
    half = HEAD_DIM // 2
    lane = np.arange(2 * HEAD_DIM)
    frequency = np.power(10000.0, -(lane % half).astype(np.float64) / half)
    angles = np.arange(length)[:, None] * frequency[None, :]
    sign = np.where(lane % HEAD_DIM < half, -1.0, 1.0)
    return np.cos(angles).astype(np.float32), (np.sin(angles) * sign).astype(np.float32)


def turn(values, cosine, sine):
    width = values.shape[1]
    half = HEAD_DIM // 2
    lane = lax.broadcasted_iota(jnp.int32, values.shape, 1)
    swapped = jnp.where(
        lane % HEAD_DIM < half,
        pltpu.roll(values, width - half, 1),
        pltpu.roll(values, half, 1),
    )
    repeats = width // cosine.shape[1]
    return values * jnp.concatenate([cosine] * repeats, axis=1) + swapped * jnp.concatenate(
        [sine] * repeats, axis=1
    )


def block_at(place, i):
    return place ^ ((i >> 1) | ((i & 1) << 1))


def pack_views(own, near, far, n):
    return own, near.at[n], far.at[0, n], far.at[1, n]


def seen(place, prefix, i, j, rows):
    query_block, key_block = block_at(place, i), block_at(place, j)
    return (key_block <= query_block) | (key_block * rows < prefix)


def mask_of(place, prefix, i, j, rows):
    key = block_at(place, j) * rows + lax.broadcasted_iota(jnp.int32, (rows, rows), 0)
    query = block_at(place, i) * rows + lax.broadcasted_iota(jnp.int32, (rows, rows), 1)
    return key <= jnp.maximum(query, prefix - 1)


def attend_kernel(where, blocks_in, parts, length, columns):
    rows, width = blocks_in[0].shape
    shard, lanes = parts[0].shape
    blocks = length // rows
    heads = columns // HEAD_DIM
    count = len(parts)
    gain_at = 3 * columns
    output_at = 3 * columns + 64
    bf16, f32 = jnp.bfloat16, jnp.float32
    cosine, sine = angle_tables(length)

    def body(*refs):
        spot, token_refs = refs[0], pack_views(*refs[1:4], 0)
        part_refs = refs[4 : 4 + count]
        cos_ref, sin_ref = refs[4 + count : 6 + count]
        (
            normed_ref,
            weight_ref,
            gain_ref,
            query_ref,
            query_t_ref,
            key_ref,
            value_ref,
            mixed_ref,
            mixed_t_ref,
            log_ref,
            sum_own_ref,
            sum_near_ref,
            sum_far_ref,
        ) = refs[6 + count : 19 + count]
        value_t_ref, score_ref, top_ref, total_ref, mix_ref, *keep, sems = refs[19 + count :]
        outward = [
            pltpu.make_async_copy(source, target, sems.at[n])
            for n, (source, target) in enumerate(
                zip(
                    keep,
                    (
                        normed_ref,
                        weight_ref,
                        query_ref,
                        query_t_ref,
                        key_ref,
                        value_ref,
                        mixed_ref,
                        mixed_t_ref,
                    ),
                )
            )
        ]
        (
            normed_ref,
            weight_ref,
            query_ref,
            query_t_ref,
            key_ref,
            value_ref,
            mixed_ref,
            mixed_t_ref,
        ) = keep
        place, dp_place, prefix = spot[0], spot[1], spot[2]
        for k in range(count):
            start = pl.multiple_of((dp_place ^ k) * shard, 16)
            weight_ref[pl.ds(start, shard), :] = part_refs[k][...]
        gain_tile = weight_ref[:, gain_at // 128 * 128 : gain_at // 128 * 128 + 128].astype(f32)
        gain_ref[...] = gain_tile.T[gain_at % 128 : gain_at % 128 + 8, :]
        gain = gain_ref[0:1, :]
        for i in range(blocks):
            tokens = token_refs[i][...].astype(f32)
            inverse = lax.rsqrt(jnp.mean(tokens * tokens, axis=-1, keepdims=True) + epsilon)
            normed = (tokens * inverse * gain).astype(bf16)
            span = pl.ds(i * rows, rows)
            normed_ref[span, :] = normed
            product = dot(normed, weight_ref[:, : 3 * columns], NN)
            spot_rows = pl.ds(pl.multiple_of(block_at(place, i) * rows, 8), rows)
            turned = turn(product[:, : 2 * columns], cos_ref[spot_rows, :], sin_ref[spot_rows, :])
            query = turned[:, :columns] * (1.0 / math.sqrt(HEAD_DIM))
            key = turned[:, columns:]
            value = product[:, 2 * columns :]
            query_t = query.T
            value_t = value.T
            for h in range(heads):
                cut = slice(h * HEAD_DIM, (h + 1) * HEAD_DIM)
                query_ref[h, span, :] = query[:, cut].astype(bf16)
                query_t_ref[h, :, span] = query_t[cut, :].astype(bf16)
                key_ref[h, span, :] = key[:, cut].astype(bf16)
                value_ref[h, span, :] = value[:, cut].astype(bf16)
                value_t_ref[h, :, span] = value_t[cut, :].astype(bf16)

        for copy in outward[:6]:
            copy.start()

        def query_block(i, carry):
            here = pl.ds(pl.multiple_of(i * rows, 128), rows)
            top_ref[...] = jnp.full(top_ref.shape, -1e30, f32)
            total_ref[...] = jnp.zeros(total_ref.shape, f32)
            mix_ref[...] = jnp.zeros(mix_ref.shape, f32)

            def scores(j, carry):
                @pl.when(seen(place, prefix, i, j, rows))
                def _():
                    there = pl.ds(pl.multiple_of(j * rows, 128), rows)
                    visible = mask_of(place, prefix, i, j, rows)
                    for h in range(heads):
                        score = dot(key_ref[h, there, :], query_t_ref[h, :, here], NN)
                        score = jnp.where(visible, score, -1e30)
                        score_ref[h, there, :] = score
                        top_ref[h : h + 1, :] = jnp.maximum(
                            top_ref[h : h + 1, :], jnp.max(score, axis=0, keepdims=True)
                        )

                return carry

            def mixing(j, carry):
                @pl.when(seen(place, prefix, i, j, rows))
                def _():
                    there = pl.ds(pl.multiple_of(j * rows, 128), rows)
                    for h in range(heads):
                        power = jnp.exp(score_ref[h, there, :] - top_ref[h : h + 1, :])
                        total_ref[h : h + 1, :] += jnp.sum(power, axis=0, keepdims=True)
                        mix_ref[h] += dot(value_t_ref[h, :, there], power.astype(bf16), NN)

                return carry

            lax.fori_loop(0, blocks, scores, 0)
            lax.fori_loop(0, blocks, mixing, 0)
            log_ref[:, here] = top_ref[...] + jnp.log(jnp.maximum(total_ref[...], 1e-30))
            mixed_t = jnp.concatenate(
                [mix_ref[h] * (1.0 / total_ref[h : h + 1, :]) for h in range(heads)], axis=0
            )
            for h in range(heads):
                mixed_t_ref[h, :, here] = mixed_t[h * HEAD_DIM : (h + 1) * HEAD_DIM, :].astype(bf16)
            mixed = mixed_t.T.astype(bf16)
            mixed_ref[here, :] = mixed
            partial = dot(mixed, weight_ref[:, output_at : output_at + columns], NT)

            @pl.when(i == 0)
            def _():
                sum_own_ref[...] = partial

            @pl.when(i == 1)
            def _():
                sum_near_ref[...] = partial

            @pl.when(i >= 2)
            def _():
                sum_far_ref[i - 2] = partial.astype(bf16)

            return carry

        lax.fori_loop(0, blocks, query_block, 0)
        for copy in outward[6:]:
            copy.start()
        for copy in outward:
            copy.wait()

    per_head = (heads, length, HEAD_DIM)
    per_head_t = (heads, HEAD_DIM, length)
    out_shape = [
        jax.ShapeDtypeStruct(shape, kind)
        for shape, kind in (
            ((length, width), bf16),
            ((count * shard, lanes), bf16),
            ((8, width), f32),
            (per_head, bf16),
            (per_head_t, bf16),
            (per_head, bf16),
            (per_head, bf16),
            ((length, columns), bf16),
            (per_head_t, bf16),
            ((8, length), f32),
            ((rows, width), f32),
            ((rows, width), f32),
            ((2, rows, width), bf16),
        )
    ]
    return pl.pallas_call(
        body,
        out_shape=out_shape,
        in_specs=[SMEM] + [VMEM] * (5 + count),
        out_specs=[HBM] * 2 + [VMEM] + [HBM] * 6 + [VMEM] * 4,
        scratch_shapes=[
            pltpu.VMEM(per_head_t, bf16),
            pltpu.VMEM((heads, length, rows), f32),
            pltpu.VMEM((8, rows), f32),
            pltpu.VMEM((8, rows), f32),
            pltpu.VMEM((heads, HEAD_DIM, rows), f32),
        ]
        + [pltpu.VMEM(out_shape[n].shape, bf16) for n in (0, 1, 3, 4, 5, 6, 7, 8)]
        + [pltpu.SemaphoreType.DMA((8,))],
        compiler_params=pltpu.CompilerParams(vmem_limit_bytes=60 * 2**20),
        cost_estimate=NO_COST,
    )(where, *blocks_in, *parts, cosine, sine)


def attend_back_kernel(
    where, blocks_in, grads_in, saved, gain_two, length, columns
):
    normed, weight, query, query_t, key, value, mixed, mixed_t, log_total = saved
    rows, width = blocks_in[0].shape
    lanes = weight.shape[1]
    blocks = length // rows
    heads = columns // HEAD_DIM
    output_at = 3 * columns + 64
    bf16, f32 = jnp.bfloat16, jnp.float32
    cosine, sine = angle_tables(length)

    def body(*refs):
        (
            spot,
            own_ref,
            near_ref,
            far_ref,
            grad_own_ref,
            grad_near_ref,
            grad_far_ref,
            normed_ref,
            weight_ref,
            query_ref,
            query_t_ref,
            key_ref,
            value_ref,
            mixed_ref,
            mixed_t_ref,
            log_ref,
            gain_two_ref,
            cos_ref,
            sin_ref,
            first_ref,
            back_own_ref,
            back_near_ref,
            back_far_ref,
            grad_in,
            grad_mix,
            grad_mix_t,
            inner,
            key_t,
            grad_query_t,
            grad_key,
            grad_value,
            grad_product,
            *keep,
            sems,
        ) = refs
        place, prefix = spot[0], spot[2]
        inward = [
            pltpu.make_async_copy(source, target, sems.at[n])
            for n, (source, target) in enumerate(
                zip(
                    (
                        weight_ref,
                        mixed_t_ref,
                        key_ref,
                        query_t_ref,
                        query_ref,
                        value_ref,
                        own_ref,
                        near_ref.at[0],
                        far_ref.at[0, 0],
                        far_ref.at[1, 0],
                        normed_ref,
                        mixed_ref,
                        cos_ref,
                        sin_ref,
                    ),
                    keep,
                )
            )
        ]
        for copy in inward:
            copy.start()
        (
            weight_ref,
            mixed_t_ref,
            key_ref,
            query_t_ref,
            query_ref,
            value_ref,
            *token_refs,
            normed_ref,
            mixed_ref,
            cos_ref,
            sin_ref,
        ) = keep
        grad_refs = (grad_own_ref, grad_near_ref, grad_far_ref.at[0], grad_far_ref.at[1])
        grad_key[...] = jnp.zeros(grad_key.shape, f32)
        grad_value[...] = jnp.zeros(grad_value.shape, f32)
        grad_query_t[...] = jnp.zeros(grad_query_t.shape, f32)
        for copy in inward[:3]:
            copy.wait()
        for h in range(heads):
            key_t[h] = key_ref[h].astype(f32).T.astype(bf16)
        for i in range(blocks):
            span = pl.ds(i * rows, rows)
            grad = grad_refs[i][...]
            grad_in[span, :] = grad
            mix = dot(grad, weight_ref[:, output_at : output_at + columns], NN)
            mix_t = mix.T
            for h in range(heads):
                cut = slice(h * HEAD_DIM, (h + 1) * HEAD_DIM)
                low = mix_t[cut, :].astype(bf16)
                grad_mix[h, span, :] = mix[:, cut].astype(bf16)
                grad_mix_t[h, :, span] = low
                inner[h : h + 1, span] = jnp.sum(
                    low.astype(f32) * mixed_t_ref[h, :, span].astype(f32), axis=0, keepdims=True
                )

        for copy in inward[3:6]:
            copy.wait()

        def pair(step, carry):
            i, j = step // blocks, step % blocks

            @pl.when(seen(place, prefix, i, j, rows))
            def _():
                here = pl.ds(pl.multiple_of(i * rows, 128), rows)
                there = pl.ds(pl.multiple_of(j * rows, 128), rows)
                visible = mask_of(place, prefix, i, j, rows)
                for h in range(heads):
                    score = dot(key_ref[h, there, :], query_t_ref[h, :, here], NN)
                    weigh = jnp.where(visible, jnp.exp(score - log_ref[h : h + 1, here]), 0.0)
                    soft = dot(value_ref[h, there, :], grad_mix_t[h, :, here], NN)
                    low = (weigh * (soft - inner[h : h + 1, here])).astype(bf16)
                    grad_value[h, there, :] += dot(weigh.astype(bf16), grad_mix[h, here, :], NN)
                    grad_key[h, there, :] += dot(low, query_ref[h, here, :], NN)
                    grad_query_t[h, :, here] += dot(key_t[h, :, there], low, NN)

            return carry

        lax.fori_loop(0, blocks * blocks, pair, 0)
        for copy in inward[6:]:
            copy.wait()
        gain = jnp.zeros((1, width), f32)
        for i in range(blocks):
            span = pl.ds(i * rows, rows)
            spot_rows = pl.ds(pl.multiple_of(block_at(place, i) * rows, 8), rows)
            turned = jnp.concatenate(
                [grad_query_t[h, :, span].T * (1.0 / math.sqrt(HEAD_DIM)) for h in range(heads)]
                + [grad_key[h, span, :] for h in range(heads)],
                axis=1,
            )
            turned = turn(turned, cos_ref[spot_rows, :], -sin_ref[spot_rows, :])
            grads = jnp.concatenate(
                [turned] + [grad_value[h, span, :] for h in range(heads)], axis=1
            ).astype(bf16)
            grad_product[span, :] = grads
            back = dot(grads, weight_ref[:, : 3 * columns], NT)
            tokens = token_refs[i][...].astype(f32)
            inverse = lax.rsqrt(jnp.mean(tokens * tokens, axis=-1, keepdims=True) + epsilon)
            gain += jnp.sum(back * tokens * inverse, axis=0, keepdims=True)
            if i < 2:
                (back_own_ref, back_near_ref)[i][...] = back
            else:
                back_far_ref[i - 2] = back.astype(bf16)
        gains = jnp.concatenate([gain, gain_two_ref[...], jnp.zeros((62, width), f32)], axis=0)
        first_ref[:, 3 * columns : output_at] = gains.T.astype(bf16)
        first_ref[:, : 3 * columns] = dot(normed_ref[...], grad_product[...], TN).astype(bf16)
        first_ref[:, output_at : output_at + columns] = dot(
            grad_in[...], mixed_ref[...], TN
        ).astype(bf16)
        if output_at + columns < lanes:
            first_ref[:, output_at + columns :] = jnp.zeros(
                (width, lanes - output_at - columns), bf16
            )

    per_head = (heads, length, HEAD_DIM)
    per_head_t = (heads, HEAD_DIM, length)
    out_shape = [
        jax.ShapeDtypeStruct(shape, kind)
        for shape, kind in (
            ((width, lanes), bf16),
            ((rows, width), f32),
            ((rows, width), f32),
            ((2, rows, width), bf16),
        )
    ]
    return pl.pallas_call(
        body,
        out_shape=out_shape,
        in_specs=[SMEM] + [HBM] * 3 + [VMEM] * 3 + [HBM] * 8 + [VMEM] * 2 + [HBM] * 2,
        out_specs=[VMEM] * len(out_shape),
        scratch_shapes=[
            pltpu.VMEM((length, width), bf16),
            pltpu.VMEM(per_head, bf16),
            pltpu.VMEM(per_head_t, bf16),
            pltpu.VMEM((8, length), f32),
            pltpu.VMEM(per_head_t, bf16),
            pltpu.VMEM(per_head_t, f32),
            pltpu.VMEM(per_head, f32),
            pltpu.VMEM(per_head, f32),
            pltpu.VMEM((length, 3 * columns), bf16),
        ]
        + [
            pltpu.VMEM(array.shape, array.dtype)
            for array in (
                weight,
                mixed_t,
                key,
                query_t,
                query,
                value,
                *[blocks_in[0]] * 4,
                normed,
                mixed,
                cosine,
                sine,
            )
        ]
        + [pltpu.SemaphoreType.DMA((14,))],
        compiler_params=pltpu.CompilerParams(vmem_limit_bytes=52 * 2**20),
        cost_estimate=NO_COST,
    )(where, *blocks_in, *grads_in, *saved, gain_two, cosine, sine)


def gated(gate_pre, up_pre):
    sigmoid = 1.0 / (1.0 + jnp.exp(-gate_pre))
    return gate_pre * sigmoid * up_pre


def gated_back(grad, gate_pre, up_pre):
    sigmoid = 1.0 / (1.0 + jnp.exp(-gate_pre))
    silu = gate_pre * sigmoid
    grad_gate = grad * up_pre * (sigmoid + silu * (1.0 - sigmoid))
    return silu * up_pre, grad_gate, grad * silu


def call(body, out, *args, scratch=(), scalars=0, limit=28):
    bf16_kinds = [jax.ShapeDtypeStruct(shape, kind) for shape, kind in out]
    return pl.pallas_call(
        body,
        out_shape=bf16_kinds,
        in_specs=[SMEM] * scalars + [VMEM] * (len(args) - scalars),
        out_specs=[VMEM] * len(out),
        scratch_shapes=[pltpu.VMEM(shape, kind) for shape, kind in scratch],
        compiler_params=pltpu.CompilerParams(vmem_limit_bytes=limit * 2**20),
        cost_estimate=NO_COST,
    )(*args)


def join_rows(spot, refs, target):
    rows = refs[0].shape[0]
    for k, ref in enumerate(refs):
        target[pl.ds(pl.multiple_of((spot ^ k) * rows, 16), rows), :] = ref[...]


def expert_kernel(where, rows, grads, pair_in, down_in):
    part = down_in[0].shape[1]
    count, width = rows[0].shape
    units = down_in[0].shape[2]
    step = count // 2
    bf16, f32 = jnp.bfloat16, jnp.float32

    def body(*refs):
        spot, rows_refs, grad_refs = refs[0], refs[1:3], refs[3:5]
        pair_refs, down_refs = refs[5:7], refs[7:9]
        down_ref, own_ref, other_ref = refs[9:12]
        act_refs, back_gate_refs, back_up_refs = refs[12:14], refs[14:16], refs[16:18]
        gate_ref, up_ref = refs[18:]
        for target, views in (
            (gate_ref, [ref.at[n, 0] for n in (0, 1) for ref in pair_refs]),
            (up_ref, [ref.at[n, 1] for n in (0, 1) for ref in pair_refs]),
            (down_ref, [ref.at[n] for n in (0, 1) for ref in down_refs]),
        ):
            join_rows(spot[0], views, target)
        for half in (1, 0):

            def chunk(i, carry, half=half):
                span = pl.ds(pl.multiple_of(i * step, 16), step)
                row = rows_refs[half][span, :]
                gate_pre = dot(row, gate_ref[...], NN)
                up_pre = dot(row, up_ref[...], NN)
                grad = dot(grad_refs[half][span, :], down_ref[...], NN)
                act, grad_gate, grad_up = gated_back(grad, gate_pre, up_pre)
                grad_gate, grad_up = grad_gate.astype(bf16), grad_up.astype(bf16)
                act_refs[half][span, :] = act.astype(bf16)
                back_gate_refs[half][span, :] = grad_gate
                back_up_refs[half][span, :] = grad_up
                back = dot(grad_gate, gate_ref[...], NT) + dot(grad_up, up_ref[...], NT)
                if half:
                    other_ref[span, :] = back.astype(bf16)
                else:
                    own_ref[span, :] = back
                return carry

            lax.fori_loop(0, 2, chunk, 0)

    weight = ((4 * part, units), bf16)
    saved = ((count, units), bf16)
    outs = call(
        body,
        [weight] + [((count, width), f32), ((count, width), bf16)] + [saved] * 6,
        where,
        *rows,
        *grads,
        *pair_in,
        *down_in,
        scratch=[weight] * 2,
        scalars=1,
        limit=52,
    )
    return outs[0], outs[1], outs[2], outs[3:5], outs[5:7], outs[7:9]


def expert_grad_kernel(rows, grads, acts, back_gates, back_ups, down):
    count, width = rows[0].shape
    units = acts[0].shape[1]
    step = 256
    bf16, f32 = jnp.bfloat16, jnp.float32

    def body(*refs):
        rows_refs, grad_refs, act_refs, gate_refs, up_refs = (refs[2 * n : 2 * n + 2] for n in range(5))
        down_ref, own_ref, other_ref, gate_out, up_out, down_out = refs[10:16]

        def chunk(i, carry):
            span = pl.ds(pl.multiple_of(i * step, 128), step)
            for left, right, target in (
                (rows_refs, gate_refs, gate_out),
                (rows_refs, up_refs, up_out),
                (grad_refs, act_refs, down_out),
            ):
                target[:, span] = (
                    dot(left[0][...], right[0][:, span], TN)
                    + dot(left[1][...], right[1][:, span], TN)
                ).astype(bf16)
            return carry

        lax.fori_loop(0, units // step, chunk, 0)
        own_ref[...] = dot(act_refs[0][...], down_ref[...], NT)
        other_ref[...] = dot(act_refs[1][...], down_ref[...], NT).astype(bf16)

    return call(
        body,
        [
            ((count, width), f32),
            ((count, width), bf16),
            *[((width, units), bf16)] * 3,
        ],
        *rows,
        *grads,
        *acts,
        *back_gates,
        *back_ups,
        down,
        limit=52,
    )


def dense_kernel(normed, pack, weight):
    rows, width = normed[0].shape
    units = weight.shape[1] // 3
    bf16, f32 = jnp.bfloat16, jnp.float32

    def body(*refs):
        normed_refs = (refs[0], refs[1], refs[2].at[0], refs[2].at[1])
        grad_refs = pack_views(*refs[3:6], 1)
        weight, back_own, back_near, back_far, out_own, out_near, out_far, total_ref = refs[6:14]
        normed_all, grad_all, wide, act_all = refs[14:]
        gate, up, down = (slice(n * units, (n + 1) * units) for n in range(3))
        for i in range(4):
            row = normed_refs[i][...]
            grad_row = grad_refs[i][...]
            span = slice(i * rows, (i + 1) * rows)
            normed_all[span, :] = row
            grad_all[span, :] = grad_row
            gate_pre = dot(row, weight[:, gate], NN)
            up_pre = dot(row, weight[:, up], NN)
            grad = dot(grad_row, weight[:, down], NN)
            act, grad_gate, grad_up = gated_back(grad, gate_pre, up_pre)
            act = act.astype(bf16)
            act_all[span, :] = act
            wide[span, :units] = grad_gate.astype(bf16)
            wide[span, units:] = grad_up.astype(bf16)
            out = dot(act, weight[:, down], NT)
            back = dot(wide[span, :], weight[:, : 2 * units], NT)
            if i < 2:
                (out_own, out_near)[i][...] = out
                (back_own, back_near)[i][...] = back
            else:
                out_far[i - 2] = out.astype(bf16)
                back_far[i - 2] = back.astype(bf16)
        total_ref[:, : 2 * units] = dot(normed_all[...], wide[...], TN).astype(bf16)
        total_ref[:, down] = dot(grad_all[...], act_all[...], TN).astype(bf16)

    blocks = [((rows, width), f32)] * 2 + [((2, rows, width), bf16)]
    return call(
        body,
        [*blocks, *blocks, ((width, 3 * units), bf16)],
        *normed,
        *pack,
        weight,
        scratch=[
            ((4 * rows, width), bf16),
            ((4 * rows, width), bf16),
            ((4 * rows, 2 * units), bf16),
            ((4 * rows, units), bf16),
        ],
    )


def join_kernel(where, *grads):
    _, rows, cols = grads[0][0].shape
    count = len(grads)
    f32 = jnp.float32

    def body(*refs):
        place = refs[0][0]
        for k in range(4):
            span = pl.ds(pl.multiple_of((place ^ k) * cols, 128), cols)
            for n in range(count):
                half = refs[1 + 3 * n + min(k, 2)].at[place >> 1 if k < 2 else k - 2]
                refs[1 + 3 * count + n][:, span] = half[...].astype(f32)

    return call(
        body,
        [((rows, 4 * cols), f32)] * count,
        where,
        *(part for grad in grads for part in grad),
        scalars=1,
    )


def mix_kernel(hidden, dense, gate_map, slots_out):
    bf16, f32 = jnp.bfloat16, jnp.float32

    def body(hidden_ref, dense_ref, map_ref, slots_ref, out_ref):
        weights = map_ref[...]
        high = weights.astype(bf16)
        low = (weights - high.astype(f32)).astype(bf16)
        slots = slots_ref[...]
        mixed = dot(high, slots, TN) + dot(low, slots, TN)
        out_ref[...] = (hidden_ref[...] + dense_ref[...] + mixed).astype(bf16)

    return call(body, [(hidden.shape, bf16)], hidden, dense, gate_map, slots_out)[0]


def paired(
    tokens,
    cotangent,
    gain_attn,
    w_query,
    w_key,
    w_value,
    w_output,
    gain_ffn,
    dense_gate,
    dense_up,
    dense_down,
    expert_gate,
    expert_up,
    expert_down,
    routes,
    slot_order,
    gate_values,
    prefix_len,
):
    dp_count = lax.axis_size("dp")
    tensor_count = lax.axis_size("tensor")
    place = lax.axis_index("tensor")
    local_rows, width = tokens.shape
    length = local_rows * tensor_count
    columns = w_query.shape[1]
    shard = w_query.shape[0]
    hidden_cols = dense_gate.shape[1]
    devices = dp_count * tensor_count
    slots = EXPERTS * CAP
    bf16, f32 = jnp.bfloat16, jnp.float32

    nn, tn = NN, TN

    gain_width = 64
    pad_width = -(4 * columns + gain_width) % 128
    first_shard = jnp.concatenate(
        [
            w_query,
            w_key,
            w_value,
            gain_attn[:, None],
            gain_ffn[:, None],
            jnp.zeros((shard, gain_width - 2), bf16),
            w_output.T,
            jnp.zeros((shard, pad_width), bf16),
        ],
        axis=1,
    )
    dp_place = lax.axis_index("dp")
    pack = jnp.stack([tokens, cotangent])
    pack_near = to_across(after(pack, first_shard))
    row, core = place // 2, place % 2

    def split(values, axis, spot):
        size = values.shape[axis] // 2
        return (
            lax.dynamic_slice_in_dim(values, spot * size, size, axis=axis),
            lax.dynamic_slice_in_dim(values, (1 - spot) * size, size, axis=axis),
        )

    def cut_pieces(pieces):
        halves = [split(piece, 1, row) for piece in pieces]
        return [jnp.stack([half[n] for half in halves]) for n in (0, 1)]

    def share_beside(own, across):
        mine, other = split(jnp.stack([own, across]), 3, core)
        return mine, to_beside(other)

    def send_grads(grad):
        blocks = grad.reshape(2, 2, -1, grad.shape[1])
        mine = lax.dynamic_index_in_dim(blocks, core, 1, keepdims=False)
        beside = to_beside(lax.dynamic_index_in_dim(blocks, 1 - core, 1, keepdims=False))
        return mine, beside

    def cross_grads(mine, beside):
        halves = [lax.dynamic_index_in_dim(half, 1 - row, 0, keepdims=False) for half in (mine, beside)]
        return to_across(jnp.stack(halves))


    expert_ids = routes.reshape(-1)
    ranking = slot_order.reshape(-1)
    same_expert = expert_ids[:, None] == expert_ids[None, :]
    earlier = ranking[None, :] < ranking[:, None]
    placed = jnp.sum((same_expert & earlier).astype(jnp.int32), axis=1)
    targets = jnp.where(placed < CAP, expert_ids * CAP + placed, -1)
    slot_ids = jnp.arange(slots, dtype=jnp.int32)
    targets_two = targets.reshape(local_rows, TOP)
    hits = [slot_ids[:, None] == targets_two[None, :, k] for k in range(TOP)]
    token_map = sum(hit.astype(bf16) for hit in hits)
    gate_map = sum(jnp.where(hits[k], gate_values[None, :, k], 0.0) for k in range(TOP))
    slot_gate = jnp.sum(gate_map, axis=1)

    groups = [[i * tensor_count + x * 2 + c for i in range(dp_count) for x in (0, 1)] for c in (0, 1)]

    def exchange(slot_rows):
        return lax.all_to_all(
            slot_rows.reshape(EXPERTS, CAP, width),
            ("dp", "tensor"),
            split_axis=0,
            concat_axis=0,
            tiled=True,
            axis_index_groups=groups,
        ).reshape(slots, width)

    def sum_cores(own, other):
        return (own + to_beside(other.astype(bf16)).astype(f32)).astype(bf16)

    slot_cotangent = (dot(token_map, cotangent, nn) * slot_gate[:, None]).astype(bf16)
    pair_own, pair_sent = cut_pieces([expert_gate, expert_up])
    line = gather_line(first_shard)
    line[2:], slot_cotangent, pair_own, pair_sent = after(
        (line[2:], slot_cotangent, pair_own, pair_sent)
    )
    parts = gather_pairs(line)
    pair_across = to_across(after(pair_sent, pack_near))
    pack_far = to_beside(after(jnp.stack([pack, pack_near]), parts))
    token_blocks = (tokens, pack_near, pack_far)
    grad_own = exchange(after(slot_cotangent, parts))
    second_shard = jnp.concatenate([dense_gate, dense_up, dense_down.T], axis=1)
    second = lax.all_gather(after(second_shard, line[1:]), "dp", axis=0, tiled=True)

    where = jnp.stack([place, dp_place, prefix_len[0]])
    (
        *saved,
        sum_own,
        sum_near,
        sum_far,
    ) = attend_kernel(where, token_blocks, parts, length, columns)
    normed_all, weights, gains_both, *saved = saved
    gain_one, gain_two = gains_both[0], gains_both[1]
    inputs = tokens.astype(f32)
    hidden = inputs + sum_across(sum_own, sum_near, sum_far, pair_across)
    grad_rows = (grad_own, to_beside(grad_own))
    hidden = after(hidden, grad_rows)
    normed_two = norm_rows(hidden, gain_two).astype(bf16)

    dispatched = dot(token_map, normed_two, nn).astype(bf16)
    own_rows = exchange(dispatched)
    normed_near = to_across(after(normed_two, dispatched))
    down_own, down_sent = cut_pieces([expert_down.T])
    down_across = to_across(after(down_sent, normed_near))
    normed_far = to_beside(jnp.stack([normed_two, normed_near]))
    back_own, back_near, back_far, out_own, out_near, out_far, second_grad = dense_kernel(
        (normed_two, normed_near, normed_far), (cotangent, pack_near, pack_far), second
    )
    second_total = lax.psum_scatter(second_grad, "dp", scatter_dimension=0, tiled=True)
    down_across = after(down_across, second_grad)
    pair_in = share_beside(pair_own, pair_across)
    down_in = [part[:, 0] for part in share_beside(down_own, down_across)]
    own_rows, back_far, out_far = after((own_rows, back_far, out_far), second_grad, down_in, pair_in)
    expert_rows = (own_rows, to_beside(own_rows))
    dense_back = sum_across(back_own, back_near, back_far)
    piece_down_t, slots_own, slots_other, acts, grads_gate, grads_up = expert_kernel(
        where, expert_rows, grad_rows, pair_in, down_in
    )
    back_rows = sum_cores(slots_own, slots_other)
    slots_back = exchange(back_rows)

    mixed_own, mixed_other, gate_grad, up_grad, down_grad = expert_grad_kernel(
        after(expert_rows, back_rows), grad_rows, acts, grads_gate, grads_up, piece_down_t
    )
    out_rows = sum_cores(mixed_own, mixed_other)
    gate_parts = send_grads(gate_grad)
    up_parts, down_parts = send_grads(up_grad), send_grads(down_grad)
    slots_back = after(slots_back, out_rows, dense_back, gate_parts, up_parts, down_parts)

    expert_back = dot(token_map, slots_back, tn)
    grad_normed_two = dense_back + expert_back
    grad_hidden_norm, grad_gain_two = norm_back(hidden, gain_two, grad_normed_two)
    grad_hidden = cotangent.astype(f32) + grad_hidden_norm

    grad_attn_own = grad_hidden.astype(bf16)
    grad_near = to_across(grad_attn_own)
    grad_far = to_beside(jnp.stack([grad_attn_own, grad_near]))
    slots_out = exchange(after(out_rows, grad_attn_own))
    gate_parts += (cross_grads(*after(gate_parts, grad_near)),)
    up_parts += (cross_grads(*after(up_parts, grad_near)),)
    first_grad, back_own, back_near, back_far = attend_back_kernel(
        where,
        token_blocks,
        (grad_attn_own, grad_near, grad_far),
        [normed_all, weights, *saved],
        grad_gain_two[None],
        length,
        columns,
    )
    first_grad = after(first_grad, slots_out, gate_parts)
    first_parts = lax.all_to_all(
        first_grad.reshape(dp_count, shard, -1), "dp", split_axis=0, concat_axis=0, tiled=True
    )
    grad_normed_one = sum_across(back_own, back_near, back_far, up_parts)
    grad_input_norm, _ = norm_back(inputs, gain_one, grad_normed_one)
    grad_tokens = grad_hidden + grad_input_norm
    down_parts, out_far = after((down_parts, out_far), first_grad)
    down_parts += (cross_grads(*down_parts),)
    dense_out = sum_across(out_own, out_near, out_far)
    slots_out, gate_parts, up_parts = after((slots_out, gate_parts, up_parts), first_grad)
    block_out = mix_kernel(hidden, dense_out, gate_map, slots_out)
    gate_total, up_total = join_kernel(where, gate_parts, up_parts)
    (down_total,) = join_kernel(where, down_parts)
    second_total = after(second_total, block_out).astype(f32)
    first_parts = after(first_parts, block_out, gate_total)
    first_total = jnp.sum(first_parts.astype(f32), axis=0)
    gains = first_total[:, 3 * columns : 3 * columns + 2].T
    gains = gains + to_beside(gains)
    gains = gains + to_across(gains)
    return (
        block_out,
        grad_tokens,
        gains[0],
        first_total[:, :columns],
        first_total[:, columns : 2 * columns],
        first_total[:, 2 * columns : 3 * columns],
        first_total[:, 3 * columns + gain_width :][:, :columns].T,
        gains[1],
        second_total[:, :hidden_cols],
        second_total[:, hidden_cols : 2 * hidden_cols],
        second_total[:, 2 * hidden_cols :].T,
        gate_total,
        up_total,
        down_total.T,
    )


def gather_rows(rows_in):
    return lax.all_gather(rows_in, "tensor", axis=0, tiled=True)


def sum_rows(rows_in):
    return lax.psum_scatter(rows_in, "tensor", scatter_dimension=0, tiled=True)


def gather_attn_rows(rows_in):
    return lax.all_gather(rows_in, "tensor", axis=0, tiled=True)


def sum_attn_rows(rows_in):
    return lax.psum_scatter(rows_in, "tensor", scatter_dimension=0, tiled=True)


def general(
    tokens,
    cotangent,
    gain_attn,
    w_query,
    w_key,
    w_value,
    w_output,
    gain_ffn,
    dense_gate,
    dense_up,
    dense_down,
    expert_gate,
    expert_up,
    expert_down,
    routes,
    slot_order,
    gate_values,
    prefix_len,
):
    dp_count = lax.axis_size("dp")
    tensor_count = lax.axis_size("tensor")
    local_rows = tokens.shape[0]
    model_width = tokens.shape[1]
    length = local_rows * tensor_count
    splits = max(1, dp_count // EXPERTS)
    per_device = max(1, EXPERTS // dp_count)
    inputs = tokens.astype(jnp.float32)
    dense_all = (
        lax.all_gather(gain_attn, "dp", axis=0, tiled=True),
        lax.all_gather(w_query, "dp", axis=0, tiled=True),
        lax.all_gather(w_key, "dp", axis=0, tiled=True),
        lax.all_gather(w_value, "dp", axis=0, tiled=True),
        lax.all_gather(w_output, "dp", axis=1, tiled=True),
        lax.all_gather(gain_ffn, "dp", axis=0, tiled=True),
        lax.all_gather(dense_gate, "dp", axis=0, tiled=True),
        lax.all_gather(dense_up, "dp", axis=0, tiled=True),
        lax.all_gather(dense_down, "dp", axis=1, tiled=True),
    )
    (
        gain_one,
        query_full,
        key_full,
        value_full,
        output_full,
        gain_two,
        gate_full,
        up_full,
        down_full,
    ) = dense_all
    gain_one = gain_one.astype(jnp.float32)
    gain_two = gain_two.astype(jnp.float32)
    positions = jnp.arange(length, dtype=jnp.int32)
    prefix_value = prefix_len[0]
    normed_one = norm_rows(inputs, gain_one).astype(jnp.bfloat16)
    head_count = query_full.shape[1] // HEAD_DIM
    normed_all = gather_attn_rows(normed_one)
    queries = rotary(
        jnp.dot(normed_all, query_full, preferred_element_type=jnp.float32).reshape(
            length, head_count, HEAD_DIM
        ),
        positions,
        1.0,
    ).astype(jnp.bfloat16)
    keys_all = rotary(
        jnp.dot(normed_all, key_full, preferred_element_type=jnp.float32).reshape(
            length, head_count, HEAD_DIM
        ),
        positions,
        1.0,
    ).astype(jnp.bfloat16)
    values_all = (
        jnp.dot(normed_all, value_full, preferred_element_type=jnp.float32)
        .astype(jnp.bfloat16)
        .reshape(length, head_count, HEAD_DIM)
    )
    score_scale = 1.0 / math.sqrt(HEAD_DIM)
    block_rows = min(512, length)
    blocks = length // block_rows
    query_blocks = queries.reshape(blocks, block_rows, head_count, HEAD_DIM)
    position_blocks = positions.reshape(blocks, block_rows)

    def block_scores(block_query, block_pos):
        scores = (
            jnp.einsum("qhd,khd->hqk", block_query, keys_all, preferred_element_type=jnp.float32)
            * score_scale
        )
        visible = (positions[None, :] <= block_pos[:, None]) | (positions[None, :] < prefix_value)
        return jnp.where(visible[None], scores, -1e30)

    def attend(block_item):
        block_query, block_pos = block_item
        scores = block_scores(block_query, block_pos)
        row_top = jnp.max(scores, axis=-1, keepdims=True)
        exponent = jnp.exp(scores - row_top)
        row_total = jnp.sum(exponent, axis=-1, keepdims=True)
        softmaxed = exponent / row_total
        mixture = jnp.einsum(
            "hqk,khd->qhd",
            softmaxed.astype(jnp.bfloat16),
            values_all,
            preferred_element_type=jnp.float32,
        ).astype(jnp.bfloat16)
        return (mixture, (row_top + jnp.log(row_total))[..., 0])

    attended, log_totals = lax.map(attend, (query_blocks, position_blocks))
    attended = attended.reshape(length, head_count * HEAD_DIM)
    hidden = inputs + sum_attn_rows(
        jnp.dot(attended, output_full, preferred_element_type=jnp.float32)
    )
    normed_two = norm_rows(hidden, gain_two).astype(jnp.bfloat16)
    normed_two_all = gather_rows(normed_two)
    gate_pre = jnp.dot(normed_two_all, gate_full, preferred_element_type=jnp.float32)
    up_pre = jnp.dot(normed_two_all, up_full, preferred_element_type=jnp.float32)
    activated = (jax.nn.silu(gate_pre) * up_pre).astype(jnp.bfloat16)
    dense_out = sum_rows(jnp.dot(activated, down_full, preferred_element_type=jnp.float32))
    expert_ids = routes.reshape(-1)
    ranking = slot_order.reshape(-1)
    same_expert = expert_ids[:, None] == expert_ids[None, :]
    earlier = ranking[None, :] < ranking[:, None]
    placed = jnp.sum((same_expert & earlier).astype(jnp.int32), axis=1)
    usable = placed < CAP
    targets = jnp.where(usable, expert_ids * CAP + placed, -1)
    slot_ids = jnp.arange(EXPERTS * CAP, dtype=jnp.int32)
    pair_map = (slot_ids[:, None] == targets[None, :]).astype(jnp.float32)
    token_map = jnp.sum(pair_map.reshape(EXPERTS * CAP, local_rows, TOP), axis=2).astype(
        jnp.bfloat16
    )
    dispatched = jnp.dot(token_map, normed_two, preferred_element_type=jnp.float32).astype(
        jnp.bfloat16
    )
    outgoing = jnp.broadcast_to(
        dispatched.reshape(EXPERTS, 1, CAP, model_width), (EXPERTS, splits, CAP, model_width)
    ).reshape(dp_count, per_device, CAP, model_width)
    expert_all = (
        lax.all_gather(expert_gate, "tensor", axis=0, tiled=True),
        lax.all_gather(expert_up, "tensor", axis=0, tiled=True),
        lax.all_gather(expert_down, "tensor", axis=1, tiled=True),
    )
    piece_width = expert_all[0].shape[1] // per_device
    gate_pieces = expert_all[0].reshape(model_width, per_device, piece_width)
    up_pieces = expert_all[1].reshape(model_width, per_device, piece_width)
    down_pieces = expert_all[2].reshape(per_device, piece_width, model_width)
    received = lax.all_to_all(outgoing, "dp", split_axis=0, concat_axis=0, tiled=True)
    gate_local = jnp.einsum(
        "sjnd,djp->sjnp", received, gate_pieces, preferred_element_type=jnp.float32
    )
    up_local = jnp.einsum("sjnd,djp->sjnp", received, up_pieces, preferred_element_type=jnp.float32)
    active_local = (jax.nn.silu(gate_local) * up_local).astype(jnp.bfloat16)
    result_local = jnp.einsum(
        "sjnp,jpd->sjnd", active_local, down_pieces, preferred_element_type=jnp.float32
    ).astype(jnp.bfloat16)
    returned = lax.all_to_all(result_local, "dp", split_axis=0, concat_axis=0, tiled=True)
    returned, kept_in, gate_local, up_local = (returned, received, gate_local, up_local)
    expert_sums = jnp.sum(
        returned.reshape(EXPERTS, splits, CAP, model_width).astype(jnp.float32), axis=1
    ).reshape(EXPERTS * CAP, model_width)
    pick_index = jnp.where(usable, targets, 0)
    pair_weight = jnp.where(usable, gate_values.reshape(-1), 0.0)
    picked = jnp.take(expert_sums, pick_index, axis=0) * pair_weight[:, None]
    expert_mix = jnp.sum(picked.reshape(local_rows, TOP, model_width), axis=1)
    block_out = (hidden + dense_out + expert_mix).astype(jnp.bfloat16)
    dense_back = (
        lax.all_gather(gain_attn, "dp", axis=0, tiled=True),
        lax.all_gather(w_query, "dp", axis=0, tiled=True),
        lax.all_gather(w_key, "dp", axis=0, tiled=True),
        lax.all_gather(w_value, "dp", axis=0, tiled=True),
        lax.all_gather(w_output, "dp", axis=1, tiled=True),
        lax.all_gather(gain_ffn, "dp", axis=0, tiled=True),
        lax.all_gather(dense_gate, "dp", axis=0, tiled=True),
        lax.all_gather(dense_up, "dp", axis=0, tiled=True),
        lax.all_gather(dense_down, "dp", axis=1, tiled=True),
    )
    (
        gain_one,
        query_full,
        key_full,
        value_full,
        output_full,
        gain_two,
        gate_full,
        up_full,
        down_full,
    ) = dense_back
    gain_one = gain_one.astype(jnp.float32)
    gain_two = gain_two.astype(jnp.float32)
    grad_out = cotangent.astype(jnp.float32)
    cotangent_all = gather_rows(cotangent)
    grad_down = jnp.einsum(
        "lf,ld->fd", activated, cotangent_all, preferred_element_type=jnp.float32
    )
    grad_act = jnp.einsum("ld,fd->lf", cotangent_all, down_full, preferred_element_type=jnp.float32)
    grad_gate_pre, grad_up_pre = swiglu_back(grad_act, gate_pre, up_pre)
    grad_gate = jnp.einsum(
        "ld,lf->df", normed_two_all, grad_gate_pre, preferred_element_type=jnp.float32
    )
    grad_up = jnp.einsum(
        "ld,lf->df", normed_two_all, grad_up_pre, preferred_element_type=jnp.float32
    )
    dense_back_in = jnp.einsum(
        "lf,df->ld", grad_gate_pre, gate_full, preferred_element_type=jnp.float32
    ) + jnp.einsum("lf,df->ld", grad_up_pre, up_full, preferred_element_type=jnp.float32)
    slot_gate = jnp.dot(pair_map, gate_values.reshape(-1), precision=lax.Precision.HIGHEST)
    slot_cotangent = jnp.dot(token_map, cotangent, preferred_element_type=jnp.float32)
    grad_slots = (slot_cotangent * slot_gate[:, None]).astype(jnp.bfloat16)
    grad_outgoing = jnp.broadcast_to(
        grad_slots.reshape(EXPERTS, 1, CAP, model_width), (EXPERTS, splits, CAP, model_width)
    ).reshape(dp_count, per_device, CAP, model_width)
    grad_received = lax.all_to_all(grad_outgoing, "dp", split_axis=0, concat_axis=0, tiled=True)
    active_local = (jax.nn.silu(gate_local) * up_local).astype(jnp.bfloat16)
    grad_down_expert = jnp.einsum(
        "sjnp,sjnd->jpd", active_local, grad_received, preferred_element_type=jnp.float32
    ).reshape(per_device * piece_width, model_width)
    grad_act_expert = jnp.einsum(
        "sjnd,jpd->sjnp", grad_received, down_pieces, preferred_element_type=jnp.float32
    )
    grad_gate_local, grad_up_local = swiglu_back(grad_act_expert, gate_local, up_local)
    grad_gate_expert = jnp.einsum(
        "sjnd,sjnp->djp", kept_in, grad_gate_local, preferred_element_type=jnp.float32
    ).reshape(model_width, per_device * piece_width)
    grad_up_expert = jnp.einsum(
        "sjnd,sjnp->djp", kept_in, grad_up_local, preferred_element_type=jnp.float32
    ).reshape(model_width, per_device * piece_width)
    grad_in_expert = (
        jnp.einsum(
            "sjnp,djp->sjnd", grad_gate_local, gate_pieces, preferred_element_type=jnp.float32
        )
        + jnp.einsum("sjnp,djp->sjnd", grad_up_local, up_pieces, preferred_element_type=jnp.float32)
    ).astype(jnp.bfloat16)
    grad_back = lax.all_to_all(grad_in_expert, "dp", split_axis=0, concat_axis=0, tiled=True)
    grad_slots_in = jnp.sum(
        grad_back.reshape(EXPERTS, splits, CAP, model_width).astype(jnp.float32), axis=1
    ).reshape(EXPERTS * CAP, model_width)
    grad_pairs = jnp.where(usable[:, None], jnp.take(grad_slots_in, pick_index, axis=0), 0.0)
    expert_back = jnp.sum(grad_pairs.reshape(local_rows, TOP, model_width), axis=1)
    grad_normed_two = sum_rows(dense_back_in) + expert_back
    grad_hidden_norm, grad_gain_two_part = norm_back(hidden, gain_two, grad_normed_two)
    grad_hidden = grad_out + grad_hidden_norm
    query_use, key_use, value_use, output_use = (query_full, key_full, value_full, output_full)
    grad_attn_in = gather_attn_rows(grad_hidden.astype(jnp.bfloat16))
    grad_output_w = jnp.einsum(
        "lc,ld->cd", attended, grad_attn_in, preferred_element_type=jnp.float32
    )
    grad_attended = (
        jnp.einsum("ld,cd->lc", grad_attn_in, output_use, preferred_element_type=jnp.float32)
        .astype(jnp.bfloat16)
        .reshape(blocks, block_rows, head_count, HEAD_DIM)
    )

    def attend_back(running, block_item):
        grad_keys, grad_values = running
        block_query, block_pos, block_grad, block_total = block_item
        scores = block_scores(block_query, block_pos)
        softmaxed = jnp.exp(scores - block_total[..., None])
        grad_soft = jnp.einsum(
            "qhd,khd->hqk", block_grad, values_all, preferred_element_type=jnp.float32
        )
        inner_sum = jnp.sum(softmaxed * grad_soft, axis=-1, keepdims=True)
        grad_scores = (softmaxed * (grad_soft - inner_sum)).astype(jnp.bfloat16)
        grad_block = (
            jnp.einsum("hqk,khd->qhd", grad_scores, keys_all, preferred_element_type=jnp.float32)
            * score_scale
        )
        grad_keys = (
            grad_keys
            + jnp.einsum(
                "hqk,qhd->khd", grad_scores, block_query, preferred_element_type=jnp.float32
            )
            * score_scale
        )
        grad_values = grad_values + jnp.einsum(
            "hqk,qhd->khd",
            softmaxed.astype(jnp.bfloat16),
            block_grad,
            preferred_element_type=jnp.float32,
        )
        return ((grad_keys, grad_values), grad_block)

    zero_start = (
        jnp.zeros((length, head_count, HEAD_DIM), jnp.float32),
        jnp.zeros((length, head_count, HEAD_DIM), jnp.float32),
    )
    (grad_keys, grad_values), grad_queries = lax.scan(
        attend_back, zero_start, (query_blocks, position_blocks, grad_attended, log_totals)
    )
    grad_queries = (
        rotary(grad_queries.reshape(length, head_count, HEAD_DIM), positions, -1.0)
        .astype(jnp.bfloat16)
        .reshape(length, head_count * HEAD_DIM)
    )
    grad_keys = (
        rotary(grad_keys, positions, -1.0)
        .astype(jnp.bfloat16)
        .reshape(length, head_count * HEAD_DIM)
    )
    grad_values = grad_values.astype(jnp.bfloat16).reshape(length, head_count * HEAD_DIM)
    grad_query_w = jnp.einsum(
        "ld,lc->dc", normed_all, grad_queries, preferred_element_type=jnp.float32
    )
    grad_key_w = jnp.einsum("ld,lc->dc", normed_all, grad_keys, preferred_element_type=jnp.float32)
    grad_value_w = jnp.einsum(
        "ld,lc->dc", normed_all, grad_values, preferred_element_type=jnp.float32
    )
    normed_back_part = (
        jnp.einsum("lc,dc->ld", grad_queries, query_use, preferred_element_type=jnp.float32)
        + jnp.einsum("lc,dc->ld", grad_keys, key_use, preferred_element_type=jnp.float32)
        + jnp.einsum("lc,dc->ld", grad_values, value_use, preferred_element_type=jnp.float32)
    )
    grad_normed_one = sum_attn_rows(normed_back_part)
    grad_input_norm, grad_gain_one_part = norm_back(inputs, gain_one, grad_normed_one)
    grad_tokens = grad_hidden + grad_input_norm
    dense_grads = (
        lax.psum_scatter(grad_gain_one_part, "dp", scatter_dimension=0, tiled=True),
        lax.psum_scatter(grad_query_w, "dp", scatter_dimension=0, tiled=True),
        lax.psum_scatter(grad_key_w, "dp", scatter_dimension=0, tiled=True),
        lax.psum_scatter(grad_value_w, "dp", scatter_dimension=0, tiled=True),
        lax.psum_scatter(grad_output_w, "dp", scatter_dimension=1, tiled=True),
        lax.psum_scatter(grad_gain_two_part, "dp", scatter_dimension=0, tiled=True),
        lax.psum_scatter(grad_gate, "dp", scatter_dimension=0, tiled=True),
        lax.psum_scatter(grad_up, "dp", scatter_dimension=0, tiled=True),
        lax.psum_scatter(grad_down, "dp", scatter_dimension=1, tiled=True),
    )
    gain_totals = lax.psum((dense_grads[0], dense_grads[5]), "tensor")
    expert_grads = (
        lax.psum_scatter(
            grad_gate_expert.astype(jnp.bfloat16), "tensor", scatter_dimension=0, tiled=True
        ).astype(jnp.float32),
        lax.psum_scatter(
            grad_up_expert.astype(jnp.bfloat16), "tensor", scatter_dimension=0, tiled=True
        ).astype(jnp.float32),
        lax.psum_scatter(
            grad_down_expert.astype(jnp.bfloat16), "tensor", scatter_dimension=1, tiled=True
        ).astype(jnp.float32),
    )
    return (
        block_out,
        grad_tokens,
        gain_totals[0],
        dense_grads[1],
        dense_grads[2],
        dense_grads[3],
        dense_grads[4],
        gain_totals[1],
        dense_grads[6],
        dense_grads[7],
        dense_grads[8],
        expert_grads[0],
        expert_grads[1],
        expert_grads[2],
    )


def solution(mesh):
    sizes = mesh.shape
    in_pairs = sizes["tensor"] == 4 and sizes["dp"] * 2 == EXPERTS
    local = paired if in_pairs else general
    return jax.shard_map(
        local,
        mesh=mesh,
        in_specs=(
            P(("dp", "tensor"), None),
            P(("dp", "tensor"), None),
            P("dp"),
            P("dp", "tensor"),
            P("dp", "tensor"),
            P("dp", "tensor"),
            P("tensor", "dp"),
            P("dp"),
            P("dp", "tensor"),
            P("dp", "tensor"),
            P("tensor", "dp"),
            P("tensor", "dp"),
            P("tensor", "dp"),
            P("dp", "tensor"),
            P(("dp", "tensor"), None),
            P(("dp", "tensor"), None),
            P(("dp", "tensor"), None),
            P("dp"),
        ),
        out_specs=(
            P(("dp", "tensor"), None),
            P(("dp", "tensor"), None),
            P("dp"),
            P("dp", "tensor"),
            P("dp", "tensor"),
            P("dp", "tensor"),
            P("tensor", "dp"),
            P("dp"),
            P("dp", "tensor"),
            P("dp", "tensor"),
            P("tensor", "dp"),
            P("tensor", "dp"),
            P("tensor", "dp"),
            P("dp", "tensor"),
        ),
        check_vma=False,
    )
```

```python
import math

import jax
import jax.numpy as jnp
import numpy as np
from jax import lax
from jax.experimental import pallas as pl
from jax.experimental.pallas import tpu as pltpu
from jax.sharding import PartitionSpec as P

HEAD_DIM = 64
EXPERTS = 16
TOP = 2
CAP = 40


epsilon = 1e-06


def norm_rows(rows_in, gain_row):
    return (
        rows_in
        * lax.rsqrt(jnp.mean(rows_in * rows_in, axis=-1, keepdims=True) + epsilon)
        * gain_row
    )


def norm_back(rows_in, gain_row, grad_out):
    inverse = lax.rsqrt(jnp.mean(rows_in * rows_in, axis=-1, keepdims=True) + epsilon)
    scaled = grad_out * gain_row
    grad_rows = inverse * scaled - rows_in * inverse**3 * jnp.mean(
        scaled * rows_in, axis=-1, keepdims=True
    )
    grad_gain = jnp.sum(grad_out * rows_in * inverse, axis=0)
    return (grad_rows, grad_gain)


def rotary(values, positions, direction):
    half_width = values.shape[-1] // 2
    frequency = jnp.power(10000.0, -jnp.arange(half_width).astype(jnp.float32) / half_width)
    angles = positions[:, None].astype(jnp.float32) * frequency[None, :]
    cosine = jnp.cos(angles)[:, None, :]
    sine_part = direction * jnp.sin(angles)[:, None, :]
    first_half = values[..., :half_width]
    second_half = values[..., half_width:]
    return jnp.concatenate(
        [
            first_half * cosine - second_half * sine_part,
            second_half * cosine + first_half * sine_part,
        ],
        axis=-1,
    )


def swiglu_back(grad_act, gate_pre, up_pre):
    sigmoid = jax.nn.sigmoid(gate_pre)
    silu_value = gate_pre * sigmoid
    grad_gate = grad_act * up_pre * sigmoid * (1.0 + gate_pre * (1.0 - sigmoid))
    grad_up = grad_act * silu_value
    return (grad_gate.astype(jnp.bfloat16), grad_up.astype(jnp.bfloat16))


def to_across(values):
    return lax.ppermute(values, "tensor", [(i, i ^ 2) for i in range(4)])


def to_beside(values):
    return lax.ppermute(values, "tensor", [(i, i ^ 1) for i in range(4)])


def gather_blocks(rows_in):
    near = jnp.stack([rows_in, to_across(rows_in)])
    return jnp.concatenate([near, to_beside(near)]).reshape(-1, rows_in.shape[-1])


def sum_across(own, near, far, *before):
    beside = to_beside(far)
    beside = [part.astype(jnp.float32) for part in after((beside[0], beside[1]))]
    sent = (near + beside[1]).astype(jnp.bfloat16)
    return own + beside[0] + to_across(after(sent, *before) if before else sent).astype(jnp.float32)


def after(value, *before):
    if not before:
        return lax.optimization_barrier(value)
    return lax.optimization_barrier((value,) + before)[0]


def sum_blocks(partial):
    blocks = partial.reshape(4, -1, partial.shape[-1])
    near = blocks[:2] + to_beside(blocks[2:].astype(jnp.bfloat16)).astype(jnp.float32)
    return near[0] + to_across(near[1].astype(jnp.bfloat16)).astype(jnp.float32)


def along(values, axis, k):
    return lax.ppermute(values, axis, [(i, i ^ k) for i in range(lax.axis_size(axis))])


def gather_line(rows_in):
    return [along(rows_in, "dp", k) if k else rows_in for k in range(0, lax.axis_size("dp"), 2)]


def gather_pairs(line):
    return [part for own in line for part in (own, along(own, "dp", 1))]


def dot(left, right, dims):
    return lax.dot_general(left, right, (dims, ((), ())), preferred_element_type=jnp.float32)


NN, NT, TN = ((1,), (0,)), ((1,), (1,)), ((0,), (0,))
ORDER = (0, 2, 1, 3)
VMEM = pl.BlockSpec(memory_space=pltpu.VMEM)
SMEM = pl.BlockSpec(memory_space=pltpu.SMEM)
HBM = pl.BlockSpec(memory_space=pltpu.HBM)
NO_COST = pl.CostEstimate(flops=0, bytes_accessed=0, transcendentals=0)


def angle_tables(length):
    half = HEAD_DIM // 2
    lane = np.arange(2 * HEAD_DIM)
    frequency = np.power(10000.0, -(lane % half).astype(np.float64) / half)
    angles = np.arange(length)[:, None] * frequency[None, :]
    sign = np.where(lane % HEAD_DIM < half, -1.0, 1.0)
    return np.cos(angles).astype(np.float32), (np.sin(angles) * sign).astype(np.float32)


def turn(values, cosine, sine):
    width = values.shape[1]
    half = HEAD_DIM // 2
    lane = lax.broadcasted_iota(jnp.int32, values.shape, 1)
    swapped = jnp.where(
        lane % HEAD_DIM < half,
        pltpu.roll(values, width - half, 1),
        pltpu.roll(values, half, 1),
    )
    repeats = width // cosine.shape[1]
    return values * jnp.concatenate([cosine] * repeats, axis=1) + swapped * jnp.concatenate(
        [sine] * repeats, axis=1
    )


def block_at(place, i):
    return place ^ ((i >> 1) | ((i & 1) << 1))


def pack_views(own, near, far, n):
    return own, near.at[n], far.at[0, n], far.at[1, n]


def seen(place, prefix, i, j, rows):
    query_block, key_block = block_at(place, i), block_at(place, j)
    return (key_block <= query_block) | (key_block * rows < prefix)


def mask_of(place, prefix, i, j, rows):
    key = block_at(place, j) * rows + lax.broadcasted_iota(jnp.int32, (rows, rows), 0)
    query = block_at(place, i) * rows + lax.broadcasted_iota(jnp.int32, (rows, rows), 1)
    return key <= jnp.maximum(query, prefix - 1)


def attend_kernel(where, blocks_in, parts, length, columns):
    rows, width = blocks_in[0].shape
    shard, lanes = parts[0].shape
    blocks = length // rows
    heads = columns // HEAD_DIM
    count = len(parts)
    gain_at = 3 * columns
    output_at = 3 * columns + 64
    bf16, f32 = jnp.bfloat16, jnp.float32
    cosine, sine = angle_tables(length)

    def body(*refs):
        spot, token_refs = refs[0], pack_views(*refs[1:4], 0)
        part_refs = refs[4 : 4 + count]
        cos_ref, sin_ref = refs[4 + count : 6 + count]
        (
            normed_ref,
            weight_ref,
            gain_ref,
            query_ref,
            query_t_ref,
            key_ref,
            value_ref,
            mixed_ref,
            mixed_t_ref,
            log_ref,
            sum_own_ref,
            sum_near_ref,
            sum_far_ref,
        ) = refs[6 + count : 19 + count]
        value_t_ref, score_ref, top_ref, total_ref, mix_ref, *keep, sems = refs[19 + count :]
        outward = [
            pltpu.make_async_copy(source, target, sems.at[n])
            for n, (source, target) in enumerate(
                zip(
                    keep,
                    (
                        normed_ref,
                        weight_ref,
                        query_ref,
                        query_t_ref,
                        key_ref,
                        value_ref,
                        mixed_ref,
                        mixed_t_ref,
                    ),
                )
            )
        ]
        (
            normed_ref,
            weight_ref,
            query_ref,
            query_t_ref,
            key_ref,
            value_ref,
            mixed_ref,
            mixed_t_ref,
        ) = keep
        place, dp_place, prefix = spot[0], spot[1], spot[2]
        for k in range(count):
            start = pl.multiple_of((dp_place ^ k) * shard, 16)
            weight_ref[pl.ds(start, shard), :] = part_refs[k][...]
        gain_tile = weight_ref[:, gain_at // 128 * 128 : gain_at // 128 * 128 + 128].astype(f32)
        gain_ref[...] = gain_tile.T[gain_at % 128 : gain_at % 128 + 8, :]
        gain = gain_ref[0:1, :]
        for i in range(blocks):
            tokens = token_refs[i][...].astype(f32)
            inverse = lax.rsqrt(jnp.mean(tokens * tokens, axis=-1, keepdims=True) + epsilon)
            normed = (tokens * inverse * gain).astype(bf16)
            span = pl.ds(i * rows, rows)
            normed_ref[span, :] = normed
            product = dot(normed, weight_ref[:, : 3 * columns], NN)
            spot_rows = pl.ds(pl.multiple_of(block_at(place, i) * rows, 8), rows)
            turned = turn(product[:, : 2 * columns], cos_ref[spot_rows, :], sin_ref[spot_rows, :])
            query = turned[:, :columns] * (1.0 / math.sqrt(HEAD_DIM))
            key = turned[:, columns:]
            value = product[:, 2 * columns :]
            query_t = query.T
            value_t = value.T
            for h in range(heads):
                cut = slice(h * HEAD_DIM, (h + 1) * HEAD_DIM)
                query_ref[h, span, :] = query[:, cut].astype(bf16)
                query_t_ref[h, :, span] = query_t[cut, :].astype(bf16)
                key_ref[h, span, :] = key[:, cut].astype(bf16)
                value_ref[h, span, :] = value[:, cut].astype(bf16)
                value_t_ref[h, :, span] = value_t[cut, :].astype(bf16)

        for copy in outward[:6]:
            copy.start()

        def query_block(i, carry):
            here = pl.ds(pl.multiple_of(i * rows, 128), rows)
            top_ref[...] = jnp.full(top_ref.shape, -1e30, f32)
            total_ref[...] = jnp.zeros(total_ref.shape, f32)
            mix_ref[...] = jnp.zeros(mix_ref.shape, f32)

            def scores(j, carry):
                @pl.when(seen(place, prefix, i, j, rows))
                def _():
                    there = pl.ds(pl.multiple_of(j * rows, 128), rows)
                    visible = mask_of(place, prefix, i, j, rows)
                    for h in range(heads):
                        score = dot(key_ref[h, there, :], query_t_ref[h, :, here], NN)
                        score = jnp.where(visible, score, -1e30)
                        score_ref[h, there, :] = score
                        top_ref[h : h + 1, :] = jnp.maximum(
                            top_ref[h : h + 1, :], jnp.max(score, axis=0, keepdims=True)
                        )

                return carry

            def mixing(j, carry):
                @pl.when(seen(place, prefix, i, j, rows))
                def _():
                    there = pl.ds(pl.multiple_of(j * rows, 128), rows)
                    for h in range(heads):
                        power = jnp.exp(score_ref[h, there, :] - top_ref[h : h + 1, :])
                        total_ref[h : h + 1, :] += jnp.sum(power, axis=0, keepdims=True)
                        mix_ref[h] += dot(value_t_ref[h, :, there], power.astype(bf16), NN)

                return carry

            lax.fori_loop(0, blocks, scores, 0)
            lax.fori_loop(0, blocks, mixing, 0)
            log_ref[:, here] = top_ref[...] + jnp.log(jnp.maximum(total_ref[...], 1e-30))
            mixed_t = jnp.concatenate(
                [mix_ref[h] * (1.0 / total_ref[h : h + 1, :]) for h in range(heads)], axis=0
            )
            for h in range(heads):
                mixed_t_ref[h, :, here] = mixed_t[h * HEAD_DIM : (h + 1) * HEAD_DIM, :].astype(bf16)
            mixed = mixed_t.T.astype(bf16)
            mixed_ref[here, :] = mixed
            partial = dot(mixed, weight_ref[:, output_at : output_at + columns], NT)

            @pl.when(i == 0)
            def _():
                sum_own_ref[...] = partial

            @pl.when(i == 1)
            def _():
                sum_near_ref[...] = partial

            @pl.when(i >= 2)
            def _():
                sum_far_ref[i - 2] = partial.astype(bf16)

            return carry

        lax.fori_loop(0, blocks, query_block, 0)
        for copy in outward[6:]:
            copy.start()
        for copy in outward:
            copy.wait()

    per_head = (heads, length, HEAD_DIM)
    per_head_t = (heads, HEAD_DIM, length)
    out_shape = [
        jax.ShapeDtypeStruct(shape, kind)
        for shape, kind in (
            ((length, width), bf16),
            ((count * shard, lanes), bf16),
            ((8, width), f32),
            (per_head, bf16),
            (per_head_t, bf16),
            (per_head, bf16),
            (per_head, bf16),
            ((length, columns), bf16),
            (per_head_t, bf16),
            ((8, length), f32),
            ((rows, width), f32),
            ((rows, width), f32),
            ((2, rows, width), bf16),
        )
    ]
    return pl.pallas_call(
        body,
        out_shape=out_shape,
        in_specs=[SMEM] + [VMEM] * (5 + count),
        out_specs=[HBM] * 2 + [VMEM] + [HBM] * 6 + [VMEM] * 4,
        scratch_shapes=[
            pltpu.VMEM(per_head_t, bf16),
            pltpu.VMEM((heads, length, rows), f32),
            pltpu.VMEM((8, rows), f32),
            pltpu.VMEM((8, rows), f32),
            pltpu.VMEM((heads, HEAD_DIM, rows), f32),
        ]
        + [pltpu.VMEM(out_shape[n].shape, bf16) for n in (0, 1, 3, 4, 5, 6, 7, 8)]
        + [pltpu.SemaphoreType.DMA((8,))],
        compiler_params=pltpu.CompilerParams(vmem_limit_bytes=60 * 2**20),
        cost_estimate=NO_COST,
    )(where, *blocks_in, *parts, cosine, sine)


def attend_back_kernel(
    where, blocks_in, grads_in, saved, gain_two, length, columns
):
    normed, weight, query, query_t, key, value, mixed, mixed_t, log_total = saved
    rows, width = blocks_in[0].shape
    lanes = weight.shape[1]
    blocks = length // rows
    heads = columns // HEAD_DIM
    output_at = 3 * columns + 64
    bf16, f32 = jnp.bfloat16, jnp.float32
    cosine, sine = angle_tables(length)

    def body(*refs):
        (
            spot,
            own_ref,
            near_ref,
            far_ref,
            grad_own_ref,
            grad_near_ref,
            grad_far_ref,
            normed_ref,
            weight_ref,
            query_ref,
            query_t_ref,
            key_ref,
            value_ref,
            mixed_ref,
            mixed_t_ref,
            log_ref,
            gain_two_ref,
            cos_ref,
            sin_ref,
            first_ref,
            back_own_ref,
            back_near_ref,
            back_far_ref,
            grad_in,
            grad_mix,
            grad_mix_t,
            inner,
            key_t,
            grad_query_t,
            grad_key,
            grad_value,
            grad_product,
            *keep,
            sems,
        ) = refs
        place, prefix = spot[0], spot[2]
        inward = [
            pltpu.make_async_copy(source, target, sems.at[n])
            for n, (source, target) in enumerate(
                zip(
                    (
                        weight_ref,
                        mixed_t_ref,
                        key_ref,
                        query_t_ref,
                        query_ref,
                        value_ref,
                        own_ref,
                        near_ref.at[0],
                        far_ref.at[0, 0],
                        far_ref.at[1, 0],
                        normed_ref,
                        mixed_ref,
                        cos_ref,
                        sin_ref,
                    ),
                    keep,
                )
            )
        ]
        for copy in inward:
            copy.start()
        (
            weight_ref,
            mixed_t_ref,
            key_ref,
            query_t_ref,
            query_ref,
            value_ref,
            *token_refs,
            normed_ref,
            mixed_ref,
            cos_ref,
            sin_ref,
        ) = keep
        grad_refs = (grad_own_ref, grad_near_ref, grad_far_ref.at[0], grad_far_ref.at[1])
        grad_key[...] = jnp.zeros(grad_key.shape, f32)
        grad_value[...] = jnp.zeros(grad_value.shape, f32)
        grad_query_t[...] = jnp.zeros(grad_query_t.shape, f32)
        for copy in inward[:3]:
            copy.wait()
        for h in range(heads):
            key_t[h] = key_ref[h].astype(f32).T.astype(bf16)
        for i in range(blocks):
            span = pl.ds(i * rows, rows)
            grad = grad_refs[i][...]
            grad_in[span, :] = grad
            mix = dot(grad, weight_ref[:, output_at : output_at + columns], NN)
            mix_t = mix.T
            for h in range(heads):
                cut = slice(h * HEAD_DIM, (h + 1) * HEAD_DIM)
                low = mix_t[cut, :].astype(bf16)
                grad_mix[h, span, :] = mix[:, cut].astype(bf16)
                grad_mix_t[h, :, span] = low
                inner[h : h + 1, span] = jnp.sum(
                    low.astype(f32) * mixed_t_ref[h, :, span].astype(f32), axis=0, keepdims=True
                )

        for copy in inward[3:6]:
            copy.wait()

        def pair(step, carry):
            i, j = step // blocks, step % blocks

            @pl.when(seen(place, prefix, i, j, rows))
            def _():
                here = pl.ds(pl.multiple_of(i * rows, 128), rows)
                there = pl.ds(pl.multiple_of(j * rows, 128), rows)
                visible = mask_of(place, prefix, i, j, rows)
                for h in range(heads):
                    score = dot(key_ref[h, there, :], query_t_ref[h, :, here], NN)
                    weigh = jnp.where(visible, jnp.exp(score - log_ref[h : h + 1, here]), 0.0)
                    soft = dot(value_ref[h, there, :], grad_mix_t[h, :, here], NN)
                    low = (weigh * (soft - inner[h : h + 1, here])).astype(bf16)
                    grad_value[h, there, :] += dot(weigh.astype(bf16), grad_mix[h, here, :], NN)
                    grad_key[h, there, :] += dot(low, query_ref[h, here, :], NN)
                    grad_query_t[h, :, here] += dot(key_t[h, :, there], low, NN)

            return carry

        lax.fori_loop(0, blocks * blocks, pair, 0)
        for copy in inward[6:]:
            copy.wait()
        gain = jnp.zeros((1, width), f32)
        for i in range(blocks):
            span = pl.ds(i * rows, rows)
            spot_rows = pl.ds(pl.multiple_of(block_at(place, i) * rows, 8), rows)
            turned = jnp.concatenate(
                [grad_query_t[h, :, span].T * (1.0 / math.sqrt(HEAD_DIM)) for h in range(heads)]
                + [grad_key[h, span, :] for h in range(heads)],
                axis=1,
            )
            turned = turn(turned, cos_ref[spot_rows, :], -sin_ref[spot_rows, :])
            grads = jnp.concatenate(
                [turned] + [grad_value[h, span, :] for h in range(heads)], axis=1
            ).astype(bf16)
            grad_product[span, :] = grads
            back = dot(grads, weight_ref[:, : 3 * columns], NT)
            tokens = token_refs[i][...].astype(f32)
            inverse = lax.rsqrt(jnp.mean(tokens * tokens, axis=-1, keepdims=True) + epsilon)
            gain += jnp.sum(back * tokens * inverse, axis=0, keepdims=True)
            if i < 2:
                (back_own_ref, back_near_ref)[i][...] = back
            else:
                back_far_ref[i - 2] = back.astype(bf16)
        gains = jnp.concatenate([gain, gain_two_ref[...], jnp.zeros((62, width), f32)], axis=0)
        first_ref[:, 3 * columns : output_at] = gains.T.astype(bf16)
        first_ref[:, : 3 * columns] = dot(normed_ref[...], grad_product[...], TN).astype(bf16)
        first_ref[:, output_at : output_at + columns] = dot(
            grad_in[...], mixed_ref[...], TN
        ).astype(bf16)
        if output_at + columns < lanes:
            first_ref[:, output_at + columns :] = jnp.zeros(
                (width, lanes - output_at - columns), bf16
            )

    per_head = (heads, length, HEAD_DIM)
    per_head_t = (heads, HEAD_DIM, length)
    out_shape = [
        jax.ShapeDtypeStruct(shape, kind)
        for shape, kind in (
            ((width, lanes), bf16),
            ((rows, width), f32),
            ((rows, width), f32),
            ((2, rows, width), bf16),
        )
    ]
    return pl.pallas_call(
        body,
        out_shape=out_shape,
        in_specs=[SMEM] + [HBM] * 3 + [VMEM] * 3 + [HBM] * 8 + [VMEM] * 2 + [HBM] * 2,
        out_specs=[VMEM] * len(out_shape),
        scratch_shapes=[
            pltpu.VMEM((length, width), bf16),
            pltpu.VMEM(per_head, bf16),
            pltpu.VMEM(per_head_t, bf16),
            pltpu.VMEM((8, length), f32),
            pltpu.VMEM(per_head_t, bf16),
            pltpu.VMEM(per_head_t, f32),
            pltpu.VMEM(per_head, f32),
            pltpu.VMEM(per_head, f32),
            pltpu.VMEM((length, 3 * columns), bf16),
        ]
        + [
            pltpu.VMEM(array.shape, array.dtype)
            for array in (
                weight,
                mixed_t,
                key,
                query_t,
                query,
                value,
                *[blocks_in[0]] * 4,
                normed,
                mixed,
                cosine,
                sine,
            )
        ]
        + [pltpu.SemaphoreType.DMA((14,))],
        compiler_params=pltpu.CompilerParams(vmem_limit_bytes=52 * 2**20),
        cost_estimate=NO_COST,
    )(where, *blocks_in, *grads_in, *saved, gain_two, cosine, sine)


def gated(gate_pre, up_pre):
    sigmoid = 1.0 / (1.0 + jnp.exp(-gate_pre))
    return gate_pre * sigmoid * up_pre


def gated_back(grad, gate_pre, up_pre):
    sigmoid = 1.0 / (1.0 + jnp.exp(-gate_pre))
    silu = gate_pre * sigmoid
    grad_gate = grad * up_pre * (sigmoid + silu * (1.0 - sigmoid))
    return silu * up_pre, grad_gate, grad * silu


def call(body, out, *args, scratch=(), scalars=0, limit=28):
    bf16_kinds = [jax.ShapeDtypeStruct(shape, kind) for shape, kind in out]
    return pl.pallas_call(
        body,
        out_shape=bf16_kinds,
        in_specs=[SMEM] * scalars + [VMEM] * (len(args) - scalars),
        out_specs=[VMEM] * len(out),
        scratch_shapes=[pltpu.VMEM(shape, kind) for shape, kind in scratch],
        compiler_params=pltpu.CompilerParams(vmem_limit_bytes=limit * 2**20),
        cost_estimate=NO_COST,
    )(*args)


def join_rows(spot, refs, target):
    rows = refs[0].shape[0]
    for k, ref in enumerate(refs):
        target[pl.ds(pl.multiple_of((spot ^ k) * rows, 16), rows), :] = ref[...]


def expert_kernel(where, rows, grads, pair_in, down_in):
    part = down_in[0].shape[1]
    count, width = rows[0].shape
    units = down_in[0].shape[2]
    step = count // 2
    bf16, f32 = jnp.bfloat16, jnp.float32

    def body(*refs):
        spot, rows_refs, grad_refs = refs[0], refs[1:3], refs[3:5]
        pair_refs, down_refs = refs[5:7], refs[7:9]
        down_ref, own_ref, other_ref = refs[9:12]
        act_refs, back_gate_refs, back_up_refs = refs[12:14], refs[14:16], refs[16:18]
        gate_ref, up_ref = refs[18:]
        for target, views in (
            (gate_ref, [ref.at[n, 0] for n in (0, 1) for ref in pair_refs]),
            (up_ref, [ref.at[n, 1] for n in (0, 1) for ref in pair_refs]),
            (down_ref, [ref.at[n] for n in (0, 1) for ref in down_refs]),
        ):
            join_rows(spot[0], views, target)
        for half in (1, 0):

            def chunk(i, carry, half=half):
                span = pl.ds(pl.multiple_of(i * step, 16), step)
                row = rows_refs[half][span, :]
                gate_pre = dot(row, gate_ref[...], NN)
                up_pre = dot(row, up_ref[...], NN)
                grad = dot(grad_refs[half][span, :], down_ref[...], NN)
                act, grad_gate, grad_up = gated_back(grad, gate_pre, up_pre)
                grad_gate, grad_up = grad_gate.astype(bf16), grad_up.astype(bf16)
                act_refs[half][span, :] = act.astype(bf16)
                back_gate_refs[half][span, :] = grad_gate
                back_up_refs[half][span, :] = grad_up
                back = dot(grad_gate, gate_ref[...], NT) + dot(grad_up, up_ref[...], NT)
                if half:
                    other_ref[span, :] = back.astype(bf16)
                else:
                    own_ref[span, :] = back
                return carry

            lax.fori_loop(0, 2, chunk, 0)

    weight = ((4 * part, units), bf16)
    saved = ((count, units), bf16)
    outs = call(
        body,
        [weight] + [((count, width), f32), ((count, width), bf16)] + [saved] * 6,
        where,
        *rows,
        *grads,
        *pair_in,
        *down_in,
        scratch=[weight] * 2,
        scalars=1,
        limit=52,
    )
    return outs[0], outs[1], outs[2], outs[3:5], outs[5:7], outs[7:9]


def expert_grad_kernel(rows, grads, acts, back_gates, back_ups, down):
    count, width = rows[0].shape
    units = acts[0].shape[1]
    step = 256
    bf16, f32 = jnp.bfloat16, jnp.float32

    def body(*refs):
        rows_refs, grad_refs, act_refs, gate_refs, up_refs = (refs[2 * n : 2 * n + 2] for n in range(5))
        down_ref, own_ref, other_ref, gate_out, up_out, down_out = refs[10:16]

        def chunk(i, carry):
            span = pl.ds(pl.multiple_of(i * step, 128), step)
            for left, right, target in (
                (rows_refs, gate_refs, gate_out),
                (rows_refs, up_refs, up_out),
                (grad_refs, act_refs, down_out),
            ):
                target[:, span] = (
                    dot(left[0][...], right[0][:, span], TN)
                    + dot(left[1][...], right[1][:, span], TN)
                ).astype(bf16)
            return carry

        lax.fori_loop(0, units // step, chunk, 0)
        own_ref[...] = dot(act_refs[0][...], down_ref[...], NT)
        other_ref[...] = dot(act_refs[1][...], down_ref[...], NT).astype(bf16)

    return call(
        body,
        [
            ((count, width), f32),
            ((count, width), bf16),
            *[((width, units), bf16)] * 3,
        ],
        *rows,
        *grads,
        *acts,
        *back_gates,
        *back_ups,
        down,
        limit=52,
    )


def dense_kernel(normed, pack, weight):
    rows, width = normed[0].shape
    units = weight.shape[1] // 3
    bf16, f32 = jnp.bfloat16, jnp.float32

    def body(*refs):
        normed_refs = (refs[0], refs[1], refs[2].at[0], refs[2].at[1])
        grad_refs = pack_views(*refs[3:6], 1)
        weight, back_own, back_near, back_far, out_own, out_near, out_far, total_ref = refs[6:14]
        normed_all, grad_all, wide, act_all = refs[14:]
        gate, up, down = (slice(n * units, (n + 1) * units) for n in range(3))
        for i in range(4):
            row = normed_refs[i][...]
            grad_row = grad_refs[i][...]
            span = slice(i * rows, (i + 1) * rows)
            normed_all[span, :] = row
            grad_all[span, :] = grad_row
            gate_pre = dot(row, weight[:, gate], NN)
            up_pre = dot(row, weight[:, up], NN)
            grad = dot(grad_row, weight[:, down], NN)
            act, grad_gate, grad_up = gated_back(grad, gate_pre, up_pre)
            act = act.astype(bf16)
            act_all[span, :] = act
            wide[span, :units] = grad_gate.astype(bf16)
            wide[span, units:] = grad_up.astype(bf16)
            out = dot(act, weight[:, down], NT)
            back = dot(wide[span, :], weight[:, : 2 * units], NT)
            if i < 2:
                (out_own, out_near)[i][...] = out
                (back_own, back_near)[i][...] = back
            else:
                out_far[i - 2] = out.astype(bf16)
                back_far[i - 2] = back.astype(bf16)
        total_ref[:, : 2 * units] = dot(normed_all[...], wide[...], TN).astype(bf16)
        total_ref[:, down] = dot(grad_all[...], act_all[...], TN).astype(bf16)

    blocks = [((rows, width), f32)] * 2 + [((2, rows, width), bf16)]
    return call(
        body,
        [*blocks, *blocks, ((width, 3 * units), bf16)],
        *normed,
        *pack,
        weight,
        scratch=[
            ((4 * rows, width), bf16),
            ((4 * rows, width), bf16),
            ((4 * rows, 2 * units), bf16),
            ((4 * rows, units), bf16),
        ],
    )


def join_kernel(where, *grads):
    _, rows, cols = grads[0][0].shape
    count = len(grads)
    f32 = jnp.float32

    def body(*refs):
        place = refs[0][0]
        for k in range(4):
            span = pl.ds(pl.multiple_of((place ^ k) * cols, 128), cols)
            for n in range(count):
                half = refs[1 + 3 * n + min(k, 2)].at[place >> 1 if k < 2 else k - 2]
                refs[1 + 3 * count + n][:, span] = half[...].astype(f32)

    return call(
        body,
        [((rows, 4 * cols), f32)] * count,
        where,
        *(part for grad in grads for part in grad),
        scalars=1,
    )


def mix_kernel(hidden, dense, gate_map, slots_out):
    bf16, f32 = jnp.bfloat16, jnp.float32

    def body(hidden_ref, dense_ref, map_ref, slots_ref, out_ref):
        weights = map_ref[...]
        high = weights.astype(bf16)
        low = (weights - high.astype(f32)).astype(bf16)
        slots = slots_ref[...]
        mixed = dot(high, slots, TN) + dot(low, slots, TN)
        out_ref[...] = (hidden_ref[...] + dense_ref[...] + mixed).astype(bf16)

    return call(body, [(hidden.shape, bf16)], hidden, dense, gate_map, slots_out)[0]


def paired(
    tokens,
    cotangent,
    gain_attn,
    w_query,
    w_key,
    w_value,
    w_output,
    gain_ffn,
    dense_gate,
    dense_up,
    dense_down,
    expert_gate,
    expert_up,
    expert_down,
    routes,
    slot_order,
    gate_values,
    prefix_len,
):
    dp_count = lax.axis_size("dp")
    tensor_count = lax.axis_size("tensor")
    place = lax.axis_index("tensor")
    local_rows, width = tokens.shape
    length = local_rows * tensor_count
    columns = w_query.shape[1]
    shard = w_query.shape[0]
    hidden_cols = dense_gate.shape[1]
    devices = dp_count * tensor_count
    slots = EXPERTS * CAP
    bf16, f32 = jnp.bfloat16, jnp.float32

    nn, tn = NN, TN

    gain_width = 64
    pad_width = -(4 * columns + gain_width) % 128
    first_shard = jnp.concatenate(
        [
            w_query,
            w_key,
            w_value,
            gain_attn[:, None],
            gain_ffn[:, None],
            jnp.zeros((shard, gain_width - 2), bf16),
            w_output.T,
            jnp.zeros((shard, pad_width), bf16),
        ],
        axis=1,
    )
    dp_place = lax.axis_index("dp")
    pack = jnp.stack([tokens, cotangent])
    pack_near = to_across(after(pack, first_shard))
    row, core = place // 2, place % 2

    def split(values, axis, spot):
        size = values.shape[axis] // 2
        return (
            lax.dynamic_slice_in_dim(values, spot * size, size, axis=axis),
            lax.dynamic_slice_in_dim(values, (1 - spot) * size, size, axis=axis),
        )

    def cut_pieces(pieces):
        halves = [split(piece, 1, row) for piece in pieces]
        return [jnp.stack([half[n] for half in halves]) for n in (0, 1)]

    def share_beside(own, across):
        mine, other = split(jnp.stack([own, across]), 3, core)
        return mine, to_beside(other)

    def send_grads(grad):
        blocks = grad.reshape(2, 2, -1, grad.shape[1])
        mine = lax.dynamic_index_in_dim(blocks, core, 1, keepdims=False)
        beside = to_beside(lax.dynamic_index_in_dim(blocks, 1 - core, 1, keepdims=False))
        return mine, beside

    def cross_grads(mine, beside):
        halves = [lax.dynamic_index_in_dim(half, 1 - row, 0, keepdims=False) for half in (mine, beside)]
        return to_across(jnp.stack(halves))


    expert_ids = routes.reshape(-1)
    ranking = slot_order.reshape(-1)
    same_expert = expert_ids[:, None] == expert_ids[None, :]
    earlier = ranking[None, :] < ranking[:, None]
    placed = jnp.sum((same_expert & earlier).astype(jnp.int32), axis=1)
    targets = jnp.where(placed < CAP, expert_ids * CAP + placed, -1)
    slot_ids = jnp.arange(slots, dtype=jnp.int32)
    targets_two = targets.reshape(local_rows, TOP)
    hits = [slot_ids[:, None] == targets_two[None, :, k] for k in range(TOP)]
    token_map = sum(hit.astype(bf16) for hit in hits)
    gate_map = sum(jnp.where(hits[k], gate_values[None, :, k], 0.0) for k in range(TOP))
    slot_gate = jnp.sum(gate_map, axis=1)

    groups = [[i * tensor_count + x * 2 + c for i in range(dp_count) for x in (0, 1)] for c in (0, 1)]

    def exchange(slot_rows):
        return lax.all_to_all(
            slot_rows.reshape(EXPERTS, CAP, width),
            ("dp", "tensor"),
            split_axis=0,
            concat_axis=0,
            tiled=True,
            axis_index_groups=groups,
        ).reshape(slots, width)

    def sum_cores(own, other):
        return (own + to_beside(other.astype(bf16)).astype(f32)).astype(bf16)

    slot_cotangent = (dot(token_map, cotangent, nn) * slot_gate[:, None]).astype(bf16)
    pair_own, pair_sent = cut_pieces([expert_gate, expert_up])
    line = gather_line(first_shard)
    line[2:], slot_cotangent, pair_own, pair_sent = after(
        (line[2:], slot_cotangent, pair_own, pair_sent)
    )
    parts = gather_pairs(line)
    pair_across = to_across(after(pair_sent, pack_near))
    pack_far = to_beside(after(jnp.stack([pack, pack_near]), parts))
    token_blocks = (tokens, pack_near, pack_far)
    grad_own = exchange(after(slot_cotangent, parts))
    second_shard = jnp.concatenate([dense_gate, dense_up, dense_down.T], axis=1)
    second = lax.all_gather(after(second_shard, line[1:]), "dp", axis=0, tiled=True)

    where = jnp.stack([place, dp_place, prefix_len[0]])
    (
        *saved,
        sum_own,
        sum_near,
        sum_far,
    ) = attend_kernel(where, token_blocks, parts, length, columns)
    normed_all, weights, gains_both, *saved = saved
    gain_one, gain_two = gains_both[0], gains_both[1]
    inputs = tokens.astype(f32)
    hidden = inputs + sum_across(sum_own, sum_near, sum_far, pair_across)
    grad_rows = (grad_own, to_beside(grad_own))
    hidden = after(hidden, grad_rows)
    normed_two = norm_rows(hidden, gain_two).astype(bf16)

    dispatched = dot(token_map, normed_two, nn).astype(bf16)
    own_rows = exchange(dispatched)
    normed_near = to_across(normed_two)
    down_own, down_sent = cut_pieces([expert_down.T])
    down_across = to_across(after(down_sent, dispatched))
    normed_far = to_beside(jnp.stack([normed_two, normed_near]))
    back_own, back_near, back_far, out_own, out_near, out_far, second_grad = dense_kernel(
        (normed_two, normed_near, normed_far), (cotangent, pack_near, pack_far), second
    )
    second_total = lax.psum_scatter(second_grad, "dp", scatter_dimension=0, tiled=True)
    down_across = after(down_across, second_grad)
    pair_in = share_beside(pair_own, pair_across)
    down_in = [part[:, 0] for part in share_beside(down_own, down_across)]
    own_rows, back_far, out_far = after((own_rows, back_far, out_far), second_grad, down_in, pair_in)
    expert_rows = (own_rows, to_beside(own_rows))
    dense_back = sum_across(back_own, back_near, back_far)
    piece_down_t, slots_own, slots_other, acts, grads_gate, grads_up = expert_kernel(
        where, expert_rows, grad_rows, pair_in, down_in
    )
    back_rows = sum_cores(slots_own, slots_other)
    slots_back = exchange(back_rows)

    mixed_own, mixed_other, gate_grad, up_grad, down_grad = expert_grad_kernel(
        after(expert_rows, back_rows), grad_rows, acts, grads_gate, grads_up, piece_down_t
    )
    out_rows = sum_cores(mixed_own, mixed_other)
    gate_parts = send_grads(gate_grad)
    up_parts, down_parts = send_grads(up_grad), send_grads(down_grad)
    slots_back = after(slots_back, out_rows, dense_back, gate_parts, up_parts, down_parts)

    expert_back = dot(token_map, slots_back, tn)
    grad_normed_two = dense_back + expert_back
    grad_hidden_norm, grad_gain_two = norm_back(hidden, gain_two, grad_normed_two)
    grad_hidden = cotangent.astype(f32) + grad_hidden_norm

    grad_attn_own = grad_hidden.astype(bf16)
    grad_near = to_across(grad_attn_own)
    grad_far = to_beside(jnp.stack([grad_attn_own, grad_near]))
    slots_out = exchange(after(out_rows, grad_attn_own))
    gate_parts += (cross_grads(*after(gate_parts, grad_near)),)
    up_parts += (cross_grads(*after(up_parts, grad_near)),)
    first_grad, back_own, back_near, back_far = attend_back_kernel(
        where,
        token_blocks,
        (grad_attn_own, grad_near, grad_far),
        [normed_all, weights, *saved],
        grad_gain_two[None],
        length,
        columns,
    )
    first_grad = after(first_grad, slots_out, gate_parts)
    first_parts = lax.all_to_all(
        first_grad.reshape(dp_count, shard, -1), "dp", split_axis=0, concat_axis=0, tiled=True
    )
    grad_normed_one = sum_across(back_own, back_near, back_far, up_parts)
    grad_input_norm, _ = norm_back(inputs, gain_one, grad_normed_one)
    grad_tokens = grad_hidden + grad_input_norm
    down_parts, out_far = after((down_parts, out_far), first_grad)
    down_parts += (cross_grads(*down_parts),)
    dense_out = sum_across(out_own, out_near, out_far)
    slots_out, gate_parts, up_parts = after((slots_out, gate_parts, up_parts), first_grad)
    block_out = mix_kernel(hidden, dense_out, gate_map, slots_out)
    gate_total, up_total = join_kernel(where, gate_parts, up_parts)
    (down_total,) = join_kernel(where, down_parts)
    second_total = after(second_total, block_out).astype(f32)
    first_parts = after(first_parts, block_out, gate_total)
    first_total = jnp.sum(first_parts.astype(f32), axis=0)
    gains = first_total[:, 3 * columns : 3 * columns + 2].T
    gains = gains + to_beside(gains)
    gains = gains + to_across(gains)
    return (
        block_out,
        grad_tokens,
        gains[0],
        first_total[:, :columns],
        first_total[:, columns : 2 * columns],
        first_total[:, 2 * columns : 3 * columns],
        first_total[:, 3 * columns + gain_width :][:, :columns].T,
        gains[1],
        second_total[:, :hidden_cols],
        second_total[:, hidden_cols : 2 * hidden_cols],
        second_total[:, 2 * hidden_cols :].T,
        gate_total,
        up_total,
        down_total.T,
    )


def gather_rows(rows_in):
    return lax.all_gather(rows_in, "tensor", axis=0, tiled=True)


def sum_rows(rows_in):
    return lax.psum_scatter(rows_in, "tensor", scatter_dimension=0, tiled=True)


def gather_attn_rows(rows_in):
    return lax.all_gather(rows_in, "tensor", axis=0, tiled=True)


def sum_attn_rows(rows_in):
    return lax.psum_scatter(rows_in, "tensor", scatter_dimension=0, tiled=True)


def general(
    tokens,
    cotangent,
    gain_attn,
    w_query,
    w_key,
    w_value,
    w_output,
    gain_ffn,
    dense_gate,
    dense_up,
    dense_down,
    expert_gate,
    expert_up,
    expert_down,
    routes,
    slot_order,
    gate_values,
    prefix_len,
):
    dp_count = lax.axis_size("dp")
    tensor_count = lax.axis_size("tensor")
    local_rows = tokens.shape[0]
    model_width = tokens.shape[1]
    length = local_rows * tensor_count
    splits = max(1, dp_count // EXPERTS)
    per_device = max(1, EXPERTS // dp_count)
    inputs = tokens.astype(jnp.float32)
    dense_all = (
        lax.all_gather(gain_attn, "dp", axis=0, tiled=True),
        lax.all_gather(w_query, "dp", axis=0, tiled=True),
        lax.all_gather(w_key, "dp", axis=0, tiled=True),
        lax.all_gather(w_value, "dp", axis=0, tiled=True),
        lax.all_gather(w_output, "dp", axis=1, tiled=True),
        lax.all_gather(gain_ffn, "dp", axis=0, tiled=True),
        lax.all_gather(dense_gate, "dp", axis=0, tiled=True),
        lax.all_gather(dense_up, "dp", axis=0, tiled=True),
        lax.all_gather(dense_down, "dp", axis=1, tiled=True),
    )
    (
        gain_one,
        query_full,
        key_full,
        value_full,
        output_full,
        gain_two,
        gate_full,
        up_full,
        down_full,
    ) = dense_all
    gain_one = gain_one.astype(jnp.float32)
    gain_two = gain_two.astype(jnp.float32)
    positions = jnp.arange(length, dtype=jnp.int32)
    prefix_value = prefix_len[0]
    normed_one = norm_rows(inputs, gain_one).astype(jnp.bfloat16)
    head_count = query_full.shape[1] // HEAD_DIM
    normed_all = gather_attn_rows(normed_one)
    queries = rotary(
        jnp.dot(normed_all, query_full, preferred_element_type=jnp.float32).reshape(
            length, head_count, HEAD_DIM
        ),
        positions,
        1.0,
    ).astype(jnp.bfloat16)
    keys_all = rotary(
        jnp.dot(normed_all, key_full, preferred_element_type=jnp.float32).reshape(
            length, head_count, HEAD_DIM
        ),
        positions,
        1.0,
    ).astype(jnp.bfloat16)
    values_all = (
        jnp.dot(normed_all, value_full, preferred_element_type=jnp.float32)
        .astype(jnp.bfloat16)
        .reshape(length, head_count, HEAD_DIM)
    )
    score_scale = 1.0 / math.sqrt(HEAD_DIM)
    block_rows = min(512, length)
    blocks = length // block_rows
    query_blocks = queries.reshape(blocks, block_rows, head_count, HEAD_DIM)
    position_blocks = positions.reshape(blocks, block_rows)

    def block_scores(block_query, block_pos):
        scores = (
            jnp.einsum("qhd,khd->hqk", block_query, keys_all, preferred_element_type=jnp.float32)
            * score_scale
        )
        visible = (positions[None, :] <= block_pos[:, None]) | (positions[None, :] < prefix_value)
        return jnp.where(visible[None], scores, -1e30)

    def attend(block_item):
        block_query, block_pos = block_item
        scores = block_scores(block_query, block_pos)
        row_top = jnp.max(scores, axis=-1, keepdims=True)
        exponent = jnp.exp(scores - row_top)
        row_total = jnp.sum(exponent, axis=-1, keepdims=True)
        softmaxed = exponent / row_total
        mixture = jnp.einsum(
            "hqk,khd->qhd",
            softmaxed.astype(jnp.bfloat16),
            values_all,
            preferred_element_type=jnp.float32,
        ).astype(jnp.bfloat16)
        return (mixture, (row_top + jnp.log(row_total))[..., 0])

    attended, log_totals = lax.map(attend, (query_blocks, position_blocks))
    attended = attended.reshape(length, head_count * HEAD_DIM)
    hidden = inputs + sum_attn_rows(
        jnp.dot(attended, output_full, preferred_element_type=jnp.float32)
    )
    normed_two = norm_rows(hidden, gain_two).astype(jnp.bfloat16)
    normed_two_all = gather_rows(normed_two)
    gate_pre = jnp.dot(normed_two_all, gate_full, preferred_element_type=jnp.float32)
    up_pre = jnp.dot(normed_two_all, up_full, preferred_element_type=jnp.float32)
    activated = (jax.nn.silu(gate_pre) * up_pre).astype(jnp.bfloat16)
    dense_out = sum_rows(jnp.dot(activated, down_full, preferred_element_type=jnp.float32))
    expert_ids = routes.reshape(-1)
    ranking = slot_order.reshape(-1)
    same_expert = expert_ids[:, None] == expert_ids[None, :]
    earlier = ranking[None, :] < ranking[:, None]
    placed = jnp.sum((same_expert & earlier).astype(jnp.int32), axis=1)
    usable = placed < CAP
    targets = jnp.where(usable, expert_ids * CAP + placed, -1)
    slot_ids = jnp.arange(EXPERTS * CAP, dtype=jnp.int32)
    pair_map = (slot_ids[:, None] == targets[None, :]).astype(jnp.float32)
    token_map = jnp.sum(pair_map.reshape(EXPERTS * CAP, local_rows, TOP), axis=2).astype(
        jnp.bfloat16
    )
    dispatched = jnp.dot(token_map, normed_two, preferred_element_type=jnp.float32).astype(
        jnp.bfloat16
    )
    outgoing = jnp.broadcast_to(
        dispatched.reshape(EXPERTS, 1, CAP, model_width), (EXPERTS, splits, CAP, model_width)
    ).reshape(dp_count, per_device, CAP, model_width)
    expert_all = (
        lax.all_gather(expert_gate, "tensor", axis=0, tiled=True),
        lax.all_gather(expert_up, "tensor", axis=0, tiled=True),
        lax.all_gather(expert_down, "tensor", axis=1, tiled=True),
    )
    piece_width = expert_all[0].shape[1] // per_device
    gate_pieces = expert_all[0].reshape(model_width, per_device, piece_width)
    up_pieces = expert_all[1].reshape(model_width, per_device, piece_width)
    down_pieces = expert_all[2].reshape(per_device, piece_width, model_width)
    received = lax.all_to_all(outgoing, "dp", split_axis=0, concat_axis=0, tiled=True)
    gate_local = jnp.einsum(
        "sjnd,djp->sjnp", received, gate_pieces, preferred_element_type=jnp.float32
    )
    up_local = jnp.einsum("sjnd,djp->sjnp", received, up_pieces, preferred_element_type=jnp.float32)
    active_local = (jax.nn.silu(gate_local) * up_local).astype(jnp.bfloat16)
    result_local = jnp.einsum(
        "sjnp,jpd->sjnd", active_local, down_pieces, preferred_element_type=jnp.float32
    ).astype(jnp.bfloat16)
    returned = lax.all_to_all(result_local, "dp", split_axis=0, concat_axis=0, tiled=True)
    returned, kept_in, gate_local, up_local = (returned, received, gate_local, up_local)
    expert_sums = jnp.sum(
        returned.reshape(EXPERTS, splits, CAP, model_width).astype(jnp.float32), axis=1
    ).reshape(EXPERTS * CAP, model_width)
    pick_index = jnp.where(usable, targets, 0)
    pair_weight = jnp.where(usable, gate_values.reshape(-1), 0.0)
    picked = jnp.take(expert_sums, pick_index, axis=0) * pair_weight[:, None]
    expert_mix = jnp.sum(picked.reshape(local_rows, TOP, model_width), axis=1)
    block_out = (hidden + dense_out + expert_mix).astype(jnp.bfloat16)
    dense_back = (
        lax.all_gather(gain_attn, "dp", axis=0, tiled=True),
        lax.all_gather(w_query, "dp", axis=0, tiled=True),
        lax.all_gather(w_key, "dp", axis=0, tiled=True),
        lax.all_gather(w_value, "dp", axis=0, tiled=True),
        lax.all_gather(w_output, "dp", axis=1, tiled=True),
        lax.all_gather(gain_ffn, "dp", axis=0, tiled=True),
        lax.all_gather(dense_gate, "dp", axis=0, tiled=True),
        lax.all_gather(dense_up, "dp", axis=0, tiled=True),
        lax.all_gather(dense_down, "dp", axis=1, tiled=True),
    )
    (
        gain_one,
        query_full,
        key_full,
        value_full,
        output_full,
        gain_two,
        gate_full,
        up_full,
        down_full,
    ) = dense_back
    gain_one = gain_one.astype(jnp.float32)
    gain_two = gain_two.astype(jnp.float32)
    grad_out = cotangent.astype(jnp.float32)
    cotangent_all = gather_rows(cotangent)
    grad_down = jnp.einsum(
        "lf,ld->fd", activated, cotangent_all, preferred_element_type=jnp.float32
    )
    grad_act = jnp.einsum("ld,fd->lf", cotangent_all, down_full, preferred_element_type=jnp.float32)
    grad_gate_pre, grad_up_pre = swiglu_back(grad_act, gate_pre, up_pre)
    grad_gate = jnp.einsum(
        "ld,lf->df", normed_two_all, grad_gate_pre, preferred_element_type=jnp.float32
    )
    grad_up = jnp.einsum(
        "ld,lf->df", normed_two_all, grad_up_pre, preferred_element_type=jnp.float32
    )
    dense_back_in = jnp.einsum(
        "lf,df->ld", grad_gate_pre, gate_full, preferred_element_type=jnp.float32
    ) + jnp.einsum("lf,df->ld", grad_up_pre, up_full, preferred_element_type=jnp.float32)
    slot_gate = jnp.dot(pair_map, gate_values.reshape(-1), precision=lax.Precision.HIGHEST)
    slot_cotangent = jnp.dot(token_map, cotangent, preferred_element_type=jnp.float32)
    grad_slots = (slot_cotangent * slot_gate[:, None]).astype(jnp.bfloat16)
    grad_outgoing = jnp.broadcast_to(
        grad_slots.reshape(EXPERTS, 1, CAP, model_width), (EXPERTS, splits, CAP, model_width)
    ).reshape(dp_count, per_device, CAP, model_width)
    grad_received = lax.all_to_all(grad_outgoing, "dp", split_axis=0, concat_axis=0, tiled=True)
    active_local = (jax.nn.silu(gate_local) * up_local).astype(jnp.bfloat16)
    grad_down_expert = jnp.einsum(
        "sjnp,sjnd->jpd", active_local, grad_received, preferred_element_type=jnp.float32
    ).reshape(per_device * piece_width, model_width)
    grad_act_expert = jnp.einsum(
        "sjnd,jpd->sjnp", grad_received, down_pieces, preferred_element_type=jnp.float32
    )
    grad_gate_local, grad_up_local = swiglu_back(grad_act_expert, gate_local, up_local)
    grad_gate_expert = jnp.einsum(
        "sjnd,sjnp->djp", kept_in, grad_gate_local, preferred_element_type=jnp.float32
    ).reshape(model_width, per_device * piece_width)
    grad_up_expert = jnp.einsum(
        "sjnd,sjnp->djp", kept_in, grad_up_local, preferred_element_type=jnp.float32
    ).reshape(model_width, per_device * piece_width)
    grad_in_expert = (
        jnp.einsum(
            "sjnp,djp->sjnd", grad_gate_local, gate_pieces, preferred_element_type=jnp.float32
        )
        + jnp.einsum("sjnp,djp->sjnd", grad_up_local, up_pieces, preferred_element_type=jnp.float32)
    ).astype(jnp.bfloat16)
    grad_back = lax.all_to_all(grad_in_expert, "dp", split_axis=0, concat_axis=0, tiled=True)
    grad_slots_in = jnp.sum(
        grad_back.reshape(EXPERTS, splits, CAP, model_width).astype(jnp.float32), axis=1
    ).reshape(EXPERTS * CAP, model_width)
    grad_pairs = jnp.where(usable[:, None], jnp.take(grad_slots_in, pick_index, axis=0), 0.0)
    expert_back = jnp.sum(grad_pairs.reshape(local_rows, TOP, model_width), axis=1)
    grad_normed_two = sum_rows(dense_back_in) + expert_back
    grad_hidden_norm, grad_gain_two_part = norm_back(hidden, gain_two, grad_normed_two)
    grad_hidden = grad_out + grad_hidden_norm
    query_use, key_use, value_use, output_use = (query_full, key_full, value_full, output_full)
    grad_attn_in = gather_attn_rows(grad_hidden.astype(jnp.bfloat16))
    grad_output_w = jnp.einsum(
        "lc,ld->cd", attended, grad_attn_in, preferred_element_type=jnp.float32
    )
    grad_attended = (
        jnp.einsum("ld,cd->lc", grad_attn_in, output_use, preferred_element_type=jnp.float32)
        .astype(jnp.bfloat16)
        .reshape(blocks, block_rows, head_count, HEAD_DIM)
    )

    def attend_back(running, block_item):
        grad_keys, grad_values = running
        block_query, block_pos, block_grad, block_total = block_item
        scores = block_scores(block_query, block_pos)
        softmaxed = jnp.exp(scores - block_total[..., None])
        grad_soft = jnp.einsum(
            "qhd,khd->hqk", block_grad, values_all, preferred_element_type=jnp.float32
        )
        inner_sum = jnp.sum(softmaxed * grad_soft, axis=-1, keepdims=True)
        grad_scores = (softmaxed * (grad_soft - inner_sum)).astype(jnp.bfloat16)
        grad_block = (
            jnp.einsum("hqk,khd->qhd", grad_scores, keys_all, preferred_element_type=jnp.float32)
            * score_scale
        )
        grad_keys = (
            grad_keys
            + jnp.einsum(
                "hqk,qhd->khd", grad_scores, block_query, preferred_element_type=jnp.float32
            )
            * score_scale
        )
        grad_values = grad_values + jnp.einsum(
            "hqk,qhd->khd",
            softmaxed.astype(jnp.bfloat16),
            block_grad,
            preferred_element_type=jnp.float32,
        )
        return ((grad_keys, grad_values), grad_block)

    zero_start = (
        jnp.zeros((length, head_count, HEAD_DIM), jnp.float32),
        jnp.zeros((length, head_count, HEAD_DIM), jnp.float32),
    )
    (grad_keys, grad_values), grad_queries = lax.scan(
        attend_back, zero_start, (query_blocks, position_blocks, grad_attended, log_totals)
    )
    grad_queries = (
        rotary(grad_queries.reshape(length, head_count, HEAD_DIM), positions, -1.0)
        .astype(jnp.bfloat16)
        .reshape(length, head_count * HEAD_DIM)
    )
    grad_keys = (
        rotary(grad_keys, positions, -1.0)
        .astype(jnp.bfloat16)
        .reshape(length, head_count * HEAD_DIM)
    )
    grad_values = grad_values.astype(jnp.bfloat16).reshape(length, head_count * HEAD_DIM)
    grad_query_w = jnp.einsum(
        "ld,lc->dc", normed_all, grad_queries, preferred_element_type=jnp.float32
    )
    grad_key_w = jnp.einsum("ld,lc->dc", normed_all, grad_keys, preferred_element_type=jnp.float32)
    grad_value_w = jnp.einsum(
        "ld,lc->dc", normed_all, grad_values, preferred_element_type=jnp.float32
    )
    normed_back_part = (
        jnp.einsum("lc,dc->ld", grad_queries, query_use, preferred_element_type=jnp.float32)
        + jnp.einsum("lc,dc->ld", grad_keys, key_use, preferred_element_type=jnp.float32)
        + jnp.einsum("lc,dc->ld", grad_values, value_use, preferred_element_type=jnp.float32)
    )
    grad_normed_one = sum_attn_rows(normed_back_part)
    grad_input_norm, grad_gain_one_part = norm_back(inputs, gain_one, grad_normed_one)
    grad_tokens = grad_hidden + grad_input_norm
    dense_grads = (
        lax.psum_scatter(grad_gain_one_part, "dp", scatter_dimension=0, tiled=True),
        lax.psum_scatter(grad_query_w, "dp", scatter_dimension=0, tiled=True),
        lax.psum_scatter(grad_key_w, "dp", scatter_dimension=0, tiled=True),
        lax.psum_scatter(grad_value_w, "dp", scatter_dimension=0, tiled=True),
        lax.psum_scatter(grad_output_w, "dp", scatter_dimension=1, tiled=True),
        lax.psum_scatter(grad_gain_two_part, "dp", scatter_dimension=0, tiled=True),
        lax.psum_scatter(grad_gate, "dp", scatter_dimension=0, tiled=True),
        lax.psum_scatter(grad_up, "dp", scatter_dimension=0, tiled=True),
        lax.psum_scatter(grad_down, "dp", scatter_dimension=1, tiled=True),
    )
    gain_totals = lax.psum((dense_grads[0], dense_grads[5]), "tensor")
    expert_grads = (
        lax.psum_scatter(
            grad_gate_expert.astype(jnp.bfloat16), "tensor", scatter_dimension=0, tiled=True
        ).astype(jnp.float32),
        lax.psum_scatter(
            grad_up_expert.astype(jnp.bfloat16), "tensor", scatter_dimension=0, tiled=True
        ).astype(jnp.float32),
        lax.psum_scatter(
            grad_down_expert.astype(jnp.bfloat16), "tensor", scatter_dimension=1, tiled=True
        ).astype(jnp.float32),
    )
    return (
        block_out,
        grad_tokens,
        gain_totals[0],
        dense_grads[1],
        dense_grads[2],
        dense_grads[3],
        dense_grads[4],
        gain_totals[1],
        dense_grads[6],
        dense_grads[7],
        dense_grads[8],
        expert_grads[0],
        expert_grads[1],
        expert_grads[2],
    )


def solution(mesh):
    sizes = mesh.shape
    in_pairs = sizes["tensor"] == 4 and sizes["dp"] * 2 == EXPERTS
    local = paired if in_pairs else general
    return jax.shard_map(
        local,
        mesh=mesh,
        in_specs=(
            P(("dp", "tensor"), None),
            P(("dp", "tensor"), None),
            P("dp"),
            P("dp", "tensor"),
            P("dp", "tensor"),
            P("dp", "tensor"),
            P("tensor", "dp"),
            P("dp"),
            P("dp", "tensor"),
            P("dp", "tensor"),
            P("tensor", "dp"),
            P("tensor", "dp"),
            P("tensor", "dp"),
            P("dp", "tensor"),
            P(("dp", "tensor"), None),
            P(("dp", "tensor"), None),
            P(("dp", "tensor"), None),
            P("dp"),
        ),
        out_specs=(
            P(("dp", "tensor"), None),
            P(("dp", "tensor"), None),
            P("dp"),
            P("dp", "tensor"),
            P("dp", "tensor"),
            P("dp", "tensor"),
            P("tensor", "dp"),
            P("dp"),
            P("dp", "tensor"),
            P("dp", "tensor"),
            P("tensor", "dp"),
            P("tensor", "dp"),
            P("tensor", "dp"),
            P("dp", "tensor"),
        ),
        check_vma=False,
    )
```

```python
import math

import jax
import jax.numpy as jnp
import numpy as np
from jax import lax
from jax.experimental import pallas as pl
from jax.experimental.pallas import tpu as pltpu
from jax.sharding import PartitionSpec as P

HEAD_DIM = 64
EXPERTS = 16
TOP = 2
CAP = 40


epsilon = 1e-06


def norm_rows(rows_in, gain_row):
    return (
        rows_in
        * lax.rsqrt(jnp.mean(rows_in * rows_in, axis=-1, keepdims=True) + epsilon)
        * gain_row
    )


def norm_back(rows_in, gain_row, grad_out):
    inverse = lax.rsqrt(jnp.mean(rows_in * rows_in, axis=-1, keepdims=True) + epsilon)
    scaled = grad_out * gain_row
    grad_rows = inverse * scaled - rows_in * inverse**3 * jnp.mean(
        scaled * rows_in, axis=-1, keepdims=True
    )
    grad_gain = jnp.sum(grad_out * rows_in * inverse, axis=0)
    return (grad_rows, grad_gain)


def rotary(values, positions, direction):
    half_width = values.shape[-1] // 2
    frequency = jnp.power(10000.0, -jnp.arange(half_width).astype(jnp.float32) / half_width)
    angles = positions[:, None].astype(jnp.float32) * frequency[None, :]
    cosine = jnp.cos(angles)[:, None, :]
    sine_part = direction * jnp.sin(angles)[:, None, :]
    first_half = values[..., :half_width]
    second_half = values[..., half_width:]
    return jnp.concatenate(
        [
            first_half * cosine - second_half * sine_part,
            second_half * cosine + first_half * sine_part,
        ],
        axis=-1,
    )


def swiglu_back(grad_act, gate_pre, up_pre):
    sigmoid = jax.nn.sigmoid(gate_pre)
    silu_value = gate_pre * sigmoid
    grad_gate = grad_act * up_pre * sigmoid * (1.0 + gate_pre * (1.0 - sigmoid))
    grad_up = grad_act * silu_value
    return (grad_gate.astype(jnp.bfloat16), grad_up.astype(jnp.bfloat16))


def to_across(values):
    return lax.ppermute(values, "tensor", [(i, i ^ 2) for i in range(4)])


def to_beside(values):
    return lax.ppermute(values, "tensor", [(i, i ^ 1) for i in range(4)])


def gather_blocks(rows_in):
    near = jnp.stack([rows_in, to_across(rows_in)])
    return jnp.concatenate([near, to_beside(near)]).reshape(-1, rows_in.shape[-1])


def sum_across(own, near, far, *before):
    beside = to_beside(far)
    beside = [part.astype(jnp.float32) for part in after((beside[0], beside[1]))]
    sent = (near + beside[1]).astype(jnp.bfloat16)
    return own + beside[0] + to_across(after(sent, *before) if before else sent).astype(jnp.float32)


def after(value, *before):
    if not before:
        return lax.optimization_barrier(value)
    return lax.optimization_barrier((value,) + before)[0]


def sum_blocks(partial):
    blocks = partial.reshape(4, -1, partial.shape[-1])
    near = blocks[:2] + to_beside(blocks[2:].astype(jnp.bfloat16)).astype(jnp.float32)
    return near[0] + to_across(near[1].astype(jnp.bfloat16)).astype(jnp.float32)


def along(values, axis, k):
    return lax.ppermute(values, axis, [(i, i ^ k) for i in range(lax.axis_size(axis))])


def gather_line(rows_in):
    return [along(rows_in, "dp", k) if k else rows_in for k in range(0, lax.axis_size("dp"), 2)]


def gather_pairs(line):
    return [part for own in line for part in (own, along(own, "dp", 1))]


def dot(left, right, dims):
    return lax.dot_general(left, right, (dims, ((), ())), preferred_element_type=jnp.float32)


NN, NT, TN = ((1,), (0,)), ((1,), (1,)), ((0,), (0,))
ORDER = (0, 2, 1, 3)
VMEM = pl.BlockSpec(memory_space=pltpu.VMEM)
SMEM = pl.BlockSpec(memory_space=pltpu.SMEM)
HBM = pl.BlockSpec(memory_space=pltpu.HBM)
NO_COST = pl.CostEstimate(flops=0, bytes_accessed=0, transcendentals=0)


def angle_tables(length):
    half = HEAD_DIM // 2
    lane = np.arange(2 * HEAD_DIM)
    frequency = np.power(10000.0, -(lane % half).astype(np.float64) / half)
    angles = np.arange(length)[:, None] * frequency[None, :]
    sign = np.where(lane % HEAD_DIM < half, -1.0, 1.0)
    return np.cos(angles).astype(np.float32), (np.sin(angles) * sign).astype(np.float32)


def turn(values, cosine, sine):
    width = values.shape[1]
    half = HEAD_DIM // 2
    lane = lax.broadcasted_iota(jnp.int32, values.shape, 1)
    swapped = jnp.where(
        lane % HEAD_DIM < half,
        pltpu.roll(values, width - half, 1),
        pltpu.roll(values, half, 1),
    )
    repeats = width // cosine.shape[1]
    return values * jnp.concatenate([cosine] * repeats, axis=1) + swapped * jnp.concatenate(
        [sine] * repeats, axis=1
    )


def block_at(place, i):
    return place ^ ((i >> 1) | ((i & 1) << 1))


def pack_views(own, near, far, n):
    return own, near.at[n], far.at[0, n], far.at[1, n]


def seen(place, prefix, i, j, rows):
    query_block, key_block = block_at(place, i), block_at(place, j)
    return (key_block <= query_block) | (key_block * rows < prefix)


def mask_of(place, prefix, i, j, rows):
    key = block_at(place, j) * rows + lax.broadcasted_iota(jnp.int32, (rows, rows), 0)
    query = block_at(place, i) * rows + lax.broadcasted_iota(jnp.int32, (rows, rows), 1)
    return key <= jnp.maximum(query, prefix - 1)


def attend_kernel(where, blocks_in, parts, length, columns):
    rows, width = blocks_in[0].shape
    shard, lanes = parts[0].shape
    blocks = length // rows
    heads = columns // HEAD_DIM
    count = len(parts)
    gain_at = 3 * columns
    output_at = 3 * columns + 64
    bf16, f32 = jnp.bfloat16, jnp.float32
    cosine, sine = angle_tables(length)

    def body(*refs):
        spot, token_refs = refs[0], pack_views(*refs[1:4], 0)
        part_refs = refs[4 : 4 + count]
        cos_ref, sin_ref = refs[4 + count : 6 + count]
        (
            normed_ref,
            weight_ref,
            gain_ref,
            query_ref,
            query_t_ref,
            key_ref,
            value_ref,
            mixed_ref,
            mixed_t_ref,
            log_ref,
            sum_own_ref,
            sum_near_ref,
            sum_far_ref,
        ) = refs[6 + count : 19 + count]
        value_t_ref, score_ref, top_ref, total_ref, mix_ref, *keep, sems = refs[19 + count :]
        outward = [
            pltpu.make_async_copy(source, target, sems.at[n])
            for n, (source, target) in enumerate(
                zip(
                    keep,
                    (
                        normed_ref,
                        weight_ref,
                        query_ref,
                        query_t_ref,
                        key_ref,
                        value_ref,
                        mixed_ref,
                        mixed_t_ref,
                    ),
                )
            )
        ]
        (
            normed_ref,
            weight_ref,
            query_ref,
            query_t_ref,
            key_ref,
            value_ref,
            mixed_ref,
            mixed_t_ref,
        ) = keep
        place, dp_place, prefix = spot[0], spot[1], spot[2]
        for k in range(count):
            start = pl.multiple_of((dp_place ^ k) * shard, 16)
            weight_ref[pl.ds(start, shard), :] = part_refs[k][...]
        gain_tile = weight_ref[:, gain_at // 128 * 128 : gain_at // 128 * 128 + 128].astype(f32)
        gain_ref[...] = gain_tile.T[gain_at % 128 : gain_at % 128 + 8, :]
        gain = gain_ref[0:1, :]
        for i in range(blocks):
            tokens = token_refs[i][...].astype(f32)
            inverse = lax.rsqrt(jnp.mean(tokens * tokens, axis=-1, keepdims=True) + epsilon)
            normed = (tokens * inverse * gain).astype(bf16)
            span = pl.ds(i * rows, rows)
            normed_ref[span, :] = normed
            product = dot(normed, weight_ref[:, : 3 * columns], NN)
            spot_rows = pl.ds(pl.multiple_of(block_at(place, i) * rows, 8), rows)
            turned = turn(product[:, : 2 * columns], cos_ref[spot_rows, :], sin_ref[spot_rows, :])
            query = turned[:, :columns] * (1.0 / math.sqrt(HEAD_DIM))
            key = turned[:, columns:]
            value = product[:, 2 * columns :]
            query_t = query.T
            value_t = value.T
            for h in range(heads):
                cut = slice(h * HEAD_DIM, (h + 1) * HEAD_DIM)
                query_ref[h, span, :] = query[:, cut].astype(bf16)
                query_t_ref[h, :, span] = query_t[cut, :].astype(bf16)
                key_ref[h, span, :] = key[:, cut].astype(bf16)
                value_ref[h, span, :] = value[:, cut].astype(bf16)
                value_t_ref[h, :, span] = value_t[cut, :].astype(bf16)

        for copy in outward[:6]:
            copy.start()

        def query_block(i, carry):
            here = pl.ds(pl.multiple_of(i * rows, 128), rows)
            top_ref[...] = jnp.full(top_ref.shape, -1e30, f32)
            total_ref[...] = jnp.zeros(total_ref.shape, f32)
            mix_ref[...] = jnp.zeros(mix_ref.shape, f32)

            def scores(j, carry):
                @pl.when(seen(place, prefix, i, j, rows))
                def _():
                    there = pl.ds(pl.multiple_of(j * rows, 128), rows)
                    visible = mask_of(place, prefix, i, j, rows)
                    for h in range(heads):
                        score = dot(key_ref[h, there, :], query_t_ref[h, :, here], NN)
                        score = jnp.where(visible, score, -1e30)
                        score_ref[h, there, :] = score
                        top_ref[h : h + 1, :] = jnp.maximum(
                            top_ref[h : h + 1, :], jnp.max(score, axis=0, keepdims=True)
                        )

                return carry

            def mixing(j, carry):
                @pl.when(seen(place, prefix, i, j, rows))
                def _():
                    there = pl.ds(pl.multiple_of(j * rows, 128), rows)
                    for h in range(heads):
                        power = jnp.exp(score_ref[h, there, :] - top_ref[h : h + 1, :])
                        total_ref[h : h + 1, :] += jnp.sum(power, axis=0, keepdims=True)
                        mix_ref[h] += dot(value_t_ref[h, :, there], power.astype(bf16), NN)

                return carry

            lax.fori_loop(0, blocks, scores, 0)
            lax.fori_loop(0, blocks, mixing, 0)
            log_ref[:, here] = top_ref[...] + jnp.log(jnp.maximum(total_ref[...], 1e-30))
            mixed_t = jnp.concatenate(
                [mix_ref[h] * (1.0 / total_ref[h : h + 1, :]) for h in range(heads)], axis=0
            )
            for h in range(heads):
                mixed_t_ref[h, :, here] = mixed_t[h * HEAD_DIM : (h + 1) * HEAD_DIM, :].astype(bf16)
            mixed = mixed_t.T.astype(bf16)
            mixed_ref[here, :] = mixed
            partial = dot(mixed, weight_ref[:, output_at : output_at + columns], NT)

            @pl.when(i == 0)
            def _():
                sum_own_ref[...] = partial

            @pl.when(i == 1)
            def _():
                sum_near_ref[...] = partial

            @pl.when(i >= 2)
            def _():
                sum_far_ref[i - 2] = partial.astype(bf16)

            return carry

        lax.fori_loop(0, blocks, query_block, 0)
        for copy in outward[6:]:
            copy.start()
        for copy in outward:
            copy.wait()

    per_head = (heads, length, HEAD_DIM)
    per_head_t = (heads, HEAD_DIM, length)
    out_shape = [
        jax.ShapeDtypeStruct(shape, kind)
        for shape, kind in (
            ((length, width), bf16),
            ((count * shard, lanes), bf16),
            ((8, width), f32),
            (per_head, bf16),
            (per_head_t, bf16),
            (per_head, bf16),
            (per_head, bf16),
            ((length, columns), bf16),
            (per_head_t, bf16),
            ((8, length), f32),
            ((rows, width), f32),
            ((rows, width), f32),
            ((2, rows, width), bf16),
        )
    ]
    return pl.pallas_call(
        body,
        out_shape=out_shape,
        in_specs=[SMEM] + [VMEM] * (5 + count),
        out_specs=[HBM] * 2 + [VMEM] + [HBM] * 6 + [VMEM] * 4,
        scratch_shapes=[
            pltpu.VMEM(per_head_t, bf16),
            pltpu.VMEM((heads, length, rows), f32),
            pltpu.VMEM((8, rows), f32),
            pltpu.VMEM((8, rows), f32),
            pltpu.VMEM((heads, HEAD_DIM, rows), f32),
        ]
        + [pltpu.VMEM(out_shape[n].shape, bf16) for n in (0, 1, 3, 4, 5, 6, 7, 8)]
        + [pltpu.SemaphoreType.DMA((8,))],
        compiler_params=pltpu.CompilerParams(vmem_limit_bytes=60 * 2**20),
        cost_estimate=NO_COST,
    )(where, *blocks_in, *parts, cosine, sine)


def attend_back_kernel(
    where, blocks_in, grads_in, saved, gain_two, length, columns
):
    normed, weight, query, query_t, key, value, mixed, mixed_t, log_total = saved
    rows, width = blocks_in[0].shape
    lanes = weight.shape[1]
    blocks = length // rows
    heads = columns // HEAD_DIM
    output_at = 3 * columns + 64
    bf16, f32 = jnp.bfloat16, jnp.float32
    cosine, sine = angle_tables(length)

    def body(*refs):
        (
            spot,
            own_ref,
            near_ref,
            far_ref,
            grad_own_ref,
            grad_near_ref,
            grad_far_ref,
            normed_ref,
            weight_ref,
            query_ref,
            query_t_ref,
            key_ref,
            value_ref,
            mixed_ref,
            mixed_t_ref,
            log_ref,
            gain_two_ref,
            cos_ref,
            sin_ref,
            first_ref,
            back_own_ref,
            back_near_ref,
            back_far_ref,
            grad_in,
            grad_mix,
            grad_mix_t,
            inner,
            key_t,
            grad_query_t,
            grad_key,
            grad_value,
            grad_product,
            *keep,
            sems,
        ) = refs
        place, prefix = spot[0], spot[2]
        inward = [
            pltpu.make_async_copy(source, target, sems.at[n])
            for n, (source, target) in enumerate(
                zip(
                    (
                        weight_ref,
                        mixed_t_ref,
                        key_ref,
                        query_t_ref,
                        query_ref,
                        value_ref,
                        own_ref,
                        near_ref.at[0],
                        far_ref.at[0, 0],
                        far_ref.at[1, 0],
                        normed_ref,
                        mixed_ref,
                        cos_ref,
                        sin_ref,
                    ),
                    keep,
                )
            )
        ]
        for copy in inward:
            copy.start()
        (
            weight_ref,
            mixed_t_ref,
            key_ref,
            query_t_ref,
            query_ref,
            value_ref,
            *token_refs,
            normed_ref,
            mixed_ref,
            cos_ref,
            sin_ref,
        ) = keep
        grad_refs = (grad_own_ref, grad_near_ref, grad_far_ref.at[0], grad_far_ref.at[1])
        grad_key[...] = jnp.zeros(grad_key.shape, f32)
        grad_value[...] = jnp.zeros(grad_value.shape, f32)
        grad_query_t[...] = jnp.zeros(grad_query_t.shape, f32)
        for copy in inward[:3]:
            copy.wait()
        for h in range(heads):
            key_t[h] = key_ref[h].astype(f32).T.astype(bf16)
        for i in range(blocks):
            span = pl.ds(i * rows, rows)
            grad = grad_refs[i][...]
            grad_in[span, :] = grad
            mix = dot(grad, weight_ref[:, output_at : output_at + columns], NN)
            mix_t = mix.T
            for h in range(heads):
                cut = slice(h * HEAD_DIM, (h + 1) * HEAD_DIM)
                low = mix_t[cut, :].astype(bf16)
                grad_mix[h, span, :] = mix[:, cut].astype(bf16)
                grad_mix_t[h, :, span] = low
                inner[h : h + 1, span] = jnp.sum(
                    low.astype(f32) * mixed_t_ref[h, :, span].astype(f32), axis=0, keepdims=True
                )

        for copy in inward[3:6]:
            copy.wait()

        def pair(step, carry):
            i, j = step // blocks, step % blocks

            @pl.when(seen(place, prefix, i, j, rows))
            def _():
                here = pl.ds(pl.multiple_of(i * rows, 128), rows)
                there = pl.ds(pl.multiple_of(j * rows, 128), rows)
                visible = mask_of(place, prefix, i, j, rows)
                for h in range(heads):
                    score = dot(key_ref[h, there, :], query_t_ref[h, :, here], NN)
                    weigh = jnp.where(visible, jnp.exp(score - log_ref[h : h + 1, here]), 0.0)
                    soft = dot(value_ref[h, there, :], grad_mix_t[h, :, here], NN)
                    low = (weigh * (soft - inner[h : h + 1, here])).astype(bf16)
                    grad_value[h, there, :] += dot(weigh.astype(bf16), grad_mix[h, here, :], NN)
                    grad_key[h, there, :] += dot(low, query_ref[h, here, :], NN)
                    grad_query_t[h, :, here] += dot(key_t[h, :, there], low, NN)

            return carry

        lax.fori_loop(0, blocks * blocks, pair, 0)
        for copy in inward[6:]:
            copy.wait()
        gain = jnp.zeros((1, width), f32)
        for i in range(blocks):
            span = pl.ds(i * rows, rows)
            spot_rows = pl.ds(pl.multiple_of(block_at(place, i) * rows, 8), rows)
            turned = jnp.concatenate(
                [grad_query_t[h, :, span].T * (1.0 / math.sqrt(HEAD_DIM)) for h in range(heads)]
                + [grad_key[h, span, :] for h in range(heads)],
                axis=1,
            )
            turned = turn(turned, cos_ref[spot_rows, :], -sin_ref[spot_rows, :])
            grads = jnp.concatenate(
                [turned] + [grad_value[h, span, :] for h in range(heads)], axis=1
            ).astype(bf16)
            grad_product[span, :] = grads
            back = dot(grads, weight_ref[:, : 3 * columns], NT)
            tokens = token_refs[i][...].astype(f32)
            inverse = lax.rsqrt(jnp.mean(tokens * tokens, axis=-1, keepdims=True) + epsilon)
            gain += jnp.sum(back * tokens * inverse, axis=0, keepdims=True)
            if i < 2:
                (back_own_ref, back_near_ref)[i][...] = back
            else:
                back_far_ref[i - 2] = back.astype(bf16)
        gains = jnp.concatenate([gain, gain_two_ref[...], jnp.zeros((62, width), f32)], axis=0)
        first_ref[:, 3 * columns : output_at] = gains.T.astype(bf16)
        first_ref[:, : 3 * columns] = dot(normed_ref[...], grad_product[...], TN).astype(bf16)
        first_ref[:, output_at : output_at + columns] = dot(
            grad_in[...], mixed_ref[...], TN
        ).astype(bf16)
        if output_at + columns < lanes:
            first_ref[:, output_at + columns :] = jnp.zeros(
                (width, lanes - output_at - columns), bf16
            )

    per_head = (heads, length, HEAD_DIM)
    per_head_t = (heads, HEAD_DIM, length)
    out_shape = [
        jax.ShapeDtypeStruct(shape, kind)
        for shape, kind in (
            ((width, lanes), bf16),
            ((rows, width), f32),
            ((rows, width), f32),
            ((2, rows, width), bf16),
        )
    ]
    return pl.pallas_call(
        body,
        out_shape=out_shape,
        in_specs=[SMEM] + [HBM] * 3 + [VMEM] * 3 + [HBM] * 8 + [VMEM] * 2 + [HBM] * 2,
        out_specs=[VMEM] * len(out_shape),
        scratch_shapes=[
            pltpu.VMEM((length, width), bf16),
            pltpu.VMEM(per_head, bf16),
            pltpu.VMEM(per_head_t, bf16),
            pltpu.VMEM((8, length), f32),
            pltpu.VMEM(per_head_t, bf16),
            pltpu.VMEM(per_head_t, f32),
            pltpu.VMEM(per_head, f32),
            pltpu.VMEM(per_head, f32),
            pltpu.VMEM((length, 3 * columns), bf16),
        ]
        + [
            pltpu.VMEM(array.shape, array.dtype)
            for array in (
                weight,
                mixed_t,
                key,
                query_t,
                query,
                value,
                *[blocks_in[0]] * 4,
                normed,
                mixed,
                cosine,
                sine,
            )
        ]
        + [pltpu.SemaphoreType.DMA((14,))],
        compiler_params=pltpu.CompilerParams(vmem_limit_bytes=52 * 2**20),
        cost_estimate=NO_COST,
    )(where, *blocks_in, *grads_in, *saved, gain_two, cosine, sine)


def gated(gate_pre, up_pre):
    sigmoid = 1.0 / (1.0 + jnp.exp(-gate_pre))
    return gate_pre * sigmoid * up_pre


def gated_back(grad, gate_pre, up_pre):
    sigmoid = 1.0 / (1.0 + jnp.exp(-gate_pre))
    silu = gate_pre * sigmoid
    grad_gate = grad * up_pre * (sigmoid + silu * (1.0 - sigmoid))
    return silu * up_pre, grad_gate, grad * silu


def call(body, out, *args, scratch=(), scalars=0, limit=28):
    bf16_kinds = [jax.ShapeDtypeStruct(shape, kind) for shape, kind in out]
    return pl.pallas_call(
        body,
        out_shape=bf16_kinds,
        in_specs=[SMEM] * scalars + [VMEM] * (len(args) - scalars),
        out_specs=[VMEM] * len(out),
        scratch_shapes=[pltpu.VMEM(shape, kind) for shape, kind in scratch],
        compiler_params=pltpu.CompilerParams(vmem_limit_bytes=limit * 2**20),
        cost_estimate=NO_COST,
    )(*args)


def join_rows(spot, refs, target):
    rows = refs[0].shape[0]
    for k, ref in enumerate(refs):
        target[pl.ds(pl.multiple_of((spot ^ k) * rows, 16), rows), :] = ref[...]


def expert_kernel(where, rows, grads, pair_in, down_in):
    part = down_in[0].shape[1]
    count, width = rows[0].shape
    units = down_in[0].shape[2]
    step = count // 2
    bf16, f32 = jnp.bfloat16, jnp.float32

    def body(*refs):
        spot, rows_refs, grad_refs = refs[0], refs[1:3], refs[3:5]
        pair_refs, down_refs = refs[5:7], refs[7:9]
        down_ref, own_ref, other_ref = refs[9:12]
        act_refs, back_gate_refs, back_up_refs = refs[12:14], refs[14:16], refs[16:18]
        gate_ref, up_ref = refs[18:]
        for target, views in (
            (gate_ref, [ref.at[n, 0] for n in (0, 1) for ref in pair_refs]),
            (up_ref, [ref.at[n, 1] for n in (0, 1) for ref in pair_refs]),
            (down_ref, [ref.at[n] for n in (0, 1) for ref in down_refs]),
        ):
            join_rows(spot[0], views, target)
        for half in (1, 0):

            def chunk(i, carry, half=half):
                span = pl.ds(pl.multiple_of(i * step, 16), step)
                row = rows_refs[half][span, :]
                gate_pre = dot(row, gate_ref[...], NN)
                up_pre = dot(row, up_ref[...], NN)
                grad = dot(grad_refs[half][span, :], down_ref[...], NN)
                act, grad_gate, grad_up = gated_back(grad, gate_pre, up_pre)
                grad_gate, grad_up = grad_gate.astype(bf16), grad_up.astype(bf16)
                act_refs[half][span, :] = act.astype(bf16)
                back_gate_refs[half][span, :] = grad_gate
                back_up_refs[half][span, :] = grad_up
                back = dot(grad_gate, gate_ref[...], NT) + dot(grad_up, up_ref[...], NT)
                if half:
                    other_ref[span, :] = back.astype(bf16)
                else:
                    own_ref[span, :] = back
                return carry

            lax.fori_loop(0, 2, chunk, 0)

    weight = ((4 * part, units), bf16)
    saved = ((count, units), bf16)
    outs = call(
        body,
        [weight] + [((count, width), f32), ((count, width), bf16)] + [saved] * 6,
        where,
        *rows,
        *grads,
        *pair_in,
        *down_in,
        scratch=[weight] * 2,
        scalars=1,
        limit=52,
    )
    return outs[0], outs[1], outs[2], outs[3:5], outs[5:7], outs[7:9]


def expert_grad_kernel(rows, grads, acts, back_gates, back_ups, down):
    count, width = rows[0].shape
    units = acts[0].shape[1]
    step = 256
    bf16, f32 = jnp.bfloat16, jnp.float32

    def body(*refs):
        rows_refs, grad_refs, act_refs, gate_refs, up_refs = (refs[2 * n : 2 * n + 2] for n in range(5))
        down_ref, own_ref, other_ref, gate_out, up_out, down_out = refs[10:16]

        def chunk(i, carry):
            span = pl.ds(pl.multiple_of(i * step, 128), step)
            for left, right, target in (
                (rows_refs, gate_refs, gate_out),
                (rows_refs, up_refs, up_out),
                (grad_refs, act_refs, down_out),
            ):
                target[:, span] = (
                    dot(left[0][...], right[0][:, span], TN)
                    + dot(left[1][...], right[1][:, span], TN)
                ).astype(bf16)
            return carry

        lax.fori_loop(0, units // step, chunk, 0)
        own_ref[...] = dot(act_refs[0][...], down_ref[...], NT)
        other_ref[...] = dot(act_refs[1][...], down_ref[...], NT).astype(bf16)

    return call(
        body,
        [
            ((count, width), f32),
            ((count, width), bf16),
            *[((width, units), bf16)] * 3,
        ],
        *rows,
        *grads,
        *acts,
        *back_gates,
        *back_ups,
        down,
        limit=52,
    )


def dense_kernel(normed, pack, weight):
    rows, width = normed[0].shape
    units = weight.shape[1] // 3
    bf16, f32 = jnp.bfloat16, jnp.float32

    def body(*refs):
        normed_refs = (refs[0], refs[1], refs[2].at[0], refs[2].at[1])
        grad_refs = pack_views(*refs[3:6], 1)
        weight, back_own, back_near, back_far, out_own, out_near, out_far, total_ref = refs[6:14]
        normed_all, grad_all, wide, act_all = refs[14:]
        gate, up, down = (slice(n * units, (n + 1) * units) for n in range(3))
        for i in range(4):
            row = normed_refs[i][...]
            grad_row = grad_refs[i][...]
            span = slice(i * rows, (i + 1) * rows)
            normed_all[span, :] = row
            grad_all[span, :] = grad_row
            gate_pre = dot(row, weight[:, gate], NN)
            up_pre = dot(row, weight[:, up], NN)
            grad = dot(grad_row, weight[:, down], NN)
            act, grad_gate, grad_up = gated_back(grad, gate_pre, up_pre)
            act = act.astype(bf16)
            act_all[span, :] = act
            wide[span, :units] = grad_gate.astype(bf16)
            wide[span, units:] = grad_up.astype(bf16)
            out = dot(act, weight[:, down], NT)
            back = dot(wide[span, :], weight[:, : 2 * units], NT)
            if i < 2:
                (out_own, out_near)[i][...] = out
                (back_own, back_near)[i][...] = back
            else:
                out_far[i - 2] = out.astype(bf16)
                back_far[i - 2] = back.astype(bf16)
        total_ref[:, : 2 * units] = dot(normed_all[...], wide[...], TN).astype(bf16)
        total_ref[:, down] = dot(grad_all[...], act_all[...], TN).astype(bf16)

    blocks = [((rows, width), f32)] * 2 + [((2, rows, width), bf16)]
    return call(
        body,
        [*blocks, *blocks, ((width, 3 * units), bf16)],
        *normed,
        *pack,
        weight,
        scratch=[
            ((4 * rows, width), bf16),
            ((4 * rows, width), bf16),
            ((4 * rows, 2 * units), bf16),
            ((4 * rows, units), bf16),
        ],
    )


def join_kernel(where, *grads):
    _, rows, cols = grads[0][0].shape
    count = len(grads)
    f32 = jnp.float32

    def body(*refs):
        place = refs[0][0]
        for k in range(4):
            span = pl.ds(pl.multiple_of((place ^ k) * cols, 128), cols)
            for n in range(count):
                half = refs[1 + 3 * n + min(k, 2)].at[place >> 1 if k < 2 else k - 2]
                refs[1 + 3 * count + n][:, span] = half[...].astype(f32)

    return call(
        body,
        [((rows, 4 * cols), f32)] * count,
        where,
        *(part for grad in grads for part in grad),
        scalars=1,
    )


def mix_kernel(hidden, dense, gate_map, slots_out):
    bf16, f32 = jnp.bfloat16, jnp.float32

    def body(hidden_ref, dense_ref, map_ref, slots_ref, out_ref):
        weights = map_ref[...]
        high = weights.astype(bf16)
        low = (weights - high.astype(f32)).astype(bf16)
        slots = slots_ref[...]
        mixed = dot(high, slots, TN) + dot(low, slots, TN)
        out_ref[...] = (hidden_ref[...] + dense_ref[...] + mixed).astype(bf16)

    return call(body, [(hidden.shape, bf16)], hidden, dense, gate_map, slots_out)[0]


def paired(
    tokens,
    cotangent,
    gain_attn,
    w_query,
    w_key,
    w_value,
    w_output,
    gain_ffn,
    dense_gate,
    dense_up,
    dense_down,
    expert_gate,
    expert_up,
    expert_down,
    routes,
    slot_order,
    gate_values,
    prefix_len,
):
    dp_count = lax.axis_size("dp")
    tensor_count = lax.axis_size("tensor")
    place = lax.axis_index("tensor")
    local_rows, width = tokens.shape
    length = local_rows * tensor_count
    columns = w_query.shape[1]
    shard = w_query.shape[0]
    hidden_cols = dense_gate.shape[1]
    devices = dp_count * tensor_count
    slots = EXPERTS * CAP
    bf16, f32 = jnp.bfloat16, jnp.float32

    nn, tn = NN, TN

    gain_width = 64
    pad_width = -(4 * columns + gain_width) % 128
    first_shard = jnp.concatenate(
        [
            w_query,
            w_key,
            w_value,
            gain_attn[:, None],
            gain_ffn[:, None],
            jnp.zeros((shard, gain_width - 2), bf16),
            w_output.T,
            jnp.zeros((shard, pad_width), bf16),
        ],
        axis=1,
    )
    dp_place = lax.axis_index("dp")
    pack = jnp.stack([tokens, cotangent])
    pack_near = to_across(after(pack, first_shard))
    row, core = place // 2, place % 2

    def split(values, axis, spot):
        size = values.shape[axis] // 2
        return (
            lax.dynamic_slice_in_dim(values, spot * size, size, axis=axis),
            lax.dynamic_slice_in_dim(values, (1 - spot) * size, size, axis=axis),
        )

    def cut_pieces(pieces):
        halves = [split(piece, 1, row) for piece in pieces]
        return [jnp.stack([half[n] for half in halves]) for n in (0, 1)]

    def share_beside(own, across):
        mine, other = split(jnp.stack([own, across]), 3, core)
        return mine, to_beside(other)

    def send_grads(grad):
        blocks = grad.reshape(2, 2, -1, grad.shape[1])
        mine = lax.dynamic_index_in_dim(blocks, core, 1, keepdims=False)
        beside = to_beside(lax.dynamic_index_in_dim(blocks, 1 - core, 1, keepdims=False))
        return mine, beside

    def cross_grads(mine, beside):
        halves = [lax.dynamic_index_in_dim(half, 1 - row, 0, keepdims=False) for half in (mine, beside)]
        return to_across(jnp.stack(halves))


    expert_ids = routes.reshape(-1)
    ranking = slot_order.reshape(-1)
    same_expert = expert_ids[:, None] == expert_ids[None, :]
    earlier = ranking[None, :] < ranking[:, None]
    placed = jnp.sum((same_expert & earlier).astype(jnp.int32), axis=1)
    targets = jnp.where(placed < CAP, expert_ids * CAP + placed, -1)
    slot_ids = jnp.arange(slots, dtype=jnp.int32)
    targets_two = targets.reshape(local_rows, TOP)
    hits = [slot_ids[:, None] == targets_two[None, :, k] for k in range(TOP)]
    token_map = sum(hit.astype(bf16) for hit in hits)
    gate_map = sum(jnp.where(hits[k], gate_values[None, :, k], 0.0) for k in range(TOP))
    slot_gate = jnp.sum(gate_map, axis=1)

    groups = [[i * tensor_count + x * 2 + c for i in range(dp_count) for x in (0, 1)] for c in (0, 1)]

    def exchange(slot_rows):
        return lax.all_to_all(
            slot_rows.reshape(EXPERTS, CAP, width),
            ("dp", "tensor"),
            split_axis=0,
            concat_axis=0,
            tiled=True,
            axis_index_groups=groups,
        ).reshape(slots, width)

    def sum_cores(own, other):
        return (own + to_beside(other.astype(bf16)).astype(f32)).astype(bf16)

    slot_cotangent = (dot(token_map, cotangent, nn) * slot_gate[:, None]).astype(bf16)
    pair_own, pair_sent = cut_pieces([expert_gate, expert_up])
    line = gather_line(first_shard)
    line[2:], slot_cotangent, pair_own, pair_sent = after(
        (line[2:], slot_cotangent, pair_own, pair_sent)
    )
    parts = gather_pairs(line)
    pair_across = to_across(after(pair_sent, pack_near))
    pack_far = to_beside(after(jnp.stack([pack, pack_near]), parts))
    token_blocks = (tokens, pack_near, pack_far)
    grad_own = exchange(after(slot_cotangent, parts))
    second_shard = jnp.concatenate([dense_gate, dense_up, dense_down.T], axis=1)
    second = lax.all_gather(after(second_shard, line[1:]), "dp", axis=0, tiled=True)

    where = jnp.stack([place, dp_place, prefix_len[0]])
    (
        *saved,
        sum_own,
        sum_near,
        sum_far,
    ) = attend_kernel(where, token_blocks, parts, length, columns)
    normed_all, weights, gains_both, *saved = saved
    gain_one, gain_two = gains_both[0], gains_both[1]
    inputs = tokens.astype(f32)
    hidden = inputs + sum_across(sum_own, sum_near, sum_far, pair_across)
    grad_rows = (grad_own, to_beside(grad_own))
    hidden = after(hidden, grad_rows)
    normed_two = norm_rows(hidden, gain_two).astype(bf16)

    dispatched = dot(token_map, normed_two, nn).astype(bf16)
    own_rows = exchange(dispatched)
    normed_near = to_across(normed_two)
    down_own, down_sent = cut_pieces([expert_down.T])
    down_across = to_across(after(down_sent, dispatched))
    normed_far = to_beside(jnp.stack([normed_two, normed_near]))
    back_own, back_near, back_far, out_own, out_near, out_far, second_grad = dense_kernel(
        (normed_two, normed_near, normed_far), (cotangent, pack_near, pack_far), second
    )
    second_total = lax.psum_scatter(second_grad, "dp", scatter_dimension=0, tiled=True)
    down_across = after(down_across, second_grad)
    pair_in = share_beside(pair_own, pair_across)
    down_in = [part[:, 0] for part in share_beside(down_own, down_across)]
    own_rows, back_far, out_far = after((own_rows, back_far, out_far), second_grad, down_in, pair_in)
    expert_rows = (own_rows, to_beside(own_rows))
    dense_back = sum_across(back_own, back_near, back_far)
    piece_down_t, slots_own, slots_other, acts, grads_gate, grads_up = expert_kernel(
        where, expert_rows, grad_rows, pair_in, down_in
    )
    back_rows = sum_cores(slots_own, slots_other)
    slots_back = exchange(back_rows)

    mixed_own, mixed_other, gate_grad, up_grad, down_grad = expert_grad_kernel(
        after(expert_rows, back_rows), grad_rows, acts, grads_gate, grads_up, piece_down_t
    )
    out_rows = sum_cores(mixed_own, mixed_other)
    gate_parts = send_grads(gate_grad)
    up_parts, down_parts = send_grads(up_grad), send_grads(down_grad)
    slots_back = after(slots_back, second_total, out_rows, dense_back, gate_parts, up_parts, down_parts)

    expert_back = dot(token_map, slots_back, tn)
    grad_normed_two = dense_back + expert_back
    grad_hidden_norm, grad_gain_two = norm_back(hidden, gain_two, grad_normed_two)
    grad_hidden = cotangent.astype(f32) + grad_hidden_norm

    grad_attn_own = grad_hidden.astype(bf16)
    grad_near = to_across(grad_attn_own)
    grad_far = to_beside(jnp.stack([grad_attn_own, grad_near]))
    slots_out = exchange(after(out_rows, grad_attn_own))
    gate_parts += (cross_grads(*after(gate_parts, grad_near)),)
    up_parts += (cross_grads(*after(up_parts, grad_near)),)
    first_grad, back_own, back_near, back_far = attend_back_kernel(
        where,
        token_blocks,
        (grad_attn_own, grad_near, grad_far),
        [normed_all, weights, *saved],
        grad_gain_two[None],
        length,
        columns,
    )
    first_grad = after(first_grad, slots_out, gate_parts)
    first_parts = lax.all_to_all(
        first_grad.reshape(dp_count, shard, -1), "dp", split_axis=0, concat_axis=0, tiled=True
    )
    grad_normed_one = sum_across(back_own, back_near, back_far, up_parts)
    grad_input_norm, _ = norm_back(inputs, gain_one, grad_normed_one)
    grad_tokens = grad_hidden + grad_input_norm
    down_parts, out_far = after((down_parts, out_far), first_grad)
    down_parts += (cross_grads(*down_parts),)
    dense_out = sum_across(out_own, out_near, out_far)
    slots_out, gate_parts, up_parts = after((slots_out, gate_parts, up_parts), first_grad)
    block_out = mix_kernel(hidden, dense_out, gate_map, slots_out)
    gate_total, up_total = join_kernel(where, gate_parts, up_parts)
    (down_total,) = join_kernel(where, down_parts)
    second_total = after(second_total, block_out).astype(f32)
    first_parts = after(first_parts, block_out, gate_total)
    first_total = jnp.sum(first_parts.astype(f32), axis=0)
    gains = first_total[:, 3 * columns : 3 * columns + 2].T
    gains = gains + to_beside(gains)
    gains = gains + to_across(gains)
    return (
        block_out,
        grad_tokens,
        gains[0],
        first_total[:, :columns],
        first_total[:, columns : 2 * columns],
        first_total[:, 2 * columns : 3 * columns],
        first_total[:, 3 * columns + gain_width :][:, :columns].T,
        gains[1],
        second_total[:, :hidden_cols],
        second_total[:, hidden_cols : 2 * hidden_cols],
        second_total[:, 2 * hidden_cols :].T,
        gate_total,
        up_total,
        down_total.T,
    )


def gather_rows(rows_in):
    return lax.all_gather(rows_in, "tensor", axis=0, tiled=True)


def sum_rows(rows_in):
    return lax.psum_scatter(rows_in, "tensor", scatter_dimension=0, tiled=True)


def gather_attn_rows(rows_in):
    return lax.all_gather(rows_in, "tensor", axis=0, tiled=True)


def sum_attn_rows(rows_in):
    return lax.psum_scatter(rows_in, "tensor", scatter_dimension=0, tiled=True)


def general(
    tokens,
    cotangent,
    gain_attn,
    w_query,
    w_key,
    w_value,
    w_output,
    gain_ffn,
    dense_gate,
    dense_up,
    dense_down,
    expert_gate,
    expert_up,
    expert_down,
    routes,
    slot_order,
    gate_values,
    prefix_len,
):
    dp_count = lax.axis_size("dp")
    tensor_count = lax.axis_size("tensor")
    local_rows = tokens.shape[0]
    model_width = tokens.shape[1]
    length = local_rows * tensor_count
    splits = max(1, dp_count // EXPERTS)
    per_device = max(1, EXPERTS // dp_count)
    inputs = tokens.astype(jnp.float32)
    dense_all = (
        lax.all_gather(gain_attn, "dp", axis=0, tiled=True),
        lax.all_gather(w_query, "dp", axis=0, tiled=True),
        lax.all_gather(w_key, "dp", axis=0, tiled=True),
        lax.all_gather(w_value, "dp", axis=0, tiled=True),
        lax.all_gather(w_output, "dp", axis=1, tiled=True),
        lax.all_gather(gain_ffn, "dp", axis=0, tiled=True),
        lax.all_gather(dense_gate, "dp", axis=0, tiled=True),
        lax.all_gather(dense_up, "dp", axis=0, tiled=True),
        lax.all_gather(dense_down, "dp", axis=1, tiled=True),
    )
    (
        gain_one,
        query_full,
        key_full,
        value_full,
        output_full,
        gain_two,
        gate_full,
        up_full,
        down_full,
    ) = dense_all
    gain_one = gain_one.astype(jnp.float32)
    gain_two = gain_two.astype(jnp.float32)
    positions = jnp.arange(length, dtype=jnp.int32)
    prefix_value = prefix_len[0]
    normed_one = norm_rows(inputs, gain_one).astype(jnp.bfloat16)
    head_count = query_full.shape[1] // HEAD_DIM
    normed_all = gather_attn_rows(normed_one)
    queries = rotary(
        jnp.dot(normed_all, query_full, preferred_element_type=jnp.float32).reshape(
            length, head_count, HEAD_DIM
        ),
        positions,
        1.0,
    ).astype(jnp.bfloat16)
    keys_all = rotary(
        jnp.dot(normed_all, key_full, preferred_element_type=jnp.float32).reshape(
            length, head_count, HEAD_DIM
        ),
        positions,
        1.0,
    ).astype(jnp.bfloat16)
    values_all = (
        jnp.dot(normed_all, value_full, preferred_element_type=jnp.float32)
        .astype(jnp.bfloat16)
        .reshape(length, head_count, HEAD_DIM)
    )
    score_scale = 1.0 / math.sqrt(HEAD_DIM)
    block_rows = min(512, length)
    blocks = length // block_rows
    query_blocks = queries.reshape(blocks, block_rows, head_count, HEAD_DIM)
    position_blocks = positions.reshape(blocks, block_rows)

    def block_scores(block_query, block_pos):
        scores = (
            jnp.einsum("qhd,khd->hqk", block_query, keys_all, preferred_element_type=jnp.float32)
            * score_scale
        )
        visible = (positions[None, :] <= block_pos[:, None]) | (positions[None, :] < prefix_value)
        return jnp.where(visible[None], scores, -1e30)

    def attend(block_item):
        block_query, block_pos = block_item
        scores = block_scores(block_query, block_pos)
        row_top = jnp.max(scores, axis=-1, keepdims=True)
        exponent = jnp.exp(scores - row_top)
        row_total = jnp.sum(exponent, axis=-1, keepdims=True)
        softmaxed = exponent / row_total
        mixture = jnp.einsum(
            "hqk,khd->qhd",
            softmaxed.astype(jnp.bfloat16),
            values_all,
            preferred_element_type=jnp.float32,
        ).astype(jnp.bfloat16)
        return (mixture, (row_top + jnp.log(row_total))[..., 0])

    attended, log_totals = lax.map(attend, (query_blocks, position_blocks))
    attended = attended.reshape(length, head_count * HEAD_DIM)
    hidden = inputs + sum_attn_rows(
        jnp.dot(attended, output_full, preferred_element_type=jnp.float32)
    )
    normed_two = norm_rows(hidden, gain_two).astype(jnp.bfloat16)
    normed_two_all = gather_rows(normed_two)
    gate_pre = jnp.dot(normed_two_all, gate_full, preferred_element_type=jnp.float32)
    up_pre = jnp.dot(normed_two_all, up_full, preferred_element_type=jnp.float32)
    activated = (jax.nn.silu(gate_pre) * up_pre).astype(jnp.bfloat16)
    dense_out = sum_rows(jnp.dot(activated, down_full, preferred_element_type=jnp.float32))
    expert_ids = routes.reshape(-1)
    ranking = slot_order.reshape(-1)
    same_expert = expert_ids[:, None] == expert_ids[None, :]
    earlier = ranking[None, :] < ranking[:, None]
    placed = jnp.sum((same_expert & earlier).astype(jnp.int32), axis=1)
    usable = placed < CAP
    targets = jnp.where(usable, expert_ids * CAP + placed, -1)
    slot_ids = jnp.arange(EXPERTS * CAP, dtype=jnp.int32)
    pair_map = (slot_ids[:, None] == targets[None, :]).astype(jnp.float32)
    token_map = jnp.sum(pair_map.reshape(EXPERTS * CAP, local_rows, TOP), axis=2).astype(
        jnp.bfloat16
    )
    dispatched = jnp.dot(token_map, normed_two, preferred_element_type=jnp.float32).astype(
        jnp.bfloat16
    )
    outgoing = jnp.broadcast_to(
        dispatched.reshape(EXPERTS, 1, CAP, model_width), (EXPERTS, splits, CAP, model_width)
    ).reshape(dp_count, per_device, CAP, model_width)
    expert_all = (
        lax.all_gather(expert_gate, "tensor", axis=0, tiled=True),
        lax.all_gather(expert_up, "tensor", axis=0, tiled=True),
        lax.all_gather(expert_down, "tensor", axis=1, tiled=True),
    )
    piece_width = expert_all[0].shape[1] // per_device
    gate_pieces = expert_all[0].reshape(model_width, per_device, piece_width)
    up_pieces = expert_all[1].reshape(model_width, per_device, piece_width)
    down_pieces = expert_all[2].reshape(per_device, piece_width, model_width)
    received = lax.all_to_all(outgoing, "dp", split_axis=0, concat_axis=0, tiled=True)
    gate_local = jnp.einsum(
        "sjnd,djp->sjnp", received, gate_pieces, preferred_element_type=jnp.float32
    )
    up_local = jnp.einsum("sjnd,djp->sjnp", received, up_pieces, preferred_element_type=jnp.float32)
    active_local = (jax.nn.silu(gate_local) * up_local).astype(jnp.bfloat16)
    result_local = jnp.einsum(
        "sjnp,jpd->sjnd", active_local, down_pieces, preferred_element_type=jnp.float32
    ).astype(jnp.bfloat16)
    returned = lax.all_to_all(result_local, "dp", split_axis=0, concat_axis=0, tiled=True)
    returned, kept_in, gate_local, up_local = (returned, received, gate_local, up_local)
    expert_sums = jnp.sum(
        returned.reshape(EXPERTS, splits, CAP, model_width).astype(jnp.float32), axis=1
    ).reshape(EXPERTS * CAP, model_width)
    pick_index = jnp.where(usable, targets, 0)
    pair_weight = jnp.where(usable, gate_values.reshape(-1), 0.0)
    picked = jnp.take(expert_sums, pick_index, axis=0) * pair_weight[:, None]
    expert_mix = jnp.sum(picked.reshape(local_rows, TOP, model_width), axis=1)
    block_out = (hidden + dense_out + expert_mix).astype(jnp.bfloat16)
    dense_back = (
        lax.all_gather(gain_attn, "dp", axis=0, tiled=True),
        lax.all_gather(w_query, "dp", axis=0, tiled=True),
        lax.all_gather(w_key, "dp", axis=0, tiled=True),
        lax.all_gather(w_value, "dp", axis=0, tiled=True),
        lax.all_gather(w_output, "dp", axis=1, tiled=True),
        lax.all_gather(gain_ffn, "dp", axis=0, tiled=True),
        lax.all_gather(dense_gate, "dp", axis=0, tiled=True),
        lax.all_gather(dense_up, "dp", axis=0, tiled=True),
        lax.all_gather(dense_down, "dp", axis=1, tiled=True),
    )
    (
        gain_one,
        query_full,
        key_full,
        value_full,
        output_full,
        gain_two,
        gate_full,
        up_full,
        down_full,
    ) = dense_back
    gain_one = gain_one.astype(jnp.float32)
    gain_two = gain_two.astype(jnp.float32)
    grad_out = cotangent.astype(jnp.float32)
    cotangent_all = gather_rows(cotangent)
    grad_down = jnp.einsum(
        "lf,ld->fd", activated, cotangent_all, preferred_element_type=jnp.float32
    )
    grad_act = jnp.einsum("ld,fd->lf", cotangent_all, down_full, preferred_element_type=jnp.float32)
    grad_gate_pre, grad_up_pre = swiglu_back(grad_act, gate_pre, up_pre)
    grad_gate = jnp.einsum(
        "ld,lf->df", normed_two_all, grad_gate_pre, preferred_element_type=jnp.float32
    )
    grad_up = jnp.einsum(
        "ld,lf->df", normed_two_all, grad_up_pre, preferred_element_type=jnp.float32
    )
    dense_back_in = jnp.einsum(
        "lf,df->ld", grad_gate_pre, gate_full, preferred_element_type=jnp.float32
    ) + jnp.einsum("lf,df->ld", grad_up_pre, up_full, preferred_element_type=jnp.float32)
    slot_gate = jnp.dot(pair_map, gate_values.reshape(-1), precision=lax.Precision.HIGHEST)
    slot_cotangent = jnp.dot(token_map, cotangent, preferred_element_type=jnp.float32)
    grad_slots = (slot_cotangent * slot_gate[:, None]).astype(jnp.bfloat16)
    grad_outgoing = jnp.broadcast_to(
        grad_slots.reshape(EXPERTS, 1, CAP, model_width), (EXPERTS, splits, CAP, model_width)
    ).reshape(dp_count, per_device, CAP, model_width)
    grad_received = lax.all_to_all(grad_outgoing, "dp", split_axis=0, concat_axis=0, tiled=True)
    active_local = (jax.nn.silu(gate_local) * up_local).astype(jnp.bfloat16)
    grad_down_expert = jnp.einsum(
        "sjnp,sjnd->jpd", active_local, grad_received, preferred_element_type=jnp.float32
    ).reshape(per_device * piece_width, model_width)
    grad_act_expert = jnp.einsum(
        "sjnd,jpd->sjnp", grad_received, down_pieces, preferred_element_type=jnp.float32
    )
    grad_gate_local, grad_up_local = swiglu_back(grad_act_expert, gate_local, up_local)
    grad_gate_expert = jnp.einsum(
        "sjnd,sjnp->djp", kept_in, grad_gate_local, preferred_element_type=jnp.float32
    ).reshape(model_width, per_device * piece_width)
    grad_up_expert = jnp.einsum(
        "sjnd,sjnp->djp", kept_in, grad_up_local, preferred_element_type=jnp.float32
    ).reshape(model_width, per_device * piece_width)
    grad_in_expert = (
        jnp.einsum(
            "sjnp,djp->sjnd", grad_gate_local, gate_pieces, preferred_element_type=jnp.float32
        )
        + jnp.einsum("sjnp,djp->sjnd", grad_up_local, up_pieces, preferred_element_type=jnp.float32)
    ).astype(jnp.bfloat16)
    grad_back = lax.all_to_all(grad_in_expert, "dp", split_axis=0, concat_axis=0, tiled=True)
    grad_slots_in = jnp.sum(
        grad_back.reshape(EXPERTS, splits, CAP, model_width).astype(jnp.float32), axis=1
    ).reshape(EXPERTS * CAP, model_width)
    grad_pairs = jnp.where(usable[:, None], jnp.take(grad_slots_in, pick_index, axis=0), 0.0)
    expert_back = jnp.sum(grad_pairs.reshape(local_rows, TOP, model_width), axis=1)
    grad_normed_two = sum_rows(dense_back_in) + expert_back
    grad_hidden_norm, grad_gain_two_part = norm_back(hidden, gain_two, grad_normed_two)
    grad_hidden = grad_out + grad_hidden_norm
    query_use, key_use, value_use, output_use = (query_full, key_full, value_full, output_full)
    grad_attn_in = gather_attn_rows(grad_hidden.astype(jnp.bfloat16))
    grad_output_w = jnp.einsum(
        "lc,ld->cd", attended, grad_attn_in, preferred_element_type=jnp.float32
    )
    grad_attended = (
        jnp.einsum("ld,cd->lc", grad_attn_in, output_use, preferred_element_type=jnp.float32)
        .astype(jnp.bfloat16)
        .reshape(blocks, block_rows, head_count, HEAD_DIM)
    )

    def attend_back(running, block_item):
        grad_keys, grad_values = running
        block_query, block_pos, block_grad, block_total = block_item
        scores = block_scores(block_query, block_pos)
        softmaxed = jnp.exp(scores - block_total[..., None])
        grad_soft = jnp.einsum(
            "qhd,khd->hqk", block_grad, values_all, preferred_element_type=jnp.float32
        )
        inner_sum = jnp.sum(softmaxed * grad_soft, axis=-1, keepdims=True)
        grad_scores = (softmaxed * (grad_soft - inner_sum)).astype(jnp.bfloat16)
        grad_block = (
            jnp.einsum("hqk,khd->qhd", grad_scores, keys_all, preferred_element_type=jnp.float32)
            * score_scale
        )
        grad_keys = (
            grad_keys
            + jnp.einsum(
                "hqk,qhd->khd", grad_scores, block_query, preferred_element_type=jnp.float32
            )
            * score_scale
        )
        grad_values = grad_values + jnp.einsum(
            "hqk,qhd->khd",
            softmaxed.astype(jnp.bfloat16),
            block_grad,
            preferred_element_type=jnp.float32,
        )
        return ((grad_keys, grad_values), grad_block)

    zero_start = (
        jnp.zeros((length, head_count, HEAD_DIM), jnp.float32),
        jnp.zeros((length, head_count, HEAD_DIM), jnp.float32),
    )
    (grad_keys, grad_values), grad_queries = lax.scan(
        attend_back, zero_start, (query_blocks, position_blocks, grad_attended, log_totals)
    )
    grad_queries = (
        rotary(grad_queries.reshape(length, head_count, HEAD_DIM), positions, -1.0)
        .astype(jnp.bfloat16)
        .reshape(length, head_count * HEAD_DIM)
    )
    grad_keys = (
        rotary(grad_keys, positions, -1.0)
        .astype(jnp.bfloat16)
        .reshape(length, head_count * HEAD_DIM)
    )
    grad_values = grad_values.astype(jnp.bfloat16).reshape(length, head_count * HEAD_DIM)
    grad_query_w = jnp.einsum(
        "ld,lc->dc", normed_all, grad_queries, preferred_element_type=jnp.float32
    )
    grad_key_w = jnp.einsum("ld,lc->dc", normed_all, grad_keys, preferred_element_type=jnp.float32)
    grad_value_w = jnp.einsum(
        "ld,lc->dc", normed_all, grad_values, preferred_element_type=jnp.float32
    )
    normed_back_part = (
        jnp.einsum("lc,dc->ld", grad_queries, query_use, preferred_element_type=jnp.float32)
        + jnp.einsum("lc,dc->ld", grad_keys, key_use, preferred_element_type=jnp.float32)
        + jnp.einsum("lc,dc->ld", grad_values, value_use, preferred_element_type=jnp.float32)
    )
    grad_normed_one = sum_attn_rows(normed_back_part)
    grad_input_norm, grad_gain_one_part = norm_back(inputs, gain_one, grad_normed_one)
    grad_tokens = grad_hidden + grad_input_norm
    dense_grads = (
        lax.psum_scatter(grad_gain_one_part, "dp", scatter_dimension=0, tiled=True),
        lax.psum_scatter(grad_query_w, "dp", scatter_dimension=0, tiled=True),
        lax.psum_scatter(grad_key_w, "dp", scatter_dimension=0, tiled=True),
        lax.psum_scatter(grad_value_w, "dp", scatter_dimension=0, tiled=True),
        lax.psum_scatter(grad_output_w, "dp", scatter_dimension=1, tiled=True),
        lax.psum_scatter(grad_gain_two_part, "dp", scatter_dimension=0, tiled=True),
        lax.psum_scatter(grad_gate, "dp", scatter_dimension=0, tiled=True),
        lax.psum_scatter(grad_up, "dp", scatter_dimension=0, tiled=True),
        lax.psum_scatter(grad_down, "dp", scatter_dimension=1, tiled=True),
    )
    gain_totals = lax.psum((dense_grads[0], dense_grads[5]), "tensor")
    expert_grads = (
        lax.psum_scatter(
            grad_gate_expert.astype(jnp.bfloat16), "tensor", scatter_dimension=0, tiled=True
        ).astype(jnp.float32),
        lax.psum_scatter(
            grad_up_expert.astype(jnp.bfloat16), "tensor", scatter_dimension=0, tiled=True
        ).astype(jnp.float32),
        lax.psum_scatter(
            grad_down_expert.astype(jnp.bfloat16), "tensor", scatter_dimension=1, tiled=True
        ).astype(jnp.float32),
    )
    return (
        block_out,
        grad_tokens,
        gain_totals[0],
        dense_grads[1],
        dense_grads[2],
        dense_grads[3],
        dense_grads[4],
        gain_totals[1],
        dense_grads[6],
        dense_grads[7],
        dense_grads[8],
        expert_grads[0],
        expert_grads[1],
        expert_grads[2],
    )


def solution(mesh):
    sizes = mesh.shape
    in_pairs = sizes["tensor"] == 4 and sizes["dp"] * 2 == EXPERTS
    local = paired if in_pairs else general
    return jax.shard_map(
        local,
        mesh=mesh,
        in_specs=(
            P(("dp", "tensor"), None),
            P(("dp", "tensor"), None),
            P("dp"),
            P("dp", "tensor"),
            P("dp", "tensor"),
            P("dp", "tensor"),
            P("tensor", "dp"),
            P("dp"),
            P("dp", "tensor"),
            P("dp", "tensor"),
            P("tensor", "dp"),
            P("tensor", "dp"),
            P("tensor", "dp"),
            P("dp", "tensor"),
            P(("dp", "tensor"), None),
            P(("dp", "tensor"), None),
            P(("dp", "tensor"), None),
            P("dp"),
        ),
        out_specs=(
            P(("dp", "tensor"), None),
            P(("dp", "tensor"), None),
            P("dp"),
            P("dp", "tensor"),
            P("dp", "tensor"),
            P("dp", "tensor"),
            P("tensor", "dp"),
            P("dp"),
            P("dp", "tensor"),
            P("dp", "tensor"),
            P("tensor", "dp"),
            P("tensor", "dp"),
            P("tensor", "dp"),
            P("dp", "tensor"),
        ),
        check_vma=False,
    )
```
